128 devices in a mesh: ex: 8 (over y, core), ctr: 16 (over z, x).
Axes of the slice: x: 4, y: 4, z: 4, core: 2. Of those that a mesh axis runs over, the one named last changes fastest.
Arguments:
- pool: bfloat16 [64, 32768], P(None, ('ex', 'ctr')), may hold values from -4 to 4
- indices: int32 [16384], P('ex'), may hold values from 0 to 4095
- labels: int32 [16384], P('ex'), may hold values from 0 to 143
- example_weight: float32 [16384], P('ex'), may hold values from 0.5 to 18, as said below
- centers: bfloat16 [64, 32768], P(None, 'ctr'), may hold values from -4 to 4
- alpha: bfloat16 [144, 32768], P(None, 'ctr'), may hold values from -1.5 to 1.5
- precond: float32 [32768, 256], P('ctr'), may hold values from -13.5 to 13.5, as said below
Outputs:
- margins: float32 [144, 16384], P(None, ('ex', 'ctr'))
The draws below stay inside these ranges and needn't reach their ends.
Inputs may be any that keep to these rules, and one draw needn't show every extreme that they name: `indices`: example e belongs to example row e // 2048 and names a column of that row's part of pool, columns (e // 2048) * 4096 to (e // 2048 + 1) * 4096 - 1. `example_weight`: positive. `precond`: rows k*256 to (k+1)*256 - 1 hold block k's matrix, column j being its column j; entries below the diagonal are zero and diagonal entries are positive.
All inputs are finite; a program needn't handle non-finite values.
Results may differ from the reference program's by a relative error of at most 0.0012.
Values may be sent and summed in bfloat16 or wider, within the bound.
No kernel may reach another device: no remote copies, remote signals or barrier semaphores. Data moves between devices by JAX's collectives and lax.ppermute only.
A program may use at most 64 MiB of HBM per device.

```python
import math
import jax
import jax.numpy as jnp
from jax import lax

FEATURES = 64
CLASSES = 144
EX_DEV = 2048
BLOCK = 256
ITERS = 2
EXAMPLES = 16384
CENTERS = 32768
POOL_ROW = 4096
N_EX = 8


def draw_example_weight(key, part):
    key = jax.random.fold_in(key, 11)
    position = jnp.arange(EXAMPLES, dtype=jnp.float32) / EXAMPLES
    base_weight = jnp.exp(jax.random.uniform(key, (EXAMPLES,), jnp.float32, math.log(0.5), math.log(2.0)))
    ramp_factor = jnp.exp(position * math.log(3.0))
    return (base_weight * ramp_factor).astype(jnp.float32)


def draw_precond(key, part):
    key = jax.random.fold_in(key, 23)
    diag_key, upper_key = jax.random.split(key)
    row_ids = jnp.arange(CENTERS, dtype=jnp.int32)[:, None]
    col_ids = jnp.arange(BLOCK, dtype=jnp.int32)[None, :]
    local_row = row_ids % BLOCK
    diagonal = jax.random.uniform(diag_key, (CENTERS, 1), jnp.float32, 0.5, 1.5)
    position = row_ids.astype(jnp.float32) / CENTERS
    upper = 0.5 * jax.random.normal(upper_key, (CENTERS, BLOCK), jnp.float32) / math.sqrt(BLOCK)
    ramp_factor = jnp.exp(position * math.log(3.0))
    entries = jnp.where(col_ids == local_row, diagonal, jnp.where(col_ids > local_row, upper, 0.0))
    return (entries * ramp_factor).astype(jnp.float32)


def plant(drawn, own_key, low, top_value):
    extent = drawn.shape
    place = [jax.random.randint(jax.random.fold_in(own_key, axis), (), 0, extent[axis]) for axis in range(len(extent))]
    drawn = drawn.at[tuple(place)].set(low)
    longest = extent.index(max(extent))
    place[longest] = (place[longest] + 1) % extent[longest]
    return drawn.at[tuple(place)].set(top_value)


def block_scale(stream_key, shape, cuts, smallest, top_value):
    loudness = 1.0
    for dim, blocks in cuts:
        heights = jax.random.uniform(jax.random.fold_in(jax.random.fold_in(stream_key, 6), dim), (blocks,), jnp.float32, smallest / len(cuts), top_value / len(cuts))
        loudness = loudness * jnp.repeat(jnp.exp(heights), shape[dim] // blocks).reshape((-1,) + (1,) * (len(shape) - 1 - dim))
    return loudness


def gaussian(stream_key, shape, width, limit, cuts=(), held_as=jnp.bfloat16):
    gain = block_scale(stream_key, shape, cuts, -0.22, 0.18) if cuts else 1.0
    drawn = jax.random.normal(stream_key, shape, jnp.float32) * width * gain
    return jnp.minimum(jnp.maximum(drawn, -limit), limit).astype(held_as)


def setup_inputs(seed: int = 0) -> dict:
    streams_of = jax.random.split(jax.random.key(seed), 8)
    pool = gaussian(streams_of[0], (FEATURES, POOL_ROW * N_EX), 1.0, 4.0, ((1, 128),))
    indices = plant(jax.random.randint(streams_of[1], (EXAMPLES,), 0, POOL_ROW), jax.random.fold_in(streams_of[1], 1), 0, POOL_ROW - 1).astype(jnp.int32)
    labels = plant(jax.random.randint(streams_of[2], (EXAMPLES,), 0, CLASSES), jax.random.fold_in(streams_of[2], 1), 0, CLASSES - 1).astype(jnp.int32)
    example_weight = draw_example_weight(jax.random.fold_in(streams_of[7], 71), 0)
    centers = gaussian(streams_of[4], (FEATURES, CENTERS), 1.0, 4.0, ((1, 16),))
    alpha = gaussian(streams_of[5], (CLASSES, CENTERS), (max(CENTERS // 2048, 1)) ** -0.5, 1.5, ((1, 16),))
    precond = draw_precond(jax.random.fold_in(streams_of[7], 71), 0)
    return {"pool": pool, "indices": indices, "labels": labels, "example_weight": example_weight, "centers": centers, "alpha": alpha, "precond": precond}


RIDGE = 1e-4


def apply_blocks(factor, vectors):
    order_size = factor.shape[1]
    blocks = factor.reshape(-1, order_size, order_size)
    pieces = vectors.reshape(vectors.shape[0], -1, order_size)
    return jnp.einsum("kij,ckj->cki", blocks, pieces, precision=lax.Precision.HIGHEST).reshape(vectors.shape)


def apply_transposed(factor, vectors):
    order_size = factor.shape[1]
    blocks = factor.reshape(-1, order_size, order_size)
    pieces = vectors.reshape(vectors.shape[0], -1, order_size)
    return jnp.einsum("kij,cki->ckj", blocks, pieces, precision=lax.Precision.HIGHEST).reshape(vectors.shape)


def reference(pool, indices, labels, example_weight, centers, alpha, precond):
    example_ids = jnp.arange(EXAMPLES, dtype=jnp.int32)
    columns = ((example_ids // EX_DEV) * POOL_ROW + indices).astype(jnp.int32)
    points = jnp.take(pool, columns, axis=1)
    center_float = centers.astype(jnp.float32)
    center_sq = jnp.sum(center_float * center_float, axis=0)

    def tile_rows(block_points):
        point_float = block_points.astype(jnp.float32)
        point_sq = jnp.sum(point_float * point_float, axis=0)
        cross_dot = jnp.dot(block_points.T, centers, preferred_element_type=jnp.float32)
        exponent_scale = 2.0 / FEATURES
        distance = point_sq[:, None] + center_sq[None, :] - 2.0 * cross_dot
        return jnp.exp(-exponent_scale * distance).astype(jnp.bfloat16)

    point_groups = points.reshape(FEATURES, N_EX, EX_DEV).transpose(1, 0, 2)
    kernel = lax.map(tile_rows, point_groups).reshape(EXAMPLES, CENTERS)

    def forward(coefficients):
        return jnp.dot(coefficients, kernel.T, preferred_element_type=jnp.float32)

    def backward(values):
        return jnp.dot(values, kernel, preferred_element_type=jnp.float32)

    margins = forward(alpha)
    probability = jax.nn.sigmoid(margins)
    target = (labels[None, :] == jnp.arange(CLASSES, dtype=jnp.int32)[:, None]).astype(jnp.float32)
    hessian = example_weight[None, :] * probability * (1.0 - probability)
    gradient = (example_weight[None, :] * (probability - target)).astype(jnp.bfloat16)
    right_side = -apply_transposed(precond, backward(gradient)) / EXAMPLES
    residual = right_side
    direction = right_side
    norm_now = jnp.sum(residual * residual, axis=1)
    for iteration in range(ITERS):
        lifted = apply_blocks(precond, direction).astype(jnp.bfloat16)
        image_rows = forward(lifted)
        weighted = (hessian * image_rows).astype(jnp.bfloat16)
        image_vec = apply_transposed(precond, backward(weighted)) / EXAMPLES + RIDGE * direction
        curvature = jnp.sum(direction * image_vec, axis=1)
        step_len = norm_now / curvature
        margins = margins + step_len[:, None] * image_rows
        if iteration + 1 < ITERS:
            residual = residual - step_len[:, None] * image_vec
            norm_next = jnp.sum(residual * residual, axis=1)
            direction = residual + (norm_next / norm_now)[:, None] * direction
            norm_now = norm_next
    return margins
```

```python
import functools

import jax
import jax.numpy as jnp
from jax import lax
from jax.experimental import pallas as pl
from jax.experimental.pallas import tpu as pltpu
from jax.sharding import PartitionSpec as P

RIDGE = 0.0001
F32 = jnp.float32
BF16 = jnp.bfloat16
VMEM_BYTES = 48 * 1024 * 1024


def split3(values):
    high = values.astype(BF16)
    rest = values - high.astype(F32)
    middle = rest.astype(BF16)
    low = (rest - middle.astype(F32)).astype(BF16)
    return high, middle, low


def tile_kernel(index_ref, pool_ref, centers_ref, alpha_ref, tile_ref, rows_ref, aug_ref):
    features, lanes = pool_ref.shape[1], pool_ref.shape[2]
    chunks = pool_ref.shape[0]
    pad = aug_ref.shape[0] - features

    def tail(squares, first):
        pieces = [p.astype(F32) for p in split3(-0.5 * squares)]
        row = lax.broadcasted_iota(jnp.int32, (pad, squares.shape[1]), 0)
        out = jnp.where((row >= 3 - first) & (row < 6 - first), 1.0, 0.0)
        for k in range(3):
            out = jnp.where(row == k + first, pieces[k], out)
        return out.astype(BF16)

    @pl.when(pl.program_id(0) == 0)
    def _():
        center_float = centers_ref[...].astype(F32)
        center_sq = jnp.sum(center_float * center_float, axis=0, keepdims=True)
        aug_ref[:features, :] = centers_ref[...]
        aug_ref[features:, :] = tail(center_sq, 3)

    index = index_ref[0]
    chunk = index // lanes
    within = index % lanes
    count = index.shape[1]
    one_hot = (lax.broadcasted_iota(jnp.int32, (lanes, count), 0) == within).astype(BF16)
    picked = jnp.dot(
        pool_ref[...].reshape(chunks * features, lanes), one_hot, preferred_element_type=F32
    ).reshape(chunks, features, count)
    points = jnp.where(chunk == 0, picked[0], 0.0)
    for k in range(1, chunks):
        points = jnp.where(chunk == k, picked[k], points)
    point_sq = jnp.sum(points * points, axis=0, keepdims=True)
    lhs = jnp.concatenate([points.astype(BF16), tail(point_sq, 0)], axis=0)
    half_distance = lax.dot_general(
        lhs, aug_ref[...], (((0,), (0,)), ((), ())), preferred_element_type=F32
    )
    values = jnp.exp(half_distance * (4.0 / features)).astype(BF16)
    tile_ref[...] = values
    rows = lax.dot_general(
        alpha_ref[...], values, (((1,), (1,)), ((), ())), preferred_element_type=F32
    )
    share = rows_ref.shape[2]
    for k in range(rows_ref.shape[0]):
        rows_ref[k] = rows[:, k * share : (k + 1) * share]


def make_tile(row_pool, indices, centers, alpha, share):
    block = 256
    chunks, features, lanes = row_pool.shape
    examples, count = indices.shape[0], centers.shape[1]
    classes = alpha.shape[0]
    steps = examples // block
    return pl.pallas_call(
        tile_kernel,
        grid=(steps,),
        in_specs=[
            pl.BlockSpec((1, 1, block), lambda i: (i, 0, 0)),
            pl.BlockSpec((chunks, features, lanes), lambda i: (0, 0, 0)),
            pl.BlockSpec((features, count), lambda i: (0, 0)),
            pl.BlockSpec((classes, count), lambda i: (0, 0)),
        ],
        out_specs=[
            pl.BlockSpec((block, count), lambda i: (i, 0)),
            pl.BlockSpec((block // share, classes, share), lambda i: (i, 0, 0)),
        ],
        out_shape=[
            jax.ShapeDtypeStruct((examples, count), BF16),
            jax.ShapeDtypeStruct((examples // share, classes, share), F32),
        ],
        scratch_shapes=[pltpu.VMEM((features + 16, count), BF16)],
        compiler_params=pltpu.CompilerParams(vmem_limit_bytes=VMEM_BYTES),
        cost_estimate=pl.CostEstimate(flops=4 << 30, bytes_accessed=10 << 20, transcendentals=4 << 20),
        name="tile",
    )(indices.reshape(steps, 1, block), row_pool, centers, alpha)


def forward_kernel(lifted_ref, tile_ref, rows_ref):
    half = lifted_ref.shape[2]
    share = rows_ref.shape[2]
    rows = sum(
        lax.dot_general(
            lifted_ref[k],
            tile_ref[:, k * half : (k + 1) * half],
            (((1,), (1,)), ((), ())),
            preferred_element_type=F32,
        )
        for k in range(lifted_ref.shape[0])
    )
    for k in range(rows_ref.shape[0]):
        rows_ref[k] = rows[:, k * share : (k + 1) * share]


def forward(lifted, tile, share):
    block = 256
    halves, classes, half = lifted.shape
    examples, count = tile.shape
    return pl.pallas_call(
        forward_kernel,
        grid=(examples // block,),
        in_specs=[
            pl.BlockSpec((halves, classes, half), lambda i: (0, 0, 0)),
            pl.BlockSpec((block, count), lambda i: (i, 0)),
        ],
        out_specs=pl.BlockSpec((block // share, classes, share), lambda i: (i, 0, 0)),
        out_shape=jax.ShapeDtypeStruct((examples // share, classes, share), F32),
        compiler_params=pltpu.CompilerParams(vmem_limit_bytes=VMEM_BYTES),
        cost_estimate=pl.CostEstimate(flops=1208 << 20, bytes_accessed=10 << 20, transcendentals=0),
        name="forward",
    )(lifted, tile)


def backward_kernel(values_ref, tile_ref, sums_ref, flat_ref):
    share = values_ref.shape[2]

    @pl.when(pl.program_id(0) == 0)
    def _():
        for k in range(values_ref.shape[0]):
            flat_ref[:, k * share : (k + 1) * share] = values_ref[k]

    sums_ref[0] = jnp.dot(flat_ref[...], tile_ref[...], preferred_element_type=F32)


def backward(values, tile):
    block = 512
    shares, classes, share = values.shape
    examples, count = tile.shape
    half = count // 2
    per_half = half // block
    return pl.pallas_call(
        backward_kernel,
        grid=(count // block,),
        in_specs=[
            pl.BlockSpec((shares, classes, share), lambda i: (0, 0, 0)),
            pl.BlockSpec((examples, block), lambda i: (0, i)),
        ],
        out_specs=pl.BlockSpec((1, classes, block), lambda i: (i // per_half, 0, i % per_half)),
        out_shape=jax.ShapeDtypeStruct((2, classes, half), F32),
        scratch_shapes=[pltpu.VMEM((classes, examples), BF16)],
        compiler_params=pltpu.CompilerParams(vmem_limit_bytes=VMEM_BYTES),
        cost_estimate=pl.CostEstimate(flops=1208 << 20, bytes_accessed=10 << 20, transcendentals=0),
        name="backward",
    )(values, tile)


def blocks_of(factor, vectors):
    order = factor.shape[1]
    return factor.reshape(-1, order, order), vectors.reshape(vectors.shape[0], -1, order)


def apply_blocks(factor, vectors):
    blocks, pieces = blocks_of(factor, vectors)
    return jnp.einsum("kij,ckj->cki", blocks, pieces, precision=lax.Precision.HIGHEST).reshape(
        vectors.shape
    )


def apply_transposed(factor, vectors):
    blocks, pieces = blocks_of(factor, vectors)
    return jnp.einsum("kij,cki->ckj", blocks, pieces, precision=lax.Precision.HIGHEST).reshape(
        vectors.shape
    )


def exchange(array, axis, pairs):
    return lax.ppermute(array, axis, pairs)


def shards(pool, indices, labels, example_weight, centers, alpha, precond):
    n_ex, n_ctr = lax.axis_size("ex"), lax.axis_size("ctr")
    classes = alpha.shape[0]
    examples = indices.shape[0]
    share = examples // n_ctr
    total = float(examples * n_ex)
    core = lax.axis_index("ex") % 2
    rows_y = n_ex // 2

    def pairs_y(flip):
        return [(2 * y + c, 2 * (y ^ flip) + c) for y in range(rows_y) for c in range(2)]

    core_pairs = [(i, i ^ 1) for i in range(n_ex)]

    def to_all(block):
        return lax.all_to_all(jnp.broadcast_to(block, (n_ctr,) + block.shape), "ctr", 0, 0)

    def sum_shares(parts):
        return jnp.sum(lax.all_to_all(parts, "ctr", 0, 0), axis=0)

    def with_rows(parts, vectors):
        flat = jnp.stack(vectors)
        flat = jnp.pad(flat, ((0, 0), (0, 2 * share - classes))).reshape(-1, share)
        flat = jnp.pad(flat, ((0, 8 - flat.shape[0]), (0, 0)))
        return jnp.concatenate(
            [parts, jnp.broadcast_to(flat, (parts.shape[0],) + flat.shape)], axis=1
        )

    def from_rows(summed, number):
        return [
            summed[classes + 2 * k : classes + 2 * k + 2].reshape(-1)[:classes]
            for k in range(number)
        ]

    def sum_examples(halves, vector=None):
        mine = lax.dynamic_index_in_dim(halves, core, 0, False)
        other = lax.dynamic_index_in_dim(halves, 1 - core, 0, False)
        if vector is not None:
            row = jnp.pad(vector, (0, mine.shape[1] - classes))[None, :]
            rows = jnp.pad(row, ((0, 7), (0, 0)))
            mine = jnp.concatenate([mine, rows], axis=0)
            other = jnp.concatenate([other, rows], axis=0)
        mine = mine + lax.ppermute(other, "ex", core_pairs)
        wide = mine.shape[1] // 2
        one, two = mine[:, :wide], mine[:, wide:]
        one = one + lax.ppermute(one, "ex", pairs_y(1))
        two = two + lax.ppermute(two, "ex", pairs_y(3))
        one = one + lax.ppermute(one, "ex", pairs_y(3))
        two = two + lax.ppermute(two, "ex", pairs_y(1))
        sums = jnp.concatenate([one[:classes], two[:classes]], axis=1)
        return sums if vector is None else (sums, one[classes, :classes])

    def both_halves(half):
        other = lax.ppermute(half, "ex", core_pairs)
        first = jnp.where(core == 0, half, other)
        second = jnp.where(core == 0, other, half)
        return jnp.stack([first, second])

    def over_cores(vector):
        return vector + lax.ppermute(vector, "ex", core_pairs)

    half = centers.shape[1] // 2
    factor = lax.dynamic_slice_in_dim(precond, core * half, half, 0)
    offset = lax.axis_index("ctr") * share
    label = lax.dynamic_slice_in_dim(labels, offset, share, 0)
    weight = lax.dynamic_slice_in_dim(example_weight, offset, share, 0)

    row_pool = to_all(pool)
    tile, base_parts = make_tile(row_pool, indices, centers, alpha, share)
    base = sum_shares(base_parts)
    probability = jax.nn.sigmoid(base)
    target = (label[None, :] == jnp.arange(classes, dtype=jnp.int32)[:, None]).astype(F32)
    hessian = weight[None, :] * probability * (1.0 - probability)
    gradient = (weight[None, :] * (probability - target)).astype(BF16)

    pulled = sum_examples(backward(to_all(gradient), tile))
    residual0 = -apply_transposed(factor, pulled) / total
    lifted0 = both_halves(apply_blocks(factor, residual0).astype(BF16))
    norm0_part = over_cores(jnp.sum(residual0 * residual0, axis=1))
    summed = sum_shares(with_rows(forward(lifted0, tile, share), [norm0_part]))
    image0 = summed[:classes]
    (norm0,) = from_rows(summed, 1)

    weighted = (hessian * image0).astype(BF16)
    curve_part = jnp.sum(weighted.astype(F32) * image0, axis=1)
    curve_rows = jnp.pad(
        jnp.pad(jnp.stack(split3(curve_part)), ((0, 0), (0, 2 * share - classes))).reshape(-1, share),
        ((0, 10), (0, 0)),
    )
    spread = to_all(jnp.concatenate([weighted, curve_rows.astype(BF16)], axis=0))
    curve_row = jnp.sum(
        spread[:, classes : classes + 6].astype(F32).reshape(-1, 3, 2 * share), axis=(0, 1)
    )[:classes]
    sums, curve = sum_examples(backward(spread[:, :classes], tile), curve_row)
    image = apply_transposed(factor, sums) / total + RIDGE * residual0
    rough = norm0 / (curve / total + RIDGE * norm0)
    residual1 = residual0 - rough[:, None] * image
    lifted1 = both_halves(apply_blocks(factor, residual1).astype(BF16))
    cross_part = over_cores(jnp.sum(residual0 * residual1, axis=1))
    norm1_part = over_cores(jnp.sum(residual1 * residual1, axis=1))
    summed = sum_shares(with_rows(forward(lifted1, tile, share), [cross_part, norm1_part]))
    image1 = summed[:classes]
    cross, norm1 = from_rows(summed, 2)

    excess = cross / (norm0 - cross)
    step0 = rough * (1.0 + excess)
    norm_next = (1.0 + excess) * ((1.0 + excess) * norm1 - 2.0 * excess * cross) + excess * excess * norm0
    ratio = norm_next / norm0
    rows = (1.0 + excess)[:, None] * image1 + (ratio - excess)[:, None] * image0
    curve1 = jnp.sum((hessian * rows).astype(BF16).astype(F32) * rows, axis=1)
    curve1 = jnp.sum(lax.all_to_all(jnp.broadcast_to(curve1, (n_ex, classes)), "ex", 0, 0), axis=0)
    curve1 = jnp.sum(lax.all_to_all(jnp.broadcast_to(curve1, (n_ctr, classes)), "ctr", 0, 0), axis=0)
    step1 = norm_next / (curve1 / total + RIDGE * (norm_next + ratio * ratio * norm0))
    return base + step0[:, None] * image0 + step1[:, None] * rows


def solution(mesh):
    return jax.shard_map(
        shards,
        mesh=mesh,
        in_specs=(
            P(None, ("ex", "ctr")),
            P("ex"),
            P("ex"),
            P("ex"),
            P(None, "ctr"),
            P(None, "ctr"),
            P("ctr", None),
        ),
        out_specs=P(None, ("ex", "ctr")),
        check_vma=False,
    )
```

```python
import functools
import math

import jax
import jax.numpy as jnp
from jax import lax
from jax.experimental import pallas as pl
from jax.experimental.pallas import tpu as pltpu
from jax.sharding import PartitionSpec as P

RIDGE = 0.0001
F32 = jnp.float32
BF16 = jnp.bfloat16
VMEM_BYTES = 24 * 1024 * 1024
DEPTH = 128
BAND = 256
EXTRA = 16
LANES = 128
NT = (((1,), (1,)), ((), ()))
TN = (((0,), (0,)), ((), ()))


def split3(values):
    high = values.astype(BF16)
    rest = values - high.astype(F32)
    middle = rest.astype(BF16)
    low = (rest - middle.astype(F32)).astype(BF16)
    return high, middle, low


SCALAR = pl.BlockSpec(memory_space=pltpu.SMEM)
WHOLE = pl.BlockSpec(memory_space=pltpu.VMEM)


def call(kernel, name, out_shape, flops, scratch=(), scalars=0, arrays=0):
    shapes = out_shape if isinstance(out_shape, list) else [out_shape]
    size = sum(math.prod(s.shape) * s.dtype.itemsize for s in shapes)
    return pl.pallas_call(
        kernel,
        out_shape=out_shape,
        scratch_shapes=list(scratch),
        in_specs=[SCALAR] * scalars + [WHOLE] * arrays,
        compiler_params=pltpu.CompilerParams(vmem_limit_bytes=VMEM_BYTES),
        cost_estimate=pl.CostEstimate(flops=flops, bytes_accessed=size, transcendentals=0),
        name=name,
    )


def rows_of(vectors):
    row = lax.broadcasted_iota(jnp.int32, (EXTRA, LANES), 0)
    out = jnp.zeros((EXTRA, LANES), F32)
    for k, vector in enumerate(vectors):
        for p, piece in enumerate(split3(vector)):
            for q in range(2):
                value = piece.astype(F32)[:, q * LANES : (q + 1) * LANES]
                out = jnp.where(row == 6 * k + 2 * p + q, value, out)
    return out.astype(BF16)


def read_rows(summed, k):
    halves = [
        sum(summed[6 * k + 2 * p + q : 6 * k + 2 * p + q + 1] for p in range(3)) for q in range(2)
    ]
    return jnp.concatenate(halves, axis=1)


def column(vector, classes):
    return jnp.broadcast_to(vector, (8, vector.shape[1])).T[:classes, :1]


def lane_sums(values):
    folded = sum(values[:, k : k + LANES] for k in range(0, values.shape[1], LANES))
    empty = jnp.zeros((2 * LANES - values.shape[0], LANES), F32)
    return jnp.sum(jnp.concatenate([folded, empty], axis=0).T, axis=0, keepdims=True)


def stack_rows(vectors):
    row = lax.broadcasted_iota(jnp.int32, (8, 2 * LANES), 0)
    out = jnp.zeros((8, 2 * LANES), F32)
    for k, vector in enumerate(vectors):
        out = jnp.where(row == k, vector, out)
    return out


def sum_parts(ref):
    total = ref[0].astype(F32)
    for k in range(1, ref.shape[0]):
        total = total + ref[k].astype(F32)
    return total


def shape(dims, dtype):
    return jax.ShapeDtypeStruct(dims, dtype)


def tail(squares, first, pad):
    pieces = [p.astype(F32) for p in split3(-0.5 * squares)]
    row = lax.broadcasted_iota(jnp.int32, (pad, squares.shape[1]), 0)
    out = jnp.where((row >= 3 - first) & (row < 6 - first), 1.0, 0.0)
    for k in range(3):
        out = jnp.where(row == k + first, pieces[k], out)
    return out


def prepare_kernel(index_ref, centers_ref, sides_ref, one_hot_ref):
    features, count = centers_ref.shape
    lanes = one_hot_ref.shape[0]
    center_float = centers_ref[...].astype(F32)
    center_sq = jnp.sum(center_float * center_float, axis=0, keepdims=True)
    side = jnp.concatenate([center_float, tail(center_sq, 3, DEPTH - features)], axis=0)
    sides_ref[...] = side.T.astype(BF16)
    within = index_ref[...] % lanes
    row = lax.broadcasted_iota(jnp.int32, (lanes, index_ref.shape[1]), 0)
    one_hot_ref[...] = (row == within).astype(F32).astype(BF16)


def prepare(indices, centers, lanes):
    features, count = centers.shape
    examples = indices.shape[0]
    return call(
        prepare_kernel,
        "prepare",
        [shape((count, DEPTH), BF16), shape((lanes, examples), BF16)],
        1 << 20,
        arrays=2,
    )(indices.reshape(1, examples), centers)


def tile_kernel(index_ref, pool_ref, one_hot_ref, sides_ref, alpha_ref, tile_ref, high_ref, low_ref, side_ref):
    chunks, features, lanes = pool_ref.shape
    count, examples = tile_ref.shape
    share = high_ref.shape[2]
    scale = 4.0 / features * math.log2(math.e)
    pool = pool_ref[...].reshape(chunks * features, lanes)

    def gather(b, carry):
        here = pl.ds(pl.multiple_of(b * BAND, BAND), BAND)
        chunk = index_ref[:, here] // lanes
        picked = jnp.dot(pool, one_hot_ref[:, here], preferred_element_type=F32)
        points = jnp.where(chunk == 0, picked[:features], 0.0)
        for k in range(1, chunks):
            points = jnp.where(chunk == k, picked[k * features : (k + 1) * features], points)
        point_sq = jnp.sum(points * points, axis=0, keepdims=True)
        side = jnp.concatenate([points, tail(point_sq, 0, DEPTH - features)], axis=0)
        side_ref[:, here] = side.astype(BF16)
        return carry

    lax.fori_loop(0, examples // BAND, gather, 0, unroll=True)

    def fill(b, carry):
        rows = pl.ds(pl.multiple_of(b * BAND, BAND), BAND)
        near = jnp.dot(sides_ref[rows, :], side_ref[...], preferred_element_type=F32)
        tile_ref[rows, :] = jnp.exp2(near * scale).astype(BF16)
        return carry

    lax.fori_loop(0, count // BAND, fill, 0, unroll=2)

    def product(b, carry):
        here = pl.ds(pl.multiple_of(b * BAND, BAND), BAND)
        rows = jnp.dot(alpha_ref[...], tile_ref[:, here], preferred_element_type=F32)
        for k in range(BAND // share):
            piece = rows[:, k * share : (k + 1) * share]
            high = piece.astype(BF16)
            high_ref[b * (BAND // share) + k] = high
            low_ref[b * (BAND // share) + k] = (piece - high.astype(F32)).astype(BF16)
        return carry

    lax.fori_loop(0, examples // BAND, product, 0, unroll=True)


def make_tile(indices, row_pool, one_hot, sides, alpha, share):
    examples, count = indices.shape[0], sides.shape[0]
    classes = alpha.shape[0]
    parts = shape((examples // share, classes, share), BF16)
    return call(
        tile_kernel,
        "tile",
        [shape((count, examples), BF16), parts, parts],
        4 << 30,
        [pltpu.VMEM((DEPTH, examples), BF16)],
        arrays=5,
    )(indices.reshape(1, examples), row_pool, one_hot, sides, alpha)


def turn_kernel(tile_ref, turned_ref):
    count, examples = tile_ref.shape

    def band(b, carry):
        start = pl.multiple_of(b * BAND, BAND)
        turned_ref[:, pl.ds(start, BAND)] = tile_ref[pl.ds(start, BAND), :].T
        return carry

    lax.fori_loop(0, count // BAND, band, 0)


def turn(tile):
    return call(turn_kernel, "turn", shape(tile.shape[::-1], BF16), 8 << 20, arrays=1)(tile)


def factors_kernel(core_ref, precond_ref, high_ref, low_ref, high_turned_ref, low_turned_ref):
    order = precond_ref.shape[1]
    half = high_ref.shape[0]
    first = core_ref[0] * half
    for k in range(half // order):
        here = slice(k * order, (k + 1) * order)
        block = precond_ref[pl.ds(pl.multiple_of(first + k * order, order), order), :]
        high = block.astype(BF16)
        high_ref[here] = high
        low_ref[here] = (block - high.astype(F32)).astype(BF16)
        turned = block.T
        high = turned.astype(BF16)
        high_turned_ref[here] = high
        low_turned_ref[here] = (turned - high.astype(F32)).astype(BF16)


def factors(core, precond):
    out = shape((precond.shape[0] // 2, precond.shape[1]), BF16)
    return call(factors_kernel, "factors", [out] * 4, 1 << 20, scalars=1, arrays=1)(core, precond)


def block_products(values, high_ref, low_ref):
    order = high_ref.shape[1]
    out = []
    for k in range(high_ref.shape[0] // order):
        here = slice(k * order, (k + 1) * order)
        block = values[:, here]
        high = block.astype(BF16)
        low = (block - high.astype(F32)).astype(BF16)
        product = jnp.dot(high, high_ref[here], preferred_element_type=F32)
        product += jnp.dot(high, low_ref[here], preferred_element_type=F32)
        product += jnp.dot(low, high_ref[here], preferred_element_type=F32)
        out.append(product)
    return jnp.concatenate(out, axis=1)


def forward_kernel(
    core_ref, own_ref, other_ref, own_part_ref, other_part_ref, tile_ref, high_ref, low_ref
):
    classes, half = own_ref.shape
    share = high_ref.shape[2]
    examples = tile_ref.shape[1]
    mine = pl.ds(pl.multiple_of(core_ref[0] * half, half), half)
    theirs = pl.ds(pl.multiple_of((1 - core_ref[0]) * half, half), half)
    part = own_part_ref[...] + other_part_ref[...]
    extra = rows_of([part[:1], part[1:2]])
    for b in range(examples // BAND):
        here = slice(b * BAND, (b + 1) * BAND)
        rows = jnp.dot(own_ref[...], tile_ref[mine, here], preferred_element_type=F32)
        rows += jnp.dot(other_ref[...], tile_ref[theirs, here], preferred_element_type=F32)
        for k in range(BAND // share):
            piece = rows[:, k * share : (k + 1) * share]
            high = piece.astype(BF16)
            at = b * (BAND // share) + k
            high_ref[at, :classes] = high
            high_ref[at, classes:] = extra
            low_ref[at] = (piece - high.astype(F32)).astype(BF16)


def forward(core, own, other, own_part, other_part, tile, share):
    classes = own.shape[0]
    shares = tile.shape[1] // share
    return call(
        forward_kernel,
        "forward",
        [shape((shares, classes + EXTRA, share), BF16), shape((shares, classes, share), BF16)],
        1208 << 20,
        scalars=1,
        arrays=5,
    )(core, own, other, own_part, other_part, tile)


def backward_kernel(core_ref, values_ref, turned_ref, other_ref, one_ref, two_ref, flat_ref):
    shares, height, share = values_ref.shape
    classes, examples = flat_ref.shape
    half = other_ref.shape[1]
    wide = half // 2
    for k in range(shares):
        flat_ref[:, k * share : (k + 1) * share] = values_ref[k, :classes]
    if height > classes:
        total = values_ref[0, classes:].astype(F32)
        for k in range(1, shares):
            total = total + values_ref[k, classes:].astype(F32)
        row = read_rows(total, 0)
        other_ref[classes:, : 2 * LANES] = jnp.broadcast_to(row, (8, 2 * LANES))
        other_ref[classes:, 2 * LANES :] = jnp.zeros((8, half - 2 * LANES), F32)
        one_ref[classes:, : 2 * LANES] = jnp.broadcast_to(row, (8, 2 * LANES))
        one_ref[classes:, 2 * LANES :] = jnp.zeros((8, wide - 2 * LANES), F32)
    for h, first in enumerate(((1 - core_ref[0]) * half, core_ref[0] * half)):
        for b in range(half // BAND):
            there = pl.ds(pl.multiple_of(first + b * BAND, BAND), BAND)
            sums = jnp.dot(flat_ref[...], turned_ref[:, there], preferred_element_type=F32)
            if h == 0:
                other_ref[:classes, b * BAND : (b + 1) * BAND] = sums
            elif b * BAND < wide:
                one_ref[:classes, b * BAND : (b + 1) * BAND] = sums
            else:
                two_ref[:, b * BAND - wide : (b + 1) * BAND - wide] = sums


def backward(core, values, turned, classes):
    examples, count = turned.shape
    height = classes + (8 if values.shape[1] > classes else 0)
    half = count // 2
    return call(
        backward_kernel,
        "backward",
        [shape((height, half), F32), shape((height, half // 2), F32), shape((classes, half // 2), F32)],
        1208 << 20,
        [pltpu.VMEM((classes, examples), BF16)],
        scalars=1,
        arrays=2,
    )(core, values, turned)


def gradient_kernel(parts_ref, label_ref, weight_ref, base_ref, hessian_ref, send_ref):
    classes, share = base_ref.shape
    base = sum_parts(parts_ref)
    base_ref[...] = base
    probability = jax.nn.sigmoid(base)
    row = lax.broadcasted_iota(jnp.int32, (classes, share), 0)
    target = jnp.where(row == label_ref[...], 1.0, 0.0)
    hessian_ref[...] = weight_ref[...] * probability * (1.0 - probability)
    gradient = (weight_ref[...] * (probability - target)).astype(BF16)
    for k in range(send_ref.shape[0]):
        send_ref[k] = gradient


def gradient(parts, label, weight):
    block = shape(parts.shape[1:], F32)
    return call(
        gradient_kernel, "gradient", [block, block, shape(parts.shape, BF16)], 1 << 20, arrays=3
    )(parts, label, weight)


def residual_kernel(
    total, one_ref, one_in_ref, two_ref, two_in_ref, high_ref, low_ref, high_turned_ref,
    low_turned_ref, residual_ref, lifted_ref, part_ref,
):
    sums = jnp.concatenate([one_ref[...] + one_in_ref[...], two_ref[...] + two_in_ref[...]], axis=1)
    residual = block_products(sums, high_ref, low_ref) * (-1.0 / total)
    residual_ref[...] = residual
    lifted_ref[...] = block_products(residual, high_turned_ref, low_turned_ref).astype(BF16)
    part_ref[...] = stack_rows([lane_sums(residual * residual)])


def first_residual(total, sums, blocks):
    classes, wide = sums[2].shape
    return call(
        functools.partial(residual_kernel, total),
        "residual",
        [
            shape((classes, 2 * wide), F32),
            shape((classes, 2 * wide), BF16),
            shape((8, 2 * LANES), F32),
        ],
        450 << 20,
        arrays=8,
    )(*sums, *blocks)


def weigh_kernel(parts_ref, hessian_ref, image_ref, norm_ref, send_ref):
    classes = hessian_ref.shape[0]
    total = sum_parts(parts_ref)
    image = total[:classes]
    image_ref[...] = image
    norm_ref[...] = stack_rows([read_rows(total[classes:], 0)])
    weighted = (hessian_ref[...] * image).astype(BF16)
    extra = rows_of([lane_sums(weighted.astype(F32) * image)])
    for k in range(send_ref.shape[0]):
        send_ref[k, :classes] = weighted
        send_ref[k, classes:] = extra


def weigh(parts, hessian):
    return call(
        weigh_kernel,
        "weigh",
        [shape(hessian.shape, F32), shape((8, 2 * LANES), F32), shape(parts.shape, BF16)],
        1 << 20,
        arrays=2,
    )(parts, hessian)


def step_kernel(
    total, one_ref, one_in_ref, two_ref, two_in_ref, high_ref, low_ref, high_turned_ref,
    low_turned_ref, residual_ref, norm_ref, lifted_ref, part_ref, rough_ref,
):
    classes = residual_ref.shape[0]
    one = one_ref[...] + one_in_ref[...]
    curve = one[classes : classes + 1, : 2 * LANES] / total
    norm = norm_ref[:1]
    lane = lax.broadcasted_iota(jnp.int32, (1, 2 * LANES), 1)
    rough = jnp.where(lane < classes, norm / (curve + RIDGE * norm), 0.0)
    rough_ref[...] = stack_rows([rough])
    sums = jnp.concatenate([one[:classes], two_ref[...] + two_in_ref[...]], axis=1)
    old = residual_ref[...]
    image = block_products(sums, high_ref, low_ref) / total + RIDGE * old
    new = old - column(rough, classes) * image
    lifted_ref[...] = block_products(new, high_turned_ref, low_turned_ref).astype(BF16)
    part_ref[...] = stack_rows([lane_sums(old * new), lane_sums(new * new)])


def step(total, sums, blocks, residual, norm):
    row = shape((8, 2 * LANES), F32)
    return call(
        functools.partial(step_kernel, total),
        "step",
        [shape(residual.shape, BF16), row, row],
        450 << 20,
        arrays=10,
    )(*sums, *blocks, residual, norm)


def curve_kernel(
    parts_ref, hessian_ref, image_ref, norm_ref, rough_ref, last_ref, scales_ref, curve_ref
):
    classes = hessian_ref.shape[0]
    total = sum_parts(parts_ref)
    last = total[:classes]
    last_ref[...] = last
    cross = read_rows(total[classes:], 0)
    norm_rough = read_rows(total[classes:], 1)
    norm = norm_ref[:1]
    lane = lax.broadcasted_iota(jnp.int32, (1, 2 * LANES), 1)
    excess = jnp.where(lane < classes, cross / (norm - cross), 0.0)
    grown = 1.0 + excess
    norm_next = grown * (grown * norm_rough - 2.0 * excess * cross) + excess * excess * norm
    ratio = jnp.where(lane < classes, norm_next / norm, 0.0)
    ridge = RIDGE * (norm_next + ratio * ratio * norm)
    scales_ref[...] = stack_rows(
        [rough_ref[:1] * grown, grown, ratio - excess, norm_next, ridge]
    )
    rows = column(grown, classes) * last + column(ratio - excess, classes) * image_ref[...]
    weighted = (hessian_ref[...] * rows).astype(BF16).astype(F32)
    curve_ref[...] = stack_rows([lane_sums(weighted * rows)])


def last_curve(parts, hessian, image, norm, rough):
    row = shape((8, 2 * LANES), F32)
    return call(
        curve_kernel,
        "curve",
        [shape(hessian.shape, F32), row, row],
        1 << 20,
        arrays=5,
    )(parts, hessian, image, norm, rough)


def margins_kernel(
    total, curve_ref, scales_ref, base_ref, base_low_ref, image_ref, image_low_ref, last_ref,
    last_low_ref, margins_ref,
):
    classes = base_ref.shape[0]
    curve = jnp.sum(curve_ref[:, 0], axis=0, keepdims=True)
    first, grown, other = scales_ref[0:1], scales_ref[1:2], scales_ref[2:3]
    lane = lax.broadcasted_iota(jnp.int32, (1, 2 * LANES), 1)
    second = jnp.where(
        lane < classes, scales_ref[3:4] / (curve / total + scales_ref[4:5]), 0.0
    )
    base = base_ref[...] + sum_parts(base_low_ref)
    image = image_ref[...] + sum_parts(image_low_ref)
    last = last_ref[...] + sum_parts(last_low_ref)
    margins_ref[...] = (
        base
        + column(first + second * other, classes) * image
        + column(second * grown, classes) * last
    )


def margins(total, curve, scales, base, base_low, image, image_low, last, last_low):
    return call(
        functools.partial(margins_kernel, total),
        "margins",
        shape(base.shape, F32),
        1 << 20,
        arrays=8,
    )(curve, scales, base, base_low, image, image_low, last, last_low)


def shards(pool, indices, labels, example_weight, centers, alpha, precond):
    n_ex, n_ctr = lax.axis_size("ex"), lax.axis_size("ctr")
    classes, count = alpha.shape
    examples = indices.shape[0]
    share = examples // n_ctr
    total = float(examples * n_ex)
    core = (lax.axis_index("ex") % 2).reshape(1)
    core_pairs = [(i, i ^ 1) for i in range(n_ex)]

    def over_y(array, flip):
        pairs = [(2 * y + c, 2 * (y ^ flip) + c) for y in range(n_ex // 2) for c in range(2)]
        return lax.ppermute(array, "ex", pairs)

    def over_cores(array):
        return lax.ppermute(array, "ex", core_pairs)

    def trade(parts):
        return lax.all_to_all(parts, "ctr", 0, 0)

    def tie(first, second):
        return lax.optimization_barrier((first, second))

    def sum_examples(products, low):
        other, one, two = products
        got = over_cores(other)
        wide = one.shape[1]
        one = one + got[:, :wide]
        two = two + got[:classes, wide:]
        one, low = tie(one, low)
        low = trade(low)
        one = one + over_y(one, 1)
        two = two + over_y(two, 3)
        one_in, two_in = over_y(one, 3), over_y(two, 1)
        one_in, low = tie(one_in, low)
        return (one, one_in, two, two_in), low

    offset = lax.axis_index("ctr") * share
    label = lax.dynamic_slice_in_dim(labels, offset, share, 0).reshape(1, share)
    weight = lax.dynamic_slice_in_dim(example_weight, offset, share, 0).reshape(1, share)

    row_pool = trade(jnp.broadcast_to(pool, (n_ctr,) + pool.shape))
    sides, one_hot = prepare(indices, centers, pool.shape[1])
    tile, base_high, base_low = make_tile(indices, row_pool, one_hot, sides, alpha, share)
    base_parts = trade(base_high)
    turned = turn(tile)
    blocks = factors(core, precond)
    base, hessian, send = gradient(base_parts, label, weight)

    sums, base_low = sum_examples(backward(core, trade(send), turned, classes), base_low)
    residual, lifted, part = first_residual(total, sums, blocks)
    high, image_low = forward(
        core, lifted, over_cores(lifted), part, over_cores(part), tile, share
    )
    image, norm, send = weigh(trade(high), hessian)

    sums, image_low = sum_examples(backward(core, trade(send), turned, classes), image_low)
    lifted, part, rough = step(total, sums, blocks, residual, norm)
    high, last_low = forward(core, lifted, over_cores(lifted), part, over_cores(part), tile, share)
    last, scales, curve = last_curve(trade(high), hessian, image, norm, rough)

    curve, last_low = tie(curve, last_low)
    last_low = trade(last_low)
    curve = curve + over_cores(curve)
    curve = curve + over_y(curve, 1)
    curve = curve + over_y(curve, 3)
    curve, last_low = tie(curve, last_low)
    curve = trade(jnp.broadcast_to(curve, (n_ctr,) + curve.shape))
    return margins(total, curve, scales, base, base_low, image, image_low, last, last_low)


def solution(mesh):
    return jax.shard_map(
        shards,
        mesh=mesh,
        in_specs=(
            P(None, ("ex", "ctr")),
            P("ex"),
            P("ex"),
            P("ex"),
            P(None, "ctr"),
            P(None, "ctr"),
            P("ctr", None),
        ),
        out_specs=P(None, ("ex", "ctr")),
        check_vma=False,
    )
```

```python
import functools
import math

import jax
import jax.numpy as jnp
from jax import lax
from jax.experimental import pallas as pl
from jax.experimental.pallas import tpu as pltpu
from jax.sharding import PartitionSpec as P

RIDGE = 0.0001
F32 = jnp.float32
F16 = jnp.float16
BF16 = jnp.bfloat16
VMEM_BYTES = 24 * 1024 * 1024
DEPTH = 128
BAND = 256
EXTRA = 16
LANES = 128
NT = (((1,), (1,)), ((), ()))
TN = (((0,), (0,)), ((), ()))


def split3(values):
    high = values.astype(BF16)
    rest = values - high.astype(F32)
    middle = rest.astype(BF16)
    low = (rest - middle.astype(F32)).astype(BF16)
    return high, middle, low


SCALAR = pl.BlockSpec(memory_space=pltpu.SMEM)
WHOLE = pl.BlockSpec(memory_space=pltpu.VMEM)


def call(kernel, name, out_shape, flops, scratch=(), scalars=0, arrays=0):
    shapes = out_shape if isinstance(out_shape, list) else [out_shape]
    size = sum(math.prod(s.shape) * s.dtype.itemsize for s in shapes)
    return pl.pallas_call(
        kernel,
        out_shape=out_shape,
        scratch_shapes=list(scratch),
        in_specs=[SCALAR] * scalars + [WHOLE] * arrays,
        compiler_params=pltpu.CompilerParams(vmem_limit_bytes=VMEM_BYTES),
        cost_estimate=pl.CostEstimate(flops=flops, bytes_accessed=size, transcendentals=0),
        name=name,
    )


def rows_of(vectors):
    row = lax.broadcasted_iota(jnp.int32, (EXTRA, LANES), 0)
    out = jnp.zeros((EXTRA, LANES), F32)
    for k, vector in enumerate(vectors):
        for p, piece in enumerate(split3(vector)):
            for q in range(2):
                value = piece.astype(F32)[:, q * LANES : (q + 1) * LANES]
                out = jnp.where(row == 6 * k + 2 * p + q, value, out)
    return out.astype(BF16)


def read_rows(summed, k):
    halves = [
        sum(summed[6 * k + 2 * p + q : 6 * k + 2 * p + q + 1] for p in range(3)) for q in range(2)
    ]
    return jnp.concatenate(halves, axis=1)


def exponents(bounds):
    return jnp.ceil(jnp.log2(jnp.maximum(bounds, 1e-30)))


def half_rows(powers, vectors):
    row = lax.broadcasted_iota(jnp.int32, (EXTRA, LANES), 0)
    pieces = [powers]
    for vector in vectors:
        power = exponents(jnp.abs(vector)) + 1.0
        scaled = vector * jnp.exp2(-power) * 2048.0
        high = jnp.floor(scaled + 0.5)
        pieces += [power, high / 2048.0, jnp.floor((scaled - high) * 2048.0 + 0.5) / 2048.0]
    out = jnp.zeros((EXTRA, LANES), F32)
    for p, piece in enumerate(pieces):
        for q in range(2):
            out = jnp.where(row == 2 * p + q, piece[:, q * LANES : (q + 1) * LANES], out)
    return out


def half_row(parts_ref, first, p):
    rows = [parts_ref[:, first + 2 * p + q, :] for q in range(2)]
    return jnp.concatenate(rows, axis=1)


def half_vector(parts_ref, first, k):
    power, high, low = (half_row(parts_ref, first, 1 + 3 * k + p) for p in range(3))
    return jnp.sum(jnp.exp2(power) * (high + low / 2048.0), axis=0, keepdims=True)


def sum_scaled(parts_ref, classes):
    scales = jnp.exp2(half_row(parts_ref, classes, 0)).T
    total = parts_ref[0, :classes] * scales[:classes, :1]
    for k in range(1, parts_ref.shape[0]):
        total = total + parts_ref[k, :classes] * scales[:classes, k : k + 1]
    return total


def column(vector, classes):
    return jnp.broadcast_to(vector, (8, vector.shape[1])).T[:classes, :1]


def lane_sums(values):
    folded = sum(values[:, k : k + LANES] for k in range(0, values.shape[1], LANES))
    empty = jnp.zeros((2 * LANES - values.shape[0], LANES), F32)
    return jnp.sum(jnp.concatenate([folded, empty], axis=0).T, axis=0, keepdims=True)


def stack_rows(vectors):
    row = lax.broadcasted_iota(jnp.int32, (8, 2 * LANES), 0)
    out = jnp.zeros((8, 2 * LANES), F32)
    for k, vector in enumerate(vectors):
        out = jnp.where(row == k, vector, out)
    return out


def sum_parts(ref):
    total = ref[0].astype(F32)
    for k in range(1, ref.shape[0]):
        total = total + ref[k].astype(F32)
    return total


def shape(dims, dtype):
    return jax.ShapeDtypeStruct(dims, dtype)


def tail(squares, first, pad):
    pieces = [p.astype(F32) for p in split3(-0.5 * squares)]
    row = lax.broadcasted_iota(jnp.int32, (pad, squares.shape[1]), 0)
    out = jnp.where((row >= 3 - first) & (row < 6 - first), 1.0, 0.0)
    for k in range(3):
        out = jnp.where(row == k + first, pieces[k], out)
    return out


def prepare_kernel(index_ref, centers_ref, sides_ref, one_hot_ref):
    features, count = centers_ref.shape
    lanes = one_hot_ref.shape[0]
    center_float = centers_ref[...].astype(F32)
    center_sq = jnp.sum(center_float * center_float, axis=0, keepdims=True)
    side = jnp.concatenate([center_float, tail(center_sq, 3, DEPTH - features)], axis=0)
    sides_ref[...] = side.T.astype(BF16)
    within = index_ref[...] % lanes
    row = lax.broadcasted_iota(jnp.int32, (lanes, index_ref.shape[1]), 0)
    one_hot_ref[...] = (row == within).astype(F32).astype(BF16)


def prepare(index, centers, lanes):
    features, count = centers.shape
    examples = index.shape[1]
    return call(
        prepare_kernel,
        "prepare",
        [shape((count, DEPTH), BF16), shape((lanes, examples), BF16)],
        1 << 20,
        arrays=2,
    )(index, centers)


def tile_kernel(
    index_ref, pool_ref, one_hot_ref, sides_ref, alpha_ref, tile_ref, turned_ref, rows_ref, side_ref
):
    chunks, features, lanes = pool_ref.shape
    count, examples = tile_ref.shape
    share = rows_ref.shape[2]
    scale = 4.0 / features * math.log2(math.e)
    pool = pool_ref[...].reshape(chunks * features, lanes)
    for b in range(examples // BAND):
        here = slice(b * BAND, (b + 1) * BAND)
        chunk = index_ref[:, here] // lanes
        picked = jnp.dot(pool, one_hot_ref[:, here], preferred_element_type=F32)
        points = jnp.where(chunk == 0, picked[:features], 0.0)
        for k in range(1, chunks):
            points = jnp.where(chunk == k, picked[k * features : (k + 1) * features], points)
        point_sq = jnp.sum(points * points, axis=0, keepdims=True)
        side = jnp.concatenate([points, tail(point_sq, 0, DEPTH - features)], axis=0)
        side_ref[:, here] = side.astype(BF16)
    for b in range(count // BAND):
        here = slice(b * BAND, (b + 1) * BAND)
        near = jnp.dot(sides_ref[here, :], side_ref[...], preferred_element_type=F32)
        values = jnp.exp2(near * scale).astype(BF16)
        tile_ref[here, :] = values
        turned_ref[:, here] = values.T
    for b in range(examples // BAND):
        here = slice(b * BAND, (b + 1) * BAND)
        rows = jnp.dot(alpha_ref[...], tile_ref[:, here], preferred_element_type=F32)
        for k in range(BAND // share):
            rows_ref[b * (BAND // share) + k] = rows[:, k * share : (k + 1) * share]


def make_tile(index, row_pool, one_hot, sides, alpha, share):
    examples, count = index.shape[1], sides.shape[0]
    classes = alpha.shape[0]
    return call(
        tile_kernel,
        "tile",
        [
            shape((count, examples), BF16),
            shape((examples, count), BF16),
            shape((examples // share, classes, share), F32),
        ],
        4 << 30,
        [pltpu.VMEM((DEPTH, examples), BF16)],
        arrays=5,
    )(index, row_pool, one_hot, sides, alpha)


def factors_kernel(core_ref, precond_ref, high_ref, low_ref, high_turned_ref, low_turned_ref):
    order = precond_ref.shape[1]
    half = high_ref.shape[0]
    first = core_ref[0] * half
    for k in range(half // order):
        here = slice(k * order, (k + 1) * order)
        block = precond_ref[pl.ds(pl.multiple_of(first + k * order, order), order), :]
        high = block.astype(BF16)
        high_ref[here] = high
        low_ref[here] = (block - high.astype(F32)).astype(BF16)
        turned = block.T
        high = turned.astype(BF16)
        high_turned_ref[here] = high
        low_turned_ref[here] = (turned - high.astype(F32)).astype(BF16)


def factors(core, precond):
    out = shape((precond.shape[0] // 2, precond.shape[1]), BF16)
    return call(factors_kernel, "factors", [out] * 4, 1 << 20, scalars=1, arrays=1)(core, precond)


def block_products(values, high_ref, low_ref):
    order = high_ref.shape[1]
    out = []
    for k in range(high_ref.shape[0] // order):
        here = slice(k * order, (k + 1) * order)
        block = values[:, here]
        high = block.astype(BF16)
        low = (block - high.astype(F32)).astype(BF16)
        product = jnp.dot(high, high_ref[here], preferred_element_type=F32)
        product += jnp.dot(high, low_ref[here], preferred_element_type=F32)
        product += jnp.dot(low, high_ref[here], preferred_element_type=F32)
        out.append(product)
    return jnp.concatenate(out, axis=1)


def forward_kernel(
    core_ref, own_ref, other_ref, own_part_ref, other_part_ref, tile_ref, rows_ref
):
    classes, half = own_ref.shape
    share = rows_ref.shape[2]
    examples = tile_ref.shape[1]
    mine = pl.ds(pl.multiple_of(core_ref[0] * half, half), half)
    theirs = pl.ds(pl.multiple_of((1 - core_ref[0]) * half, half), half)
    part = own_part_ref[...] + other_part_ref[...]
    powers = exponents(part[2:3]) - 14.0
    extra = half_rows(powers, [part[:1], part[1:2]])
    scales = column(jnp.exp2(-powers), classes)
    for b in range(examples // BAND):
        here = slice(b * BAND, (b + 1) * BAND)
        rows = jnp.dot(own_ref[...], tile_ref[mine, here], preferred_element_type=F32)
        rows += jnp.dot(other_ref[...], tile_ref[theirs, here], preferred_element_type=F32)
        rows *= scales
        for k in range(BAND // share):
            at = b * (BAND // share) + k
            rows_ref[at, :classes] = rows[:, k * share : (k + 1) * share]
            rows_ref[at, classes:] = extra


def forward(core, own, other, own_part, other_part, tile, share):
    classes = own.shape[0]
    shares = tile.shape[1] // share
    return call(
        forward_kernel,
        "forward",
        shape((shares, classes + EXTRA, share), F32),
        1208 << 20,
        scalars=1,
        arrays=5,
    )(core, own, other, own_part, other_part, tile)


def backward_kernel(core_ref, values_ref, turned_ref, other_ref, one_ref, two_ref, flat_ref):
    shares, height, share = values_ref.shape
    classes, examples = flat_ref.shape
    half = other_ref.shape[1]
    wide = half // 2
    for k in range(shares):
        flat_ref[:, k * share : (k + 1) * share] = values_ref[k, :classes]
    if height > classes:
        total = values_ref[0, classes:].astype(F32)
        for k in range(1, shares):
            total = total + values_ref[k, classes:].astype(F32)
        row = read_rows(total, 0)
        other_ref[classes:, : 2 * LANES] = jnp.broadcast_to(row, (8, 2 * LANES))
        other_ref[classes:, 2 * LANES :] = jnp.zeros((8, half - 2 * LANES), F32)
        one_ref[classes:, : 2 * LANES] = jnp.broadcast_to(row, (8, 2 * LANES))
        one_ref[classes:, 2 * LANES :] = jnp.zeros((8, wide - 2 * LANES), F32)
    for h, first in enumerate(((1 - core_ref[0]) * half, core_ref[0] * half)):
        for b in range(half // BAND):
            there = pl.ds(pl.multiple_of(first + b * BAND, BAND), BAND)
            sums = jnp.dot(flat_ref[...], turned_ref[:, there], preferred_element_type=F32)
            if h == 0:
                other_ref[:classes, b * BAND : (b + 1) * BAND] = sums
            elif b * BAND < wide:
                one_ref[:classes, b * BAND : (b + 1) * BAND] = sums
            else:
                two_ref[:, b * BAND - wide : (b + 1) * BAND - wide] = sums


def backward(core, values, turned, classes):
    examples, count = turned.shape
    height = classes + (8 if values.shape[1] > classes else 0)
    half = count // 2
    return call(
        backward_kernel,
        "backward",
        [shape((height, half), F32), shape((height, half // 2), F32), shape((classes, half // 2), F32)],
        1208 << 20,
        [pltpu.VMEM((classes, examples), BF16)],
        scalars=1,
        arrays=2,
    )(core, values, turned)


def gradient_kernel(base_ref, label_ref, weight_ref, hessian_ref, send_ref):
    classes, share = base_ref.shape
    base = base_ref[...]
    probability = jax.nn.sigmoid(base)
    row = lax.broadcasted_iota(jnp.int32, (classes, share), 0)
    target = jnp.where(row == label_ref[...], 1.0, 0.0)
    hessian_ref[...] = weight_ref[...] * probability * (1.0 - probability)
    gradient = (weight_ref[...] * (probability - target)).astype(BF16)
    for k in range(send_ref.shape[0]):
        send_ref[k] = gradient


def gradient(base, label, weight, shares):
    return call(
        gradient_kernel,
        "gradient",
        [shape(base.shape, F32), shape((shares,) + base.shape, BF16)],
        1 << 20,
        arrays=3,
    )(base, label, weight)


def residual_kernel(
    total, one_ref, one_in_ref, two_ref, two_in_ref, high_ref, low_ref, high_turned_ref,
    low_turned_ref, residual_ref, lifted_ref, part_ref,
):
    sums = jnp.concatenate([one_ref[...] + one_in_ref[...], two_ref[...] + two_in_ref[...]], axis=1)
    residual = block_products(sums, high_ref, low_ref) * (-1.0 / total)
    residual_ref[...] = residual
    lifted = block_products(residual, high_turned_ref, low_turned_ref).astype(BF16)
    lifted_ref[...] = lifted
    zero = jnp.zeros((1, 2 * LANES), F32)
    part_ref[...] = stack_rows(
        [lane_sums(residual * residual), zero, lane_sums(jnp.abs(lifted.astype(F32)))]
    )


def first_residual(total, sums, blocks):
    classes, wide = sums[2].shape
    return call(
        functools.partial(residual_kernel, total),
        "residual",
        [
            shape((classes, 2 * wide), F32),
            shape((classes, 2 * wide), BF16),
            shape((8, 2 * LANES), F32),
        ],
        450 << 20,
        arrays=8,
    )(*sums, *blocks)


def weigh_kernel(parts_ref, hessian_ref, image_ref, norm_ref, send_ref):
    classes = hessian_ref.shape[0]
    image = sum_scaled(parts_ref, classes)
    image_ref[...] = image
    norm_ref[...] = stack_rows([half_vector(parts_ref, classes, 0)])
    weighted = (hessian_ref[...] * image).astype(BF16)
    extra = rows_of([lane_sums(weighted.astype(F32) * image)])
    for k in range(send_ref.shape[0]):
        send_ref[k, :classes] = weighted
        send_ref[k, classes:] = extra


def weigh(parts, hessian):
    return call(
        weigh_kernel,
        "weigh",
        [shape(hessian.shape, F32), shape((8, 2 * LANES), F32), shape(parts.shape, BF16)],
        1 << 20,
        arrays=2,
    )(parts, hessian)


def step_kernel(
    total, one_ref, one_in_ref, two_ref, two_in_ref, high_ref, low_ref, high_turned_ref,
    low_turned_ref, residual_ref, norm_ref, lifted_ref, part_ref, rough_ref,
):
    classes = residual_ref.shape[0]
    one = one_ref[...] + one_in_ref[...]
    curve = one[classes : classes + 1, : 2 * LANES] / total
    norm = norm_ref[:1]
    lane = lax.broadcasted_iota(jnp.int32, (1, 2 * LANES), 1)
    rough = jnp.where(lane < classes, norm / (curve + RIDGE * norm), 0.0)
    rough_ref[...] = stack_rows([rough])
    sums = jnp.concatenate([one[:classes], two_ref[...] + two_in_ref[...]], axis=1)
    old = residual_ref[...]
    image = block_products(sums, high_ref, low_ref) / total + RIDGE * old
    new = old - column(rough, classes) * image
    lifted = block_products(new, high_turned_ref, low_turned_ref).astype(BF16)
    lifted_ref[...] = lifted
    part_ref[...] = stack_rows(
        [lane_sums(old * new), lane_sums(new * new), lane_sums(jnp.abs(lifted.astype(F32)))]
    )


def step(total, sums, blocks, residual, norm):
    row = shape((8, 2 * LANES), F32)
    return call(
        functools.partial(step_kernel, total),
        "step",
        [shape(residual.shape, BF16), row, row],
        450 << 20,
        arrays=10,
    )(*sums, *blocks, residual, norm)


def curve_kernel(
    parts_ref, hessian_ref, image_ref, norm_ref, rough_ref, last_ref, scales_ref, curve_ref
):
    classes = hessian_ref.shape[0]
    last = sum_scaled(parts_ref, classes)
    last_ref[...] = last
    cross = half_vector(parts_ref, classes, 0)
    norm_rough = half_vector(parts_ref, classes, 1)
    norm = norm_ref[:1]
    lane = lax.broadcasted_iota(jnp.int32, (1, 2 * LANES), 1)
    excess = jnp.where(lane < classes, cross / (norm - cross), 0.0)
    grown = 1.0 + excess
    norm_next = grown * (grown * norm_rough - 2.0 * excess * cross) + excess * excess * norm
    ratio = jnp.where(lane < classes, norm_next / norm, 0.0)
    ridge = RIDGE * (norm_next + ratio * ratio * norm)
    scales_ref[...] = stack_rows(
        [rough_ref[:1] * grown, grown, ratio - excess, norm_next, ridge]
    )
    rows = column(grown, classes) * last + column(ratio - excess, classes) * image_ref[...]
    weighted = (hessian_ref[...] * rows).astype(BF16).astype(F32)
    curve_ref[...] = stack_rows([lane_sums(weighted * rows)])


def last_curve(parts, hessian, image, norm, rough):
    row = shape((8, 2 * LANES), F32)
    return call(
        curve_kernel,
        "curve",
        [shape(hessian.shape, F32), row, row],
        1 << 20,
        arrays=5,
    )(parts, hessian, image, norm, rough)


def margins_kernel(total, curve_ref, scales_ref, base_ref, image_ref, last_ref, margins_ref):
    classes = base_ref.shape[0]
    curve = jnp.sum(curve_ref[:, 0], axis=0, keepdims=True)
    first, grown, other = scales_ref[0:1], scales_ref[1:2], scales_ref[2:3]
    lane = lax.broadcasted_iota(jnp.int32, (1, 2 * LANES), 1)
    second = jnp.where(
        lane < classes, scales_ref[3:4] / (curve / total + scales_ref[4:5]), 0.0
    )
    margins_ref[...] = (
        base_ref[...]
        + column(first + second * other, classes) * image_ref[...]
        + column(second * grown, classes) * last_ref[...]
    )


def margins(total, curve, scales, base, image, last):
    return call(
        functools.partial(margins_kernel, total), "margins", shape(base.shape, F32), 1 << 20, arrays=5
    )(curve, scales, base, image, last)


def shards(pool, indices, labels, example_weight, centers, alpha, precond):
    n_ex, n_ctr = lax.axis_size("ex"), lax.axis_size("ctr")
    classes, count = alpha.shape
    examples = indices.shape[0]
    share = examples // n_ctr
    total = float(examples * n_ex)
    core = (lax.axis_index("ex") % 2).reshape(1)
    core_pairs = [(i, i ^ 1) for i in range(n_ex)]

    def over_y(array, flip):
        pairs = [(2 * y + c, 2 * (y ^ flip) + c) for y in range(n_ex // 2) for c in range(2)]
        return lax.ppermute(array, "ex", pairs)

    def over_cores(array):
        return lax.ppermute(array, "ex", core_pairs)

    def trade(parts):
        return lax.all_to_all(parts, "ctr", 0, 0)

    def trade_halves(parts):
        return trade(parts.astype(F16)).astype(F32)

    def sum_examples(products):
        other, one, two = products
        got = over_cores(other)
        wide = one.shape[1]
        one = one + got[:, :wide]
        two = two + got[:classes, wide:]
        one = one + over_y(one, 1)
        two = two + over_y(two, 3)
        return one, over_y(one, 3), two, over_y(two, 1)

    offset = lax.axis_index("ctr") * share
    label = lax.dynamic_slice_in_dim(labels, offset, share, 0).reshape(1, share)
    weight = lax.dynamic_slice_in_dim(example_weight, offset, share, 0).reshape(1, share)
    index = indices.reshape(1, examples)
    sides, one_hot = prepare(index, centers, pool.shape[1])
    blocks = factors(core, precond)
    row_pool = trade(jnp.broadcast_to(pool, (n_ctr,) + pool.shape))
    row_pool, sides, one_hot, index, label, weight, core, *blocks = lax.optimization_barrier(
        (row_pool, sides, one_hot, index, label, weight, core, *blocks)
    )
    tile, turned, rows = make_tile(index, row_pool, one_hot, sides, alpha, share)
    base = jnp.sum(trade_halves(rows), axis=0)
    hessian, send = gradient(base, label, weight, n_ctr)

    sums = sum_examples(backward(core, trade(send), turned, classes))
    residual, lifted, part = first_residual(total, sums, blocks)
    rows = forward(core, lifted, over_cores(lifted), part, over_cores(part), tile, share)
    image, norm, send = weigh(trade_halves(rows), hessian)

    sums = sum_examples(backward(core, trade(send), turned, classes))
    lifted, part, rough = step(total, sums, blocks, residual, norm)
    rows = forward(core, lifted, over_cores(lifted), part, over_cores(part), tile, share)
    last, scales, curve = last_curve(trade_halves(rows), hessian, image, norm, rough)

    curve = curve + over_cores(curve)
    curve = curve + over_y(curve, 1)
    curve = curve + over_y(curve, 3)
    curve = trade(jnp.broadcast_to(curve, (n_ctr,) + curve.shape))
    return margins(total, curve, scales, base, image, last)


def solution(mesh):
    return jax.shard_map(
        shards,
        mesh=mesh,
        in_specs=(
            P(None, ("ex", "ctr")),
            P("ex"),
            P("ex"),
            P("ex"),
            P(None, "ctr"),
            P(None, "ctr"),
            P("ctr", None),
        ),
        out_specs=P(None, ("ex", "ctr")),
        check_vma=False,
    )
```

```python
import functools
import math

import jax
import jax.numpy as jnp
from jax import lax
from jax.experimental import pallas as pl
from jax.experimental.pallas import tpu as pltpu
from jax.sharding import PartitionSpec as P

RIDGE = 0.0001
F32 = jnp.float32
F16 = jnp.float16
BF16 = jnp.bfloat16
VMEM_BYTES = 24 * 1024 * 1024
DEPTH = 128
BAND = 256
EXTRA = 16
LANES = 128
NT = (((1,), (1,)), ((), ()))
TN = (((0,), (0,)), ((), ()))


def split3(values):
    high = values.astype(BF16)
    rest = values - high.astype(F32)
    middle = rest.astype(BF16)
    low = (rest - middle.astype(F32)).astype(BF16)
    return high, middle, low


SCALAR = pl.BlockSpec(memory_space=pltpu.SMEM)
WHOLE = pl.BlockSpec(memory_space=pltpu.VMEM)
ANYWHERE = pl.BlockSpec(memory_space=pl.ANY)


def call(kernel, name, out_shape, flops, scratch=(), scalars=0, anywhere=0, arrays=0):
    shapes = out_shape if isinstance(out_shape, list) else [out_shape]
    size = sum(math.prod(s.shape) * s.dtype.itemsize for s in shapes)
    return pl.pallas_call(
        kernel,
        out_shape=out_shape,
        scratch_shapes=list(scratch),
        in_specs=[SCALAR] * scalars + [ANYWHERE] * anywhere + [WHOLE] * arrays,
        compiler_params=pltpu.CompilerParams(vmem_limit_bytes=VMEM_BYTES),
        cost_estimate=pl.CostEstimate(flops=flops, bytes_accessed=size, transcendentals=0),
        name=name,
    )


def rows_of(vectors):
    row = lax.broadcasted_iota(jnp.int32, (EXTRA, LANES), 0)
    out = jnp.zeros((EXTRA, LANES), F32)
    for k, vector in enumerate(vectors):
        for p, piece in enumerate(split3(vector)):
            for q in range(2):
                value = piece.astype(F32)[:, q * LANES : (q + 1) * LANES]
                out = jnp.where(row == 6 * k + 2 * p + q, value, out)
    return out.astype(BF16)


def read_rows(summed, k):
    halves = [
        sum(summed[6 * k + 2 * p + q : 6 * k + 2 * p + q + 1] for p in range(3)) for q in range(2)
    ]
    return jnp.concatenate(halves, axis=1)


def exponents(bounds):
    return jnp.ceil(jnp.log2(jnp.maximum(bounds, 1e-30)))


def half_pieces(powers, vectors):
    pieces = [powers]
    for vector in vectors:
        power = exponents(jnp.abs(vector)) + 1.0
        scaled = vector * jnp.exp2(-power) * 2048.0
        high = jnp.floor(scaled + 0.5)
        pieces += [power, high / 2048.0, jnp.floor((scaled - high) * 2048.0 + 0.5) / 2048.0]
    return pieces


def half_rows(powers, vectors):
    row = lax.broadcasted_iota(jnp.int32, (EXTRA, LANES), 0)
    out = jnp.zeros((EXTRA, LANES), F32)
    for p, piece in enumerate(half_pieces(powers, vectors)):
        for q in range(2):
            out = jnp.where(row == 2 * p + q, piece[:, q * LANES : (q + 1) * LANES], out)
    return out


def half_row(parts_ref, first, p):
    rows = [parts_ref[:, first + 2 * p + q, :] for q in range(2)]
    return jnp.concatenate(rows, axis=1)


def half_vector(parts_ref, first, k):
    power, high, low = (half_row(parts_ref, first, 1 + 3 * k + p) for p in range(3))
    return jnp.sum(jnp.exp2(power) * (high + low / 2048.0), axis=0, keepdims=True)


def sum_scaled(parts_ref, classes):
    scales = jnp.exp2(half_row(parts_ref, classes, 0)).T
    total = parts_ref[0, :classes] * scales[:classes, :1]
    for k in range(1, parts_ref.shape[0]):
        total = total + parts_ref[k, :classes] * scales[:classes, k : k + 1]
    return total


def column(vector, classes):
    return jnp.broadcast_to(vector, (8, vector.shape[1])).T[:classes, :1]


def lane_sums(values):
    folded = sum(values[:, k : k + LANES] for k in range(0, values.shape[1], LANES))
    empty = jnp.zeros((2 * LANES - values.shape[0], LANES), F32)
    return jnp.sum(jnp.concatenate([folded, empty], axis=0).T, axis=0, keepdims=True)


def stack_rows(vectors):
    row = lax.broadcasted_iota(jnp.int32, (8, 2 * LANES), 0)
    out = jnp.zeros((8, 2 * LANES), F32)
    for k, vector in enumerate(vectors):
        out = jnp.where(row == k, vector, out)
    return out


def sum_parts(ref):
    total = ref[0].astype(F32)
    for k in range(1, ref.shape[0]):
        total = total + ref[k].astype(F32)
    return total


def shape(dims, dtype):
    return jax.ShapeDtypeStruct(dims, dtype)


def tail(squares, first, pad):
    pieces = [p.astype(F32) for p in split3(-0.5 * squares)]
    row = lax.broadcasted_iota(jnp.int32, (pad, squares.shape[1]), 0)
    out = jnp.where((row >= 3 - first) & (row < 6 - first), 1.0, 0.0)
    for k in range(3):
        out = jnp.where(row == k + first, pieces[k], out)
    return out


def copies_kernel(block_ref, copies_ref):
    for k in range(copies_ref.shape[0]):
        copies_ref[k] = block_ref[...]


def copies(block, number):
    return call(copies_kernel, "copies", shape((number,) + block.shape, block.dtype), 1 << 20, arrays=1)(
        block
    )


def prepare_kernel(index_ref, centers_ref, sides_ref, one_hot_ref, chunk_ref):
    features, count = centers_ref.shape
    lanes = one_hot_ref.shape[0]
    center_float = centers_ref[...].astype(F32)
    center_sq = jnp.sum(center_float * center_float, axis=0, keepdims=True)
    side = jnp.concatenate([center_float, tail(center_sq, 3, DEPTH - features)], axis=0)
    sides_ref[...] = side.T.astype(BF16)
    chunk_ref[...] = index_ref[...] // lanes
    within = index_ref[...] % lanes
    row = lax.broadcasted_iota(jnp.int32, (lanes, index_ref.shape[1]), 0)
    one_hot_ref[...] = (row == within).astype(F32).astype(BF16)


def prepare(index, centers, lanes):
    features, count = centers.shape
    examples = index.shape[1]
    return call(
        prepare_kernel,
        "prepare",
        [shape((count, DEPTH), BF16), shape((lanes, examples), BF16), shape(index.shape, jnp.int32)],
        1 << 20,
        arrays=2,
    )(index, centers)


def tile_kernel(
    alpha_hbm, chunk_ref, pool_ref, one_hot_ref, sides_ref, tile_ref, turned_ref, rows_ref,
    side_ref, alpha_ref, alpha_sem,
):
    fetch = pltpu.make_async_copy(alpha_hbm, alpha_ref, alpha_sem)
    fetch.start()
    chunks, features, lanes = pool_ref.shape
    count, examples = tile_ref.shape
    share = rows_ref.shape[2]
    scale = 4.0 / features * math.log2(math.e)
    pool = pool_ref[...].reshape(chunks * features, lanes)
    for b in range(examples // BAND):
        here = slice(b * BAND, (b + 1) * BAND)
        chunk = chunk_ref[:, here]
        picked = jnp.dot(pool, one_hot_ref[:, here], preferred_element_type=F32)
        points = jnp.where(chunk == 0, picked[:features], 0.0)
        for k in range(1, chunks):
            points = jnp.where(chunk == k, picked[k * features : (k + 1) * features], points)
        point_sq = jnp.sum(points * points, axis=0, keepdims=True)
        side = jnp.concatenate([points, tail(point_sq, 0, DEPTH - features)], axis=0)
        side_ref[:, here] = side.astype(BF16)
    for b in range(count // BAND):
        here = slice(b * BAND, (b + 1) * BAND)
        near = jnp.dot(sides_ref[here, :], side_ref[...], preferred_element_type=F32)
        values = jnp.exp2(near * scale).astype(BF16)
        tile_ref[here, :] = values
        turned_ref[:, here] = values.T
    fetch.wait()
    for b in range(examples // BAND):
        here = slice(b * BAND, (b + 1) * BAND)
        rows = jnp.dot(alpha_ref[...], tile_ref[:, here], preferred_element_type=F32)
        for k in range(BAND // share):
            rows_ref[b * (BAND // share) + k] = rows[:, k * share : (k + 1) * share]


def make_tile(chunk, row_pool, one_hot, sides, alpha, share):
    examples, count = chunk.shape[1], sides.shape[0]
    classes = alpha.shape[0]
    return call(
        tile_kernel,
        "tile",
        [
            shape((count, examples), BF16),
            shape((examples, count), BF16),
            shape((examples // share, classes, share), F32),
        ],
        4 << 30,
        [
            pltpu.VMEM((DEPTH, examples), BF16),
            pltpu.VMEM(alpha.shape, BF16),
            pltpu.SemaphoreType.DMA,
        ],
        anywhere=1,
        arrays=4,
    )(alpha, chunk, row_pool, one_hot, sides)


def factors_kernel(core_ref, precond_ref, high_ref, low_ref, high_turned_ref, low_turned_ref):
    order = precond_ref.shape[1]
    half = high_ref.shape[0]
    first = core_ref[0] * half
    for k in range(half // order):
        here = slice(k * order, (k + 1) * order)
        block = precond_ref[pl.ds(pl.multiple_of(first + k * order, order), order), :]
        high = block.astype(BF16)
        high_ref[here] = high
        low_ref[here] = (block - high.astype(F32)).astype(BF16)
        turned = block.T
        high = turned.astype(BF16)
        high_turned_ref[here] = high
        low_turned_ref[here] = (turned - high.astype(F32)).astype(BF16)


def factors(core, precond):
    out = shape((precond.shape[0] // 2, precond.shape[1]), BF16)
    return call(factors_kernel, "factors", [out] * 4, 1 << 20, scalars=1, arrays=1)(core, precond)


def block_products(values, high_ref, low_ref):
    order = high_ref.shape[1]
    out = []
    for k in range(high_ref.shape[0] // order):
        here = slice(k * order, (k + 1) * order)
        block = values[:, here]
        high = block.astype(BF16)
        low = (block - high.astype(F32)).astype(BF16)
        product = jnp.dot(high, high_ref[here], preferred_element_type=F32)
        product += jnp.dot(high, low_ref[here], preferred_element_type=F32)
        product += jnp.dot(low, high_ref[here], preferred_element_type=F32)
        out.append(product)
    return jnp.concatenate(out, axis=1)


def forward_kernel(
    core_ref, own_ref, other_ref, own_part_ref, other_part_ref, tile_ref, rows_ref
):
    classes, half = own_ref.shape
    share = rows_ref.shape[2]
    examples = tile_ref.shape[1]
    mine = pl.ds(pl.multiple_of(core_ref[0] * half, half), half)
    theirs = pl.ds(pl.multiple_of((1 - core_ref[0]) * half, half), half)
    part = own_part_ref[...] + other_part_ref[...]
    powers = exponents(part[2:3]) - 14.0
    extra = half_rows(powers, [part[:1], part[1:2]])
    scales = column(jnp.exp2(-powers), classes)
    for b in range(examples // BAND):
        here = slice(b * BAND, (b + 1) * BAND)
        rows = jnp.dot(own_ref[...], tile_ref[mine, here], preferred_element_type=F32)
        rows += jnp.dot(other_ref[...], tile_ref[theirs, here], preferred_element_type=F32)
        rows *= scales
        for k in range(BAND // share):
            at = b * (BAND // share) + k
            rows_ref[at, :classes] = rows[:, k * share : (k + 1) * share]
            rows_ref[at, classes:] = extra


def forward(core, own, other, own_part, other_part, tile, share):
    classes = own.shape[0]
    shares = tile.shape[1] // share
    return call(
        forward_kernel,
        "forward",
        shape((shares, classes + EXTRA, share), F32),
        1208 << 20,
        scalars=1,
        arrays=5,
    )(core, own, other, own_part, other_part, tile)


def backward_kernel(core_ref, values_ref, turned_ref, other_ref, own_ref, flat_ref):
    shares, height, share = values_ref.shape
    classes, examples = flat_ref.shape
    half = other_ref.shape[1]
    for k in range(shares):
        flat_ref[:, k * share : (k + 1) * share] = values_ref[k, :classes]
    if height > classes:
        total = values_ref[0, classes:].astype(F32)
        for k in range(1, shares):
            total = total + values_ref[k, classes:].astype(F32)
        row = jnp.broadcast_to(read_rows(total, 0), (8, 2 * LANES))
        for ref in (other_ref, own_ref):
            ref[classes:, : 2 * LANES] = row
            ref[classes:, 2 * LANES :] = jnp.zeros((8, half - 2 * LANES), F32)
    for first, ref in (((1 - core_ref[0]) * half, other_ref), (core_ref[0] * half, own_ref)):
        for b in range(half // BAND):
            there = pl.ds(pl.multiple_of(first + b * BAND, BAND), BAND)
            ref[:classes, b * BAND : (b + 1) * BAND] = jnp.dot(
                flat_ref[...], turned_ref[:, there], preferred_element_type=F32
            )


def backward(core, values, turned, classes):
    examples, count = turned.shape
    height = classes + (8 if values.shape[1] > classes else 0)
    half = shape((height, count // 2), F32)
    return call(
        backward_kernel,
        "backward",
        [half, half],
        1208 << 20,
        [pltpu.VMEM((classes, examples), BF16)],
        scalars=1,
        arrays=2,
    )(core, values, turned)


def pack_halves(ref, values, vectors):
    classes, wide = values.shape
    size = jnp.max(jnp.abs(values), axis=1, keepdims=True)
    powers = exponents(size) - 14.0
    ref[:classes] = values * jnp.exp2(-powers)
    empty = jnp.zeros((2 * LANES - classes, LANES), F32)
    powers = jnp.concatenate([jnp.broadcast_to(powers, (classes, LANES)), empty], axis=0).T[:1]
    row = lax.broadcasted_iota(jnp.int32, (EXTRA, 2 * LANES), 0)
    out = jnp.zeros((EXTRA, 2 * LANES), F32)
    for p, piece in enumerate(half_pieces(powers, vectors)):
        out = jnp.where(row == p, piece, out)
    ref[classes:, : 2 * LANES] = out
    ref[classes:, 2 * LANES :] = jnp.zeros((EXTRA, wide - 2 * LANES), F32)


def unpack_halves(ref):
    classes = ref.shape[0] - EXTRA
    return ref[:classes] * column(jnp.exp2(ref[classes : classes + 1, : 2 * LANES]), classes)


def unpack_vector(ref):
    classes = ref.shape[0] - EXTRA
    power, high, low = (ref[classes + p : classes + p + 1, : 2 * LANES] for p in range(1, 4))
    return jnp.exp2(power) * (high + low / 2048.0)


def join_kernel(own_ref, got_ref, one_ref, two_ref):
    classes, wide = one_ref.shape[0] - EXTRA, one_ref.shape[1]
    for k, ref in enumerate((one_ref, two_ref)):
        here = slice(k * wide, (k + 1) * wide)
        vectors = []
        if k == 0 and own_ref.shape[0] > classes:
            row = slice(classes, classes + 1)
            vectors = [own_ref[row, : 2 * LANES] + got_ref[row, : 2 * LANES]]
        pack_halves(ref, own_ref[:classes, here] + got_ref[:classes, here], vectors)


def join(own, got, classes):
    half = shape((classes + EXTRA, own.shape[1] // 2), F32)
    return call(join_kernel, "join", [half, half], 1 << 20, arrays=2)(own, got)


def add_kernel(own_ref, got_ref, sum_ref):
    vector = unpack_vector(own_ref) + unpack_vector(got_ref)
    pack_halves(sum_ref, unpack_halves(own_ref) + unpack_halves(got_ref), [vector])


def add_halves(own, got):
    return call(add_kernel, "add", shape(own.shape, F32), 1 << 20, arrays=2)(own, got)


def gradient_kernel(base_ref, label_ref, weight_ref, hessian_ref, send_ref):
    classes, share = base_ref.shape
    base = base_ref[...]
    probability = jax.nn.sigmoid(base)
    row = lax.broadcasted_iota(jnp.int32, (classes, share), 0)
    target = jnp.where(row == label_ref[...], 1.0, 0.0)
    hessian_ref[...] = weight_ref[...] * probability * (1.0 - probability)
    gradient = (weight_ref[...] * (probability - target)).astype(BF16)
    for k in range(send_ref.shape[0]):
        send_ref[k] = gradient


def gradient(base, label, weight, shares):
    return call(
        gradient_kernel,
        "gradient",
        [shape(base.shape, F32), shape((shares,) + base.shape, BF16)],
        1 << 20,
        arrays=3,
    )(base, label, weight)


def residual_kernel(
    total, one_ref, one_in_ref, two_ref, two_in_ref, high_ref, low_ref, high_turned_ref,
    low_turned_ref, residual_ref, lifted_ref, part_ref,
):
    one = unpack_halves(one_ref) + unpack_halves(one_in_ref)
    two = unpack_halves(two_ref) + unpack_halves(two_in_ref)
    sums = jnp.concatenate([one, two], axis=1)
    residual = block_products(sums, high_ref, low_ref) * (-1.0 / total)
    residual_ref[...] = residual
    lifted = block_products(residual, high_turned_ref, low_turned_ref).astype(BF16)
    lifted_ref[...] = lifted
    zero = jnp.zeros((1, 2 * LANES), F32)
    part_ref[...] = stack_rows(
        [lane_sums(residual * residual), zero, lane_sums(jnp.abs(lifted.astype(F32)))]
    )


def first_residual(total, sums, blocks):
    classes, wide = sums[2].shape[0] - EXTRA, sums[2].shape[1]
    return call(
        functools.partial(residual_kernel, total),
        "residual",
        [
            shape((classes, 2 * wide), F32),
            shape((classes, 2 * wide), BF16),
            shape((8, 2 * LANES), F32),
        ],
        450 << 20,
        arrays=8,
    )(*sums, *blocks)


def weigh_kernel(parts_ref, hessian_ref, image_ref, norm_ref, send_ref):
    classes = hessian_ref.shape[0]
    image = sum_scaled(parts_ref, classes)
    image_ref[...] = image
    norm_ref[...] = stack_rows([half_vector(parts_ref, classes, 0)])
    weighted = (hessian_ref[...] * image).astype(BF16)
    extra = rows_of([lane_sums(weighted.astype(F32) * image)])
    for k in range(send_ref.shape[0]):
        send_ref[k, :classes] = weighted
        send_ref[k, classes:] = extra


def weigh(parts, hessian):
    return call(
        weigh_kernel,
        "weigh",
        [shape(hessian.shape, F32), shape((8, 2 * LANES), F32), shape(parts.shape, BF16)],
        1 << 20,
        arrays=2,
    )(parts, hessian)


def step_kernel(
    total, one_ref, one_in_ref, two_ref, two_in_ref, high_ref, low_ref, high_turned_ref,
    low_turned_ref, residual_ref, norm_ref, lifted_ref, part_ref, rough_ref,
):
    classes = residual_ref.shape[0]
    one = unpack_halves(one_ref) + unpack_halves(one_in_ref)
    two = unpack_halves(two_ref) + unpack_halves(two_in_ref)
    curve = (unpack_vector(one_ref) + unpack_vector(one_in_ref)) / total
    norm = norm_ref[:1]
    lane = lax.broadcasted_iota(jnp.int32, (1, 2 * LANES), 1)
    rough = jnp.where(lane < classes, norm / (curve + RIDGE * norm), 0.0)
    rough_ref[...] = stack_rows([rough])
    sums = jnp.concatenate([one, two], axis=1)
    old = residual_ref[...]
    image = block_products(sums, high_ref, low_ref) / total + RIDGE * old
    new = old - column(rough, classes) * image
    lifted = block_products(new, high_turned_ref, low_turned_ref).astype(BF16)
    lifted_ref[...] = lifted
    part_ref[...] = stack_rows(
        [lane_sums(old * new), lane_sums(new * new), lane_sums(jnp.abs(lifted.astype(F32)))]
    )


def step(total, sums, blocks, residual, norm):
    row = shape((8, 2 * LANES), F32)
    return call(
        functools.partial(step_kernel, total),
        "step",
        [shape(residual.shape, BF16), row, row],
        450 << 20,
        arrays=10,
    )(*sums, *blocks, residual, norm)


def curve_kernel(
    parts_ref, hessian_ref, image_ref, norm_ref, rough_ref, last_ref, scales_ref, curve_ref
):
    classes = hessian_ref.shape[0]
    last = sum_scaled(parts_ref, classes)
    last_ref[...] = last
    cross = half_vector(parts_ref, classes, 0)
    norm_rough = half_vector(parts_ref, classes, 1)
    norm = norm_ref[:1]
    lane = lax.broadcasted_iota(jnp.int32, (1, 2 * LANES), 1)
    excess = jnp.where(lane < classes, cross / (norm - cross), 0.0)
    grown = 1.0 + excess
    norm_next = grown * (grown * norm_rough - 2.0 * excess * cross) + excess * excess * norm
    ratio = jnp.where(lane < classes, norm_next / norm, 0.0)
    ridge = RIDGE * (norm_next + ratio * ratio * norm)
    scales_ref[...] = stack_rows(
        [rough_ref[:1] * grown, grown, ratio - excess, norm_next, ridge]
    )
    rows = column(grown, classes) * last + column(ratio - excess, classes) * image_ref[...]
    weighted = (hessian_ref[...] * rows).astype(BF16).astype(F32)
    curve_ref[...] = stack_rows([lane_sums(weighted * rows)])


def last_curve(parts, hessian, image, norm, rough):
    row = shape((8, 2 * LANES), F32)
    return call(
        curve_kernel,
        "curve",
        [shape(hessian.shape, F32), row, row],
        1 << 20,
        arrays=5,
    )(parts, hessian, image, norm, rough)


def margins_kernel(total, curve_ref, scales_ref, base_ref, image_ref, last_ref, margins_ref):
    classes = base_ref.shape[0]
    curve = jnp.sum(curve_ref[:, 0], axis=0, keepdims=True)
    first, grown, other = scales_ref[0:1], scales_ref[1:2], scales_ref[2:3]
    lane = lax.broadcasted_iota(jnp.int32, (1, 2 * LANES), 1)
    second = jnp.where(
        lane < classes, scales_ref[3:4] / (curve / total + scales_ref[4:5]), 0.0
    )
    margins_ref[...] = (
        base_ref[...]
        + column(first + second * other, classes) * image_ref[...]
        + column(second * grown, classes) * last_ref[...]
    )


def margins(total, curve, scales, base, image, last):
    return call(
        functools.partial(margins_kernel, total), "margins", shape(base.shape, F32), 1 << 20, arrays=5
    )(curve, scales, base, image, last)


def shards(pool, indices, labels, example_weight, centers, alpha, precond):
    n_ex, n_ctr = lax.axis_size("ex"), lax.axis_size("ctr")
    classes, count = alpha.shape
    examples = indices.shape[0]
    share = examples // n_ctr
    total = float(examples * n_ex)
    core = (lax.axis_index("ex") % 2).reshape(1)
    core_pairs = [(i, i ^ 1) for i in range(n_ex)]

    def over_y(array, flip):
        pairs = [(2 * y + c, 2 * (y ^ flip) + c) for y in range(n_ex // 2) for c in range(2)]
        return lax.ppermute(array, "ex", pairs)

    def over_cores(array):
        return lax.ppermute(array, "ex", core_pairs)

    def trade(parts):
        return lax.all_to_all(parts, "ctr", 0, 0)

    def trade_halves(parts):
        return trade(parts.astype(F16)).astype(F32)

    def swap(array, flip):
        array = lax.reduce_precision(array, 5, 10)
        return array, over_y(array.astype(F16), flip).astype(F32)

    def sum_examples(own, got):
        one, two = join(own, got, classes)
        one, two = swap(one, 1), swap(two, 3)
        one, two = add_halves(*one), add_halves(*two)
        return *swap(one, 3), *swap(two, 1)

    offset = lax.axis_index("ctr") * share
    label = lax.dynamic_slice_in_dim(labels, offset, share, 0).reshape(1, share)
    weight = lax.dynamic_slice_in_dim(example_weight, offset, share, 0).reshape(1, share)
    index = indices.reshape(1, examples)
    sides, one_hot, chunk = prepare(index, centers, pool.shape[1])
    row_pool = trade(copies(pool, n_ctr))
    row_pool, sides, one_hot, chunk, label, weight, core = lax.optimization_barrier(
        (row_pool, sides, one_hot, chunk, label, weight, core)
    )
    tile, turned, rows = make_tile(chunk, row_pool, one_hot, sides, alpha, share)
    base = jnp.sum(trade_halves(rows), axis=0)
    hessian, send = gradient(base, label, weight, n_ctr)

    other, own = backward(core, trade(send), turned, classes)
    got = over_cores(other)
    got, late_core = lax.optimization_barrier((got, core))
    blocks = factors(late_core, precond)
    sums = sum_examples(own, got)
    residual, lifted, part = first_residual(total, sums, blocks)
    rows = forward(core, lifted, over_cores(lifted), part, over_cores(part), tile, share)
    image, norm, send = weigh(trade_halves(rows), hessian)

    other, own = backward(core, trade(send), turned, classes)
    sums = sum_examples(own, over_cores(other))
    lifted, part, rough = step(total, sums, blocks, residual, norm)
    rows = forward(core, lifted, over_cores(lifted), part, over_cores(part), tile, share)
    last, scales, curve = last_curve(trade_halves(rows), hessian, image, norm, rough)

    curve = lax.all_to_all(jnp.broadcast_to(curve, (n_ex,) + curve.shape), "ex", 0, 0)
    curve = jnp.sum(curve, axis=0)
    curve = trade(jnp.broadcast_to(curve, (n_ctr,) + curve.shape))
    return margins(total, curve, scales, base, image, last)


def solution(mesh):
    return jax.shard_map(
        shards,
        mesh=mesh,
        in_specs=(
            P(None, ("ex", "ctr")),
            P("ex"),
            P("ex"),
            P("ex"),
            P(None, "ctr"),
            P(None, "ctr"),
            P("ctr", None),
        ),
        out_specs=P(None, ("ex", "ctr")),
        check_vma=False,
    )
```

```python
import functools
import math

import jax
import jax.numpy as jnp
from jax import lax
from jax.experimental import pallas as pl
from jax.experimental.pallas import tpu as pltpu
from jax.sharding import PartitionSpec as P

RIDGE = 0.0001
F32 = jnp.float32
F16 = jnp.float16
BF16 = jnp.bfloat16
VMEM_BYTES = 24 * 1024 * 1024
DEPTH = 128
BAND = 256
EXTRA = 16
SCALARS = 8
LANES = 128
NT = (((1,), (1,)), ((), ()))
TN = (((0,), (0,)), ((), ()))


def split3(values):
    high = values.astype(BF16)
    rest = values - high.astype(F32)
    middle = rest.astype(BF16)
    low = (rest - middle.astype(F32)).astype(BF16)
    return high, middle, low


SCALAR = pl.BlockSpec(memory_space=pltpu.SMEM)
WHOLE = pl.BlockSpec(memory_space=pltpu.VMEM)
ANYWHERE = pl.BlockSpec(memory_space=pl.ANY)


def call(kernel, name, out_shape, flops, scratch=(), scalars=0, anywhere=0, arrays=0):
    shapes = out_shape if isinstance(out_shape, list) else [out_shape]
    size = sum(math.prod(s.shape) * s.dtype.itemsize for s in shapes)
    return pl.pallas_call(
        kernel,
        out_shape=out_shape,
        scratch_shapes=list(scratch),
        in_specs=[SCALAR] * scalars + [ANYWHERE] * anywhere + [WHOLE] * arrays,
        compiler_params=pltpu.CompilerParams(vmem_limit_bytes=VMEM_BYTES),
        cost_estimate=pl.CostEstimate(flops=flops, bytes_accessed=size, transcendentals=0),
        name=name,
    )


def rows_of(vectors):
    row = lax.broadcasted_iota(jnp.int32, (EXTRA, LANES), 0)
    out = jnp.zeros((EXTRA, LANES), F32)
    for k, vector in enumerate(vectors):
        for p, piece in enumerate(split3(vector)):
            for q in range(2):
                value = piece.astype(F32)[:, q * LANES : (q + 1) * LANES]
                out = jnp.where(row == 6 * k + 2 * p + q, value, out)
    return out.astype(BF16)


def read_rows(summed, k):
    halves = [
        sum(summed[6 * k + 2 * p + q : 6 * k + 2 * p + q + 1] for p in range(3)) for q in range(2)
    ]
    return jnp.concatenate(halves, axis=1)


def exponents(bounds):
    return jnp.ceil(jnp.log2(jnp.maximum(bounds, 1e-30)))


def half_pieces(powers, vectors):
    pieces = [powers]
    for vector in vectors:
        power = exponents(jnp.abs(vector)) + 1.0
        scaled = vector * jnp.exp2(-power) * 2048.0
        high = jnp.floor(scaled + 0.5)
        pieces += [power, high / 2048.0, jnp.floor((scaled - high) * 2048.0 + 0.5) / 2048.0]
    return pieces


def half_rows(powers, vectors):
    row = lax.broadcasted_iota(jnp.int32, (SCALARS, LANES), 0)
    lane = lax.broadcasted_iota(jnp.int32, (SCALARS, LANES), 1)
    out = jnp.zeros((SCALARS, LANES), F32)
    for p, piece in enumerate(half_pieces(powers, vectors)):
        out = jnp.where(row == p, piece[:, :LANES], out)
        rest = piece[:, LANES : LANES + 16]
        rest = jnp.concatenate([rest] * (LANES // 16), axis=1)
        out = jnp.where((row == SCALARS - 1) & (lane // 16 == p), rest, out)
    return out


def half_row(parts_ref, first, p):
    rest = parts_ref[:, first + SCALARS - 1, :][:, 16 * p : 16 * p + 16]
    empty = jnp.zeros((parts_ref.shape[0], LANES - 16), F32)
    return jnp.concatenate([parts_ref[:, first + p, :], rest, empty], axis=1)


def half_vector(parts_ref, first, k):
    power, high, low = (half_row(parts_ref, first, 1 + 3 * k + p) for p in range(3))
    return jnp.sum(jnp.exp2(power) * (high + low / 2048.0), axis=0, keepdims=True)


def sum_scaled(parts_ref, classes):
    scales = jnp.exp2(half_row(parts_ref, classes, 0)).T
    total = parts_ref[0, :classes] * scales[:classes, :1]
    for k in range(1, parts_ref.shape[0]):
        total = total + parts_ref[k, :classes] * scales[:classes, k : k + 1]
    return total


def column(vector, classes):
    return jnp.broadcast_to(vector, (8, vector.shape[1])).T[:classes, :1]


def lane_sums(values):
    folded = sum(values[:, k : k + LANES] for k in range(0, values.shape[1], LANES))
    empty = jnp.zeros((2 * LANES - values.shape[0], LANES), F32)
    return jnp.sum(jnp.concatenate([folded, empty], axis=0).T, axis=0, keepdims=True)


def stack_rows(vectors):
    row = lax.broadcasted_iota(jnp.int32, (8, 2 * LANES), 0)
    out = jnp.zeros((8, 2 * LANES), F32)
    for k, vector in enumerate(vectors):
        out = jnp.where(row == k, vector, out)
    return out


def sum_parts(ref):
    total = ref[0].astype(F32)
    for k in range(1, ref.shape[0]):
        total = total + ref[k].astype(F32)
    return total


def shape(dims, dtype):
    return jax.ShapeDtypeStruct(dims, dtype)


def tail(squares, first, pad):
    pieces = [p.astype(F32) for p in split3(-0.5 * squares)]
    row = lax.broadcasted_iota(jnp.int32, (pad, squares.shape[1]), 0)
    out = jnp.where((row >= 3 - first) & (row < 6 - first), 1.0, 0.0)
    for k in range(3):
        out = jnp.where(row == k + first, pieces[k], out)
    return out


def copies_kernel(block_ref, copies_ref):
    features, lanes = block_ref.shape
    for k in range(copies_ref.shape[0]):
        for q in range(lanes // LANES):
            copies_ref[k, q * features : (q + 1) * features] = block_ref[
                :, q * LANES : (q + 1) * LANES
            ]


def copies(block, number):
    out = shape((number, block.size // LANES, LANES), block.dtype)
    return call(copies_kernel, "copies", out, 1 << 20, arrays=1)(block)


def prepare_kernel(index_ref, centers_ref, sides_ref, one_hot_ref, chunk_ref):
    features, count = centers_ref.shape
    lanes = one_hot_ref.shape[0]
    center_float = centers_ref[...].astype(F32)
    center_sq = jnp.sum(center_float * center_float, axis=0, keepdims=True)
    side = jnp.concatenate([center_float, tail(center_sq, 3, DEPTH - features)], axis=0)
    sides_ref[...] = side.T.astype(BF16)
    chunk_ref[...] = index_ref[...] // lanes
    within = index_ref[...] % lanes
    row = lax.broadcasted_iota(jnp.int32, (lanes, index_ref.shape[1]), 0)
    one_hot_ref[...] = (row == within).astype(F32).astype(BF16)


def prepare(index, centers, lanes):
    features, count = centers.shape
    examples = index.shape[1]
    return call(
        prepare_kernel,
        "prepare",
        [shape((count, DEPTH), BF16), shape((lanes, examples), BF16), shape(index.shape, jnp.int32)],
        1 << 20,
        arrays=2,
    )(index, centers)


def tile_kernel(
    alpha_hbm, chunk_ref, pool_ref, one_hot_ref, sides_ref, tile_ref, turned_ref, rows_ref,
    side_ref, alpha_ref, alpha_sem,
):
    fetch = pltpu.make_async_copy(alpha_hbm, alpha_ref, alpha_sem)
    fetch.start()
    chunks, height, _ = pool_ref.shape
    lanes = one_hot_ref.shape[0]
    features = height * LANES // lanes
    count, examples = tile_ref.shape
    share = rows_ref.shape[2]
    scale = 4.0 / features * math.log2(math.e)
    pool = jnp.concatenate(
        [
            pool_ref[:, q * features : (q + 1) * features, :].reshape(chunks * features, LANES)
            for q in range(lanes // LANES)
        ],
        axis=1,
    )
    for b in range(examples // BAND):
        here = slice(b * BAND, (b + 1) * BAND)
        chunk = chunk_ref[:, here]
        picked = jnp.dot(pool, one_hot_ref[:, here], preferred_element_type=F32)
        points = jnp.where(chunk == 0, picked[:features], 0.0)
        for k in range(1, chunks):
            points = jnp.where(chunk == k, picked[k * features : (k + 1) * features], points)
        point_sq = jnp.sum(points * points, axis=0, keepdims=True)
        side = jnp.concatenate([points, tail(point_sq, 0, DEPTH - features)], axis=0)
        side_ref[:, here] = side.astype(BF16)
    for b in range(count // BAND):
        here = slice(b * BAND, (b + 1) * BAND)
        near = jnp.dot(sides_ref[here, :], side_ref[...], preferred_element_type=F32)
        values = jnp.exp2(near * scale).astype(BF16)
        tile_ref[here, :] = values
        turned_ref[:, here] = values.T
    fetch.wait()
    for b in range(examples // BAND):
        here = slice(b * BAND, (b + 1) * BAND)
        rows = jnp.dot(alpha_ref[...], tile_ref[:, here], preferred_element_type=F32)
        for k in range(BAND // share):
            rows_ref[b * (BAND // share) + k] = rows[:, k * share : (k + 1) * share]


def make_tile(chunk, row_pool, one_hot, sides, alpha, share):
    examples, count = chunk.shape[1], sides.shape[0]
    classes = alpha.shape[0]
    return call(
        tile_kernel,
        "tile",
        [
            shape((count, examples), BF16),
            shape((examples, count), BF16),
            shape((examples // share, classes, share), F32),
        ],
        4 << 30,
        [
            pltpu.VMEM((DEPTH, examples), BF16),
            pltpu.VMEM(alpha.shape, BF16),
            pltpu.SemaphoreType.DMA,
        ],
        anywhere=1,
        arrays=4,
    )(alpha, chunk, row_pool, one_hot, sides)


def factors_kernel(core_ref, precond_ref, high_ref, low_ref, high_turned_ref, low_turned_ref):
    order = precond_ref.shape[1]
    half = high_ref.shape[0]
    first = core_ref[0] * half
    for k in range(half // order):
        here = slice(k * order, (k + 1) * order)
        block = precond_ref[pl.ds(pl.multiple_of(first + k * order, order), order), :]
        high = block.astype(BF16)
        high_ref[here] = high
        low_ref[here] = (block - high.astype(F32)).astype(BF16)
        turned = block.T
        high = turned.astype(BF16)
        high_turned_ref[here] = high
        low_turned_ref[here] = (turned - high.astype(F32)).astype(BF16)


def factors(core, precond):
    out = shape((precond.shape[0] // 2, precond.shape[1]), BF16)
    return call(factors_kernel, "factors", [out] * 4, 1 << 20, scalars=1, arrays=1)(core, precond)


def block_products(values, high_ref, low_ref):
    order = high_ref.shape[1]
    out = []
    for k in range(high_ref.shape[0] // order):
        here = slice(k * order, (k + 1) * order)
        block = values[:, here]
        high = block.astype(BF16)
        low = (block - high.astype(F32)).astype(BF16)
        product = jnp.dot(high, high_ref[here], preferred_element_type=F32)
        product += jnp.dot(high, low_ref[here], preferred_element_type=F32)
        product += jnp.dot(low, high_ref[here], preferred_element_type=F32)
        out.append(product)
    return jnp.concatenate(out, axis=1)


def forward_own_kernel(core_ref, own_ref, tile_ref, first_ref):
    half = own_ref.shape[1]
    mine = pl.ds(pl.multiple_of(core_ref[0] * half, half), half)
    for b in range(first_ref.shape[1] // BAND):
        here = slice(b * BAND, (b + 1) * BAND)
        first_ref[:, here] = jnp.dot(own_ref[...], tile_ref[mine, here], preferred_element_type=F32)


def forward_kernel(
    core_ref, first_ref, other_ref, own_part_ref, other_part_ref, tile_ref, rows_ref
):
    classes, half = other_ref.shape
    share = rows_ref.shape[2]
    examples = tile_ref.shape[1]
    theirs = pl.ds(pl.multiple_of((1 - core_ref[0]) * half, half), half)
    part = own_part_ref[...] + other_part_ref[...]
    powers = exponents(part[2:3]) - 14.0
    extra = half_rows(powers, [part[:1], part[1:2]])
    scales = column(jnp.exp2(-powers), classes)
    for b in range(examples // BAND):
        here = slice(b * BAND, (b + 1) * BAND)
        rows = jnp.dot(other_ref[...], tile_ref[theirs, here], preferred_element_type=F32)
        rows = (rows + first_ref[:, here]) * scales
        for k in range(BAND // share):
            at = b * (BAND // share) + k
            rows_ref[at, :classes] = rows[:, k * share : (k + 1) * share]
            rows_ref[at, classes:] = extra


def forward(core, lifted, other, own_part, other_part, tile, share):
    classes = lifted.shape[0]
    examples = tile.shape[1]
    first = call(
        forward_own_kernel,
        "forward_own",
        shape((classes, examples), F32),
        604 << 20,
        scalars=1,
        arrays=2,
    )(core, lifted, tile)
    return call(
        forward_kernel,
        "forward",
        shape((examples // share, classes + SCALARS, share), F32),
        604 << 20,
        scalars=1,
        arrays=5,
    )(core, first, other, own_part, other_part, tile)


def backward_other_kernel(core_ref, values_ref, turned_ref, other_ref, flat_ref, row_ref):
    shares, height, share = values_ref.shape
    classes, examples = flat_ref.shape
    half = other_ref.shape[1]
    for k in range(shares):
        flat_ref[:, k * share : (k + 1) * share] = values_ref[k, :classes]
    row = jnp.zeros((8, 2 * LANES), F32)
    if height > classes:
        total = values_ref[0, classes:].astype(F32)
        for k in range(1, shares):
            total = total + values_ref[k, classes:].astype(F32)
        row = jnp.broadcast_to(read_rows(total, 0), (8, 2 * LANES))
    row_ref[...] = row
    other_ref[classes:, : 2 * LANES] = row
    other_ref[classes:, 2 * LANES :] = jnp.zeros((8, half - 2 * LANES), F32)
    for b in range(half // BAND):
        there = pl.ds(pl.multiple_of((1 - core_ref[0]) * half + b * BAND, BAND), BAND)
        other_ref[:classes, b * BAND : (b + 1) * BAND] = jnp.dot(
            flat_ref[...], turned_ref[:, there], preferred_element_type=F32
        )


def backward_own_kernel(core_ref, flat_ref, turned_ref, own_ref):
    half = own_ref.shape[1]
    for b in range(half // BAND):
        there = pl.ds(pl.multiple_of(core_ref[0] * half + b * BAND, BAND), BAND)
        own_ref[:, b * BAND : (b + 1) * BAND] = jnp.dot(
            flat_ref[...], turned_ref[:, there], preferred_element_type=F32
        )


def backward_other(core, values, turned, classes):
    examples, count = turned.shape
    return call(
        backward_other_kernel,
        "backward_other",
        [
            shape((classes + 8, count // 2), F32),
            shape((classes, examples), BF16),
            shape((8, 2 * LANES), F32),
        ],
        604 << 20,
        scalars=1,
        arrays=2,
    )(core, values, turned)


def backward_own(core, flat, turned):
    return call(
        backward_own_kernel,
        "backward_own",
        shape((flat.shape[0], turned.shape[1] // 2), F32),
        604 << 20,
        scalars=1,
        arrays=2,
    )(core, flat, turned)


def pack_halves(ref, values, vectors):
    classes, wide = values.shape
    size = jnp.max(jnp.abs(values), axis=1, keepdims=True)
    powers = exponents(size) - 14.0
    ref[:classes] = values * jnp.exp2(-powers)
    empty = jnp.zeros((2 * LANES - classes, LANES), F32)
    powers = jnp.concatenate([jnp.broadcast_to(powers, (classes, LANES)), empty], axis=0).T[:1]
    row = lax.broadcasted_iota(jnp.int32, (EXTRA, 2 * LANES), 0)
    out = jnp.zeros((EXTRA, 2 * LANES), F32)
    for p, piece in enumerate(half_pieces(powers, vectors)):
        out = jnp.where(row == p, piece, out)
    ref[classes:, : 2 * LANES] = out
    ref[classes:, 2 * LANES :] = jnp.zeros((EXTRA, wide - 2 * LANES), F32)


def unpack_halves(ref):
    classes = ref.shape[0] - EXTRA
    return ref[:classes] * column(jnp.exp2(ref[classes : classes + 1, : 2 * LANES]), classes)


def unpack_vector(ref):
    classes = ref.shape[0] - EXTRA
    power, high, low = (ref[classes + p : classes + p + 1, : 2 * LANES] for p in range(1, 4))
    return jnp.exp2(power) * (high + low / 2048.0)


def join_kernel(own_ref, row_ref, got_ref, one_ref, two_ref):
    classes, wide = own_ref.shape[0], one_ref.shape[1]
    for k, ref in enumerate((one_ref, two_ref)):
        here = slice(k * wide, (k + 1) * wide)
        vectors = [row_ref[:1] + got_ref[classes : classes + 1, : 2 * LANES]] if k == 0 else []
        pack_halves(ref, own_ref[:, here] + got_ref[:classes, here], vectors)


def join(own, row, got):
    half = shape((own.shape[0] + EXTRA, own.shape[1] // 2), F32)
    return call(join_kernel, "join", [half, half], 1 << 20, arrays=3)(own, row, got)


def add_kernel(own_ref, got_ref, sum_ref):
    vector = unpack_vector(own_ref) + unpack_vector(got_ref)
    pack_halves(sum_ref, unpack_halves(own_ref) + unpack_halves(got_ref), [vector])


def add_halves(own, got):
    return call(add_kernel, "add", shape(own.shape, F32), 1 << 20, arrays=2)(own, got)


def gradient_kernel(base_ref, label_ref, weight_ref, hessian_ref, send_ref):
    classes, share = base_ref.shape
    base = base_ref[...]
    probability = jax.nn.sigmoid(base)
    row = lax.broadcasted_iota(jnp.int32, (classes, share), 0)
    target = jnp.where(row == label_ref[...], 1.0, 0.0)
    hessian_ref[...] = weight_ref[...] * probability * (1.0 - probability)
    gradient = (weight_ref[...] * (probability - target)).astype(BF16)
    for k in range(send_ref.shape[0]):
        send_ref[k] = gradient


def gradient(base, label, weight, shares):
    return call(
        gradient_kernel,
        "gradient",
        [shape(base.shape, F32), shape((shares,) + base.shape, BF16)],
        1 << 20,
        arrays=3,
    )(base, label, weight)


def residual_kernel(
    total, one_ref, one_in_ref, two_ref, two_in_ref, high_ref, low_ref, high_turned_ref,
    low_turned_ref, residual_ref, lifted_ref, part_ref,
):
    one = unpack_halves(one_ref) + unpack_halves(one_in_ref)
    two = unpack_halves(two_ref) + unpack_halves(two_in_ref)
    sums = jnp.concatenate([one, two], axis=1)
    residual = block_products(sums, high_ref, low_ref) * (-1.0 / total)
    residual_ref[...] = residual
    lifted = block_products(residual, high_turned_ref, low_turned_ref).astype(BF16)
    lifted_ref[...] = lifted
    zero = jnp.zeros((1, 2 * LANES), F32)
    part_ref[...] = stack_rows(
        [lane_sums(residual * residual), zero, lane_sums(jnp.abs(lifted.astype(F32)))]
    )


def first_residual(total, sums, blocks):
    classes, wide = sums[2].shape[0] - EXTRA, sums[2].shape[1]
    return call(
        functools.partial(residual_kernel, total),
        "residual",
        [
            shape((classes, 2 * wide), F32),
            shape((classes, 2 * wide), BF16),
            shape((8, 2 * LANES), F32),
        ],
        450 << 20,
        arrays=8,
    )(*sums, *blocks)


def weigh_kernel(parts_ref, hessian_ref, image_ref, norm_ref, send_ref):
    classes = hessian_ref.shape[0]
    image = sum_scaled(parts_ref, classes)
    image_ref[...] = image
    norm_ref[...] = stack_rows([half_vector(parts_ref, classes, 0)])
    weighted = (hessian_ref[...] * image).astype(BF16)
    extra = rows_of([lane_sums(weighted.astype(F32) * image)])
    for k in range(send_ref.shape[0]):
        send_ref[k, :classes] = weighted
        send_ref[k, classes:] = extra


def weigh(parts, hessian):
    return call(
        weigh_kernel,
        "weigh",
        [
            shape(hessian.shape, F32),
            shape((8, 2 * LANES), F32),
            shape((parts.shape[0], hessian.shape[0] + EXTRA, hessian.shape[1]), BF16),
        ],
        1 << 20,
        arrays=2,
    )(parts, hessian)


def step_kernel(
    total, one_ref, one_in_ref, two_ref, two_in_ref, high_ref, low_ref, high_turned_ref,
    low_turned_ref, residual_ref, norm_ref, lifted_ref, part_ref, rough_ref,
):
    classes = residual_ref.shape[0]
    one = unpack_halves(one_ref) + unpack_halves(one_in_ref)
    two = unpack_halves(two_ref) + unpack_halves(two_in_ref)
    curve = (unpack_vector(one_ref) + unpack_vector(one_in_ref)) / total
    norm = norm_ref[:1]
    lane = lax.broadcasted_iota(jnp.int32, (1, 2 * LANES), 1)
    rough = jnp.where(lane < classes, norm / (curve + RIDGE * norm), 0.0)
    rough_ref[...] = stack_rows([rough])
    sums = jnp.concatenate([one, two], axis=1)
    old = residual_ref[...]
    image = block_products(sums, high_ref, low_ref) / total + RIDGE * old
    new = old - column(rough, classes) * image
    lifted = block_products(new, high_turned_ref, low_turned_ref).astype(BF16)
    lifted_ref[...] = lifted
    part_ref[...] = stack_rows(
        [lane_sums(old * new), lane_sums(new * new), lane_sums(jnp.abs(lifted.astype(F32)))]
    )


def step(total, sums, blocks, residual, norm):
    row = shape((8, 2 * LANES), F32)
    return call(
        functools.partial(step_kernel, total),
        "step",
        [shape(residual.shape, BF16), row, row],
        450 << 20,
        arrays=10,
    )(*sums, *blocks, residual, norm)


def curve_kernel(
    parts_ref, hessian_ref, image_ref, norm_ref, rough_ref, last_ref, scales_ref, curve_ref
):
    classes = hessian_ref.shape[0]
    last = sum_scaled(parts_ref, classes)
    last_ref[...] = last
    cross = half_vector(parts_ref, classes, 0)
    norm_rough = half_vector(parts_ref, classes, 1)
    norm = norm_ref[:1]
    lane = lax.broadcasted_iota(jnp.int32, (1, 2 * LANES), 1)
    excess = jnp.where(lane < classes, cross / (norm - cross), 0.0)
    grown = 1.0 + excess
    norm_next = grown * (grown * norm_rough - 2.0 * excess * cross) + excess * excess * norm
    ratio = jnp.where(lane < classes, norm_next / norm, 0.0)
    ridge = RIDGE * (norm_next + ratio * ratio * norm)
    scales_ref[...] = stack_rows(
        [rough_ref[:1] * grown, grown, ratio - excess, norm_next, ridge]
    )
    rows = column(grown, classes) * last + column(ratio - excess, classes) * image_ref[...]
    weighted = (hessian_ref[...] * rows).astype(BF16).astype(F32)
    curve_ref[...] = lane_sums(weighted * rows)


def last_curve(parts, hessian, image, norm, rough):
    row = shape((8, 2 * LANES), F32)
    return call(
        curve_kernel,
        "curve",
        [shape(hessian.shape, F32), row, shape((1, 2 * LANES), F32)],
        1 << 20,
        arrays=5,
    )(parts, hessian, image, norm, rough)


def margins_kernel(total, curve_ref, scales_ref, base_ref, image_ref, last_ref, margins_ref):
    classes = base_ref.shape[0]
    curve = jnp.sum(curve_ref[:, 0], axis=0, keepdims=True)
    first, grown, other = scales_ref[0:1], scales_ref[1:2], scales_ref[2:3]
    lane = lax.broadcasted_iota(jnp.int32, (1, 2 * LANES), 1)
    second = jnp.where(
        lane < classes, scales_ref[3:4] / (curve / total + scales_ref[4:5]), 0.0
    )
    margins_ref[...] = (
        base_ref[...]
        + column(first + second * other, classes) * image_ref[...]
        + column(second * grown, classes) * last_ref[...]
    )


def margins(total, curve, scales, base, image, last):
    return call(
        functools.partial(margins_kernel, total), "margins", shape(base.shape, F32), 1 << 20, arrays=5
    )(curve, scales, base, image, last)


def shards(pool, indices, labels, example_weight, centers, alpha, precond):
    n_ex, n_ctr = lax.axis_size("ex"), lax.axis_size("ctr")
    classes, count = alpha.shape
    examples = indices.shape[0]
    share = examples // n_ctr
    total = float(examples * n_ex)
    core = (lax.axis_index("ex") % 2).reshape(1)
    core_pairs = [(i, i ^ 1) for i in range(n_ex)]

    def over_y(array, flip):
        pairs = [(2 * y + c, 2 * (y ^ flip) + c) for y in range(n_ex // 2) for c in range(2)]
        return lax.ppermute(array, "ex", pairs)

    def over_cores(array):
        return lax.ppermute(array, "ex", core_pairs)

    def trade(parts):
        return lax.all_to_all(parts, "ctr", 0, 0)

    def trade_halves(parts):
        return trade(parts.astype(F16)).astype(F32)

    def swap(array, flip):
        array = lax.reduce_precision(array, 5, 10)
        return array, over_y(array.astype(F16), flip).astype(F32)

    def sum_examples(own, row, got):
        one, two = join(own, row, got)
        one, two = swap(one, 1), swap(two, 3)
        one, two = add_halves(*one), add_halves(*two)
        return *swap(one, 3), *swap(two, 1)

    offset = lax.axis_index("ctr") * share
    label = lax.dynamic_slice_in_dim(labels, offset, share, 0).reshape(1, share)
    weight = lax.dynamic_slice_in_dim(example_weight, offset, share, 0).reshape(1, share)
    index = indices.reshape(1, examples)
    sides, one_hot, chunk = prepare(index, centers, pool.shape[1])
    row_pool = trade(copies(pool, n_ctr))
    row_pool, sides, one_hot, chunk, label, weight, core = lax.optimization_barrier(
        (row_pool, sides, one_hot, chunk, label, weight, core)
    )
    tile, turned, rows = make_tile(chunk, row_pool, one_hot, sides, alpha, share)
    base = jnp.sum(trade_halves(rows), axis=0)
    hessian, send = gradient(base, label, weight, n_ctr)

    other, flat, row = backward_other(core, trade(send), turned, classes)
    got = over_cores(other)
    own = backward_own(core, flat, turned)
    got, late_core = lax.optimization_barrier((got, core))
    blocks = factors(late_core, precond)
    sums = sum_examples(own, row, got)
    residual, lifted, part = first_residual(total, sums, blocks)
    rows = forward(core, lifted, over_cores(lifted), part, over_cores(part), tile, share)
    image, norm, send = weigh(trade_halves(rows), hessian)

    other, flat, row = backward_other(core, trade(send), turned, classes)
    got = over_cores(other)
    sums = sum_examples(backward_own(core, flat, turned), row, got)
    lifted, part, rough = step(total, sums, blocks, residual, norm)
    rows = forward(core, lifted, over_cores(lifted), part, over_cores(part), tile, share)
    last, scales, curve = last_curve(trade_halves(rows), hessian, image, norm, rough)

    curve = lax.all_to_all(jnp.broadcast_to(curve, (n_ex,) + curve.shape), "ex", 0, 0)
    curve = jnp.sum(curve, axis=0)
    curve = trade(jnp.broadcast_to(curve, (n_ctr,) + curve.shape))
    return margins(total, curve, scales, base, image, last)


def solution(mesh):
    return jax.shard_map(
        shards,
        mesh=mesh,
        in_specs=(
            P(None, ("ex", "ctr")),
            P("ex"),
            P("ex"),
            P("ex"),
            P(None, "ctr"),
            P(None, "ctr"),
            P("ctr", None),
        ),
        out_specs=P(None, ("ex", "ctr")),
        check_vma=False,
    )
```

```python
import functools
import math

import jax
import jax.numpy as jnp
from jax import lax
from jax.experimental import pallas as pl
from jax.experimental.pallas import tpu as pltpu
from jax.sharding import PartitionSpec as P

RIDGE = 0.0001
F32 = jnp.float32
F16 = jnp.float16
BF16 = jnp.bfloat16
VMEM_BYTES = 24 * 1024 * 1024
DEPTH = 128
BAND = 256
EXTRA = 16
SCALARS = 8
LANES = 128
NT = (((1,), (1,)), ((), ()))
TN = (((0,), (0,)), ((), ()))


def split3(values):
    high = values.astype(BF16)
    rest = values - high.astype(F32)
    middle = rest.astype(BF16)
    low = (rest - middle.astype(F32)).astype(BF16)
    return high, middle, low


SCALAR = pl.BlockSpec(memory_space=pltpu.SMEM)
WHOLE = pl.BlockSpec(memory_space=pltpu.VMEM)
ANYWHERE = pl.BlockSpec(memory_space=pl.ANY)


def call(kernel, name, out_shape, flops, scratch=(), scalars=0, anywhere=0, arrays=0):
    shapes = out_shape if isinstance(out_shape, list) else [out_shape]
    size = sum(math.prod(s.shape) * s.dtype.itemsize for s in shapes)
    return pl.pallas_call(
        kernel,
        out_shape=out_shape,
        scratch_shapes=list(scratch),
        in_specs=[SCALAR] * scalars + [ANYWHERE] * anywhere + [WHOLE] * arrays,
        compiler_params=pltpu.CompilerParams(vmem_limit_bytes=VMEM_BYTES),
        cost_estimate=pl.CostEstimate(flops=flops, bytes_accessed=size, transcendentals=0),
        name=name,
    )


def rows_of(vectors):
    row = lax.broadcasted_iota(jnp.int32, (EXTRA, LANES), 0)
    out = jnp.zeros((EXTRA, LANES), F32)
    for k, vector in enumerate(vectors):
        for p, piece in enumerate(split3(vector)):
            for q in range(2):
                value = piece.astype(F32)[:, q * LANES : (q + 1) * LANES]
                out = jnp.where(row == 6 * k + 2 * p + q, value, out)
    return out.astype(BF16)


def read_rows(summed, k):
    halves = [
        sum(summed[6 * k + 2 * p + q : 6 * k + 2 * p + q + 1] for p in range(3)) for q in range(2)
    ]
    return jnp.concatenate(halves, axis=1)


def exponents(bounds):
    return jnp.ceil(jnp.log2(jnp.maximum(bounds, 1e-30)))


def half_pieces(powers, vectors):
    pieces = [powers]
    for vector in vectors:
        power = exponents(jnp.abs(vector)) + 1.0
        scaled = vector * jnp.exp2(-power) * 2048.0
        high = jnp.floor(scaled + 0.5)
        pieces += [power, high / 2048.0, jnp.floor((scaled - high) * 2048.0 + 0.5) / 2048.0]
    return pieces


def half_rows(powers, vectors):
    row = lax.broadcasted_iota(jnp.int32, (SCALARS, LANES), 0)
    lane = lax.broadcasted_iota(jnp.int32, (SCALARS, LANES), 1)
    out = jnp.zeros((SCALARS, LANES), F32)
    for p, piece in enumerate(half_pieces(powers, vectors)):
        out = jnp.where(row == p, piece[:, :LANES], out)
        rest = piece[:, LANES : LANES + 16]
        rest = jnp.concatenate([rest] * (LANES // 16), axis=1)
        out = jnp.where((row == SCALARS - 1) & (lane // 16 == p), rest, out)
    return out


def half_row(parts_ref, first, p):
    rest = parts_ref[:, first + SCALARS - 1, :][:, 16 * p : 16 * p + 16]
    empty = jnp.zeros((parts_ref.shape[0], LANES - 16), F32)
    return jnp.concatenate([parts_ref[:, first + p, :], rest, empty], axis=1)


def half_vector(parts_ref, first, k):
    power, high, low = (half_row(parts_ref, first, 1 + 3 * k + p) for p in range(3))
    return jnp.sum(jnp.exp2(power) * (high + low / 2048.0), axis=0, keepdims=True)


def sum_scaled(parts_ref, classes):
    scales = jnp.exp2(half_row(parts_ref, classes, 0)).T
    total = parts_ref[0, :classes] * scales[:classes, :1]
    for k in range(1, parts_ref.shape[0]):
        total = total + parts_ref[k, :classes] * scales[:classes, k : k + 1]
    return total


def column(vector, classes):
    return jnp.broadcast_to(vector, (8, vector.shape[1])).T[:classes, :1]


def lane_sums(values):
    folded = sum(values[:, k : k + LANES] for k in range(0, values.shape[1], LANES))
    empty = jnp.zeros((2 * LANES - values.shape[0], LANES), F32)
    return jnp.sum(jnp.concatenate([folded, empty], axis=0).T, axis=0, keepdims=True)


def stack_rows(vectors):
    row = lax.broadcasted_iota(jnp.int32, (8, 2 * LANES), 0)
    out = jnp.zeros((8, 2 * LANES), F32)
    for k, vector in enumerate(vectors):
        out = jnp.where(row == k, vector, out)
    return out


def sum_parts(ref):
    total = ref[0].astype(F32)
    for k in range(1, ref.shape[0]):
        total = total + ref[k].astype(F32)
    return total


def shape(dims, dtype):
    return jax.ShapeDtypeStruct(dims, dtype)


def tail(squares, first, pad):
    pieces = [p.astype(F32) for p in split3(-0.5 * squares)]
    row = lax.broadcasted_iota(jnp.int32, (pad, squares.shape[1]), 0)
    out = jnp.where((row >= 3 - first) & (row < 6 - first), 1.0, 0.0)
    for k in range(3):
        out = jnp.where(row == k + first, pieces[k], out)
    return out


def copies_kernel(block_ref, copies_ref):
    features, lanes = block_ref.shape
    for k in range(copies_ref.shape[0]):
        for q in range(lanes // LANES):
            copies_ref[k, q * features : (q + 1) * features] = block_ref[
                :, q * LANES : (q + 1) * LANES
            ]


def copies(block, number):
    out = shape((number, block.size // LANES, LANES), block.dtype)
    return call(copies_kernel, "copies", out, 1 << 20, arrays=1)(block)


def prepare_kernel(index_ref, centers_ref, sides_ref, one_hot_ref, chunk_ref):
    features, count = centers_ref.shape
    lanes = one_hot_ref.shape[0]
    center_float = centers_ref[...].astype(F32)
    center_sq = jnp.sum(center_float * center_float, axis=0, keepdims=True)
    side = jnp.concatenate([center_float, tail(center_sq, 3, DEPTH - features)], axis=0)
    sides_ref[...] = side.T.astype(BF16)
    chunk_ref[...] = index_ref[...] // lanes
    within = index_ref[...] % lanes
    row = lax.broadcasted_iota(jnp.int32, (lanes, index_ref.shape[1]), 0)
    one_hot_ref[...] = (row == within).astype(F32).astype(BF16)


def prepare(index, centers, lanes):
    features, count = centers.shape
    examples = index.shape[1]
    return call(
        prepare_kernel,
        "prepare",
        [shape((count, DEPTH), BF16), shape((lanes, examples), BF16), shape(index.shape, jnp.int32)],
        1 << 20,
        arrays=2,
    )(index, centers)


def tile_kernel(
    alpha_hbm, chunk_ref, pool_ref, one_hot_ref, sides_ref, tile_ref, turned_ref, rows_ref,
    side_ref, alpha_ref, alpha_sem,
):
    fetch = pltpu.make_async_copy(alpha_hbm, alpha_ref, alpha_sem)
    fetch.start()
    chunks, height, _ = pool_ref.shape
    lanes = one_hot_ref.shape[0]
    features = height * LANES // lanes
    count, examples = tile_ref.shape
    share = rows_ref.shape[2]
    scale = 4.0 / features * math.log2(math.e)
    pool = jnp.concatenate(
        [
            pool_ref[:, q * features : (q + 1) * features, :].reshape(chunks * features, LANES)
            for q in range(lanes // LANES)
        ],
        axis=1,
    )
    for b in range(examples // BAND):
        here = slice(b * BAND, (b + 1) * BAND)
        chunk = chunk_ref[:, here]
        picked = jnp.dot(pool, one_hot_ref[:, here], preferred_element_type=F32)
        points = jnp.where(chunk == 0, picked[:features], 0.0)
        for k in range(1, chunks):
            points = jnp.where(chunk == k, picked[k * features : (k + 1) * features], points)
        point_sq = jnp.sum(points * points, axis=0, keepdims=True)
        side = jnp.concatenate([points, tail(point_sq, 0, DEPTH - features)], axis=0)
        side_ref[:, here] = side.astype(BF16)
    for b in range(count // BAND):
        here = slice(b * BAND, (b + 1) * BAND)
        near = jnp.dot(sides_ref[here, :], side_ref[...], preferred_element_type=F32)
        values = jnp.exp2(near * scale).astype(BF16)
        tile_ref[here, :] = values
        turned_ref[:, here] = values.T
    fetch.wait()
    for b in range(examples // BAND):
        here = slice(b * BAND, (b + 1) * BAND)
        rows = jnp.dot(alpha_ref[...], tile_ref[:, here], preferred_element_type=F32)
        for k in range(BAND // share):
            rows_ref[b * (BAND // share) + k] = rows[:, k * share : (k + 1) * share]


def make_tile(chunk, row_pool, one_hot, sides, alpha, share):
    examples, count = chunk.shape[1], sides.shape[0]
    classes = alpha.shape[0]
    return call(
        tile_kernel,
        "tile",
        [
            shape((count, examples), BF16),
            shape((examples, count), BF16),
            shape((examples // share, classes, share), F32),
        ],
        4 << 30,
        [
            pltpu.VMEM((DEPTH, examples), BF16),
            pltpu.VMEM(alpha.shape, BF16),
            pltpu.SemaphoreType.DMA,
        ],
        anywhere=1,
        arrays=4,
    )(alpha, chunk, row_pool, one_hot, sides)


def factors_kernel(core_ref, precond_ref, high_ref, low_ref, high_turned_ref, low_turned_ref):
    order = precond_ref.shape[1]
    half = high_ref.shape[0]
    first = core_ref[0] * half
    for k in range(half // order):
        here = slice(k * order, (k + 1) * order)
        block = precond_ref[pl.ds(pl.multiple_of(first + k * order, order), order), :]
        high = block.astype(BF16)
        high_ref[here] = high
        low_ref[here] = (block - high.astype(F32)).astype(BF16)
        turned = block.T
        high = turned.astype(BF16)
        high_turned_ref[here] = high
        low_turned_ref[here] = (turned - high.astype(F32)).astype(BF16)


def factors(core, precond):
    out = shape((precond.shape[0] // 2, precond.shape[1]), BF16)
    return call(factors_kernel, "factors", [out] * 4, 1 << 20, scalars=1, arrays=1)(core, precond)


def block_products(values, high_ref, low_ref):
    order = high_ref.shape[1]
    out = []
    for k in range(high_ref.shape[0] // order):
        here = slice(k * order, (k + 1) * order)
        block = values[:, here]
        high = block.astype(BF16)
        low = (block - high.astype(F32)).astype(BF16)
        product = jnp.dot(high, high_ref[here], preferred_element_type=F32)
        product += jnp.dot(high, low_ref[here], preferred_element_type=F32)
        product += jnp.dot(low, high_ref[here], preferred_element_type=F32)
        out.append(product)
    return jnp.concatenate(out, axis=1)


def forward_own_kernel(core_ref, own_ref, tile_ref, first_ref):
    half = own_ref.shape[1]
    mine = pl.ds(pl.multiple_of(core_ref[0] * half, half), half)
    for b in range(first_ref.shape[1] // BAND):
        here = slice(b * BAND, (b + 1) * BAND)
        first_ref[:, here] = jnp.dot(own_ref[...], tile_ref[mine, here], preferred_element_type=F32)


def forward_kernel(
    core_ref, first_ref, other_ref, own_part_ref, other_part_ref, tile_ref, rows_ref
):
    classes, half = other_ref.shape
    share = rows_ref.shape[2]
    examples = tile_ref.shape[1]
    theirs = pl.ds(pl.multiple_of((1 - core_ref[0]) * half, half), half)
    part = own_part_ref[...] + other_part_ref[...]
    powers = exponents(part[2:3]) - 14.0
    extra = half_rows(powers, [part[:1], part[1:2]])
    scales = column(jnp.exp2(-powers), classes)
    for b in range(examples // BAND):
        here = slice(b * BAND, (b + 1) * BAND)
        rows = jnp.dot(other_ref[...], tile_ref[theirs, here], preferred_element_type=F32)
        rows = (rows + first_ref[:, here]) * scales
        for k in range(BAND // share):
            at = b * (BAND // share) + k
            rows_ref[at, :classes] = rows[:, k * share : (k + 1) * share]
            rows_ref[at, classes:] = extra


def forward(core, lifted, other, own_part, other_part, tile, share):
    classes = lifted.shape[0]
    examples = tile.shape[1]
    first = call(
        forward_own_kernel,
        "forward_own",
        shape((classes, examples), F32),
        604 << 20,
        scalars=1,
        arrays=2,
    )(core, lifted, tile)
    return call(
        forward_kernel,
        "forward",
        shape((examples // share, classes + SCALARS, share), F32),
        604 << 20,
        scalars=1,
        arrays=5,
    )(core, first, other, own_part, other_part, tile)


def backward_other_kernel(core_ref, values_ref, turned_ref, other_ref, flat_ref, row_ref):
    shares, height, share = values_ref.shape
    classes, examples = flat_ref.shape
    half = other_ref.shape[1]
    for k in range(shares):
        flat_ref[:, k * share : (k + 1) * share] = values_ref[k, :classes]
    row = jnp.zeros((8, 2 * LANES), F32)
    if height > classes:
        total = values_ref[0, classes:].astype(F32)
        for k in range(1, shares):
            total = total + values_ref[k, classes:].astype(F32)
        row = jnp.broadcast_to(read_rows(total, 0), (8, 2 * LANES))
    row_ref[...] = row
    other_ref[classes:, : 2 * LANES] = row
    other_ref[classes:, 2 * LANES :] = jnp.zeros((8, half - 2 * LANES), F32)
    for b in range(half // BAND):
        there = pl.ds(pl.multiple_of((1 - core_ref[0]) * half + b * BAND, BAND), BAND)
        other_ref[:classes, b * BAND : (b + 1) * BAND] = jnp.dot(
            flat_ref[...], turned_ref[:, there], preferred_element_type=F32
        )


def backward_own_kernel(core_ref, flat_ref, turned_ref, own_ref):
    half = own_ref.shape[1]
    for b in range(half // BAND):
        there = pl.ds(pl.multiple_of(core_ref[0] * half + b * BAND, BAND), BAND)
        own_ref[:, b * BAND : (b + 1) * BAND] = jnp.dot(
            flat_ref[...], turned_ref[:, there], preferred_element_type=F32
        )


def backward_other(core, values, turned, classes):
    examples, count = turned.shape
    return call(
        backward_other_kernel,
        "backward_other",
        [
            shape((classes + 8, count // 2), F32),
            shape((classes, examples), BF16),
            shape((8, 2 * LANES), F32),
        ],
        604 << 20,
        scalars=1,
        arrays=2,
    )(core, values, turned)


def backward_own(core, flat, turned):
    return call(
        backward_own_kernel,
        "backward_own",
        shape((flat.shape[0], turned.shape[1] // 2), F32),
        604 << 20,
        scalars=1,
        arrays=2,
    )(core, flat, turned)


def pack_halves(ref, values, vectors):
    classes, wide = values.shape
    size = jnp.max(jnp.abs(values), axis=1, keepdims=True)
    powers = exponents(size) - 14.0
    ref[:classes] = values * jnp.exp2(-powers)
    empty = jnp.zeros((2 * LANES - classes, LANES), F32)
    powers = jnp.concatenate([jnp.broadcast_to(powers, (classes, LANES)), empty], axis=0).T[:1]
    row = lax.broadcasted_iota(jnp.int32, (SCALARS, 2 * LANES), 0)
    out = jnp.zeros((SCALARS, 2 * LANES), F32)
    for p, piece in enumerate(half_pieces(powers, vectors)):
        out = jnp.where(row == p, piece, out)
    ref[classes:, : 2 * LANES] = out
    ref[classes:, 2 * LANES :] = jnp.zeros((SCALARS, wide - 2 * LANES), F32)


def unpack_halves(ref):
    classes = ref.shape[0] - SCALARS
    return ref[:classes] * column(jnp.exp2(ref[classes : classes + 1, : 2 * LANES]), classes)


def unpack_vector(ref):
    classes = ref.shape[0] - SCALARS
    power, high, low = (ref[classes + p : classes + p + 1, : 2 * LANES] for p in range(1, 4))
    return jnp.exp2(power) * (high + low / 2048.0)


def join_kernel(own_ref, row_ref, got_ref, one_ref, two_ref):
    classes, wide = own_ref.shape[0], one_ref.shape[1]
    for k, ref in enumerate((one_ref, two_ref)):
        here = slice(k * wide, (k + 1) * wide)
        vectors = [row_ref[:1] + got_ref[classes : classes + 1, : 2 * LANES]] if k == 0 else []
        pack_halves(ref, own_ref[:, here] + got_ref[:classes, here], vectors)


def join(own, row, got):
    half = shape((own.shape[0] + SCALARS, own.shape[1] // 2), F32)
    return call(join_kernel, "join", [half, half], 1 << 20, arrays=3)(own, row, got)


def add_kernel(own_ref, got_ref, sum_ref):
    vector = unpack_vector(own_ref) + unpack_vector(got_ref)
    pack_halves(sum_ref, unpack_halves(own_ref) + unpack_halves(got_ref), [vector])


def add_halves(own, got):
    return call(add_kernel, "add", shape(own.shape, F32), 1 << 20, arrays=2)(own, got)


def gradient_kernel(base_ref, label_ref, weight_ref, hessian_ref, send_ref):
    classes, share = base_ref.shape
    base = base_ref[...]
    probability = jax.nn.sigmoid(base)
    row = lax.broadcasted_iota(jnp.int32, (classes, share), 0)
    target = jnp.where(row == label_ref[...], 1.0, 0.0)
    hessian_ref[...] = weight_ref[...] * probability * (1.0 - probability)
    gradient = (weight_ref[...] * (probability - target)).astype(BF16)
    for k in range(send_ref.shape[0]):
        send_ref[k] = gradient


def gradient(base, label, weight, shares):
    return call(
        gradient_kernel,
        "gradient",
        [shape(base.shape, F32), shape((shares,) + base.shape, BF16)],
        1 << 20,
        arrays=3,
    )(base, label, weight)


def residual_kernel(
    total, one_ref, one_in_ref, two_ref, two_in_ref, high_ref, low_ref, high_turned_ref,
    low_turned_ref, residual_ref, lifted_ref, part_ref,
):
    one = unpack_halves(one_ref) + unpack_halves(one_in_ref)
    two = unpack_halves(two_ref) + unpack_halves(two_in_ref)
    sums = jnp.concatenate([one, two], axis=1)
    residual = block_products(sums, high_ref, low_ref) * (-1.0 / total)
    residual_ref[...] = residual
    lifted = block_products(residual, high_turned_ref, low_turned_ref).astype(BF16)
    lifted_ref[...] = lifted
    zero = jnp.zeros((1, 2 * LANES), F32)
    part_ref[...] = stack_rows(
        [lane_sums(residual * residual), zero, lane_sums(jnp.abs(lifted.astype(F32)))]
    )


def first_residual(total, sums, blocks):
    classes, wide = sums[2].shape[0] - SCALARS, sums[2].shape[1]
    return call(
        functools.partial(residual_kernel, total),
        "residual",
        [
            shape((classes, 2 * wide), F32),
            shape((classes, 2 * wide), BF16),
            shape((8, 2 * LANES), F32),
        ],
        450 << 20,
        arrays=8,
    )(*sums, *blocks)


def weigh_kernel(parts_ref, hessian_ref, image_ref, norm_ref, send_ref):
    classes = hessian_ref.shape[0]
    image = sum_scaled(parts_ref, classes)
    image_ref[...] = image
    norm_ref[...] = stack_rows([half_vector(parts_ref, classes, 0)])
    weighted = (hessian_ref[...] * image).astype(BF16)
    extra = rows_of([lane_sums(weighted.astype(F32) * image)])
    for k in range(send_ref.shape[0]):
        send_ref[k, :classes] = weighted
        send_ref[k, classes:] = extra


def weigh(parts, hessian):
    return call(
        weigh_kernel,
        "weigh",
        [
            shape(hessian.shape, F32),
            shape((8, 2 * LANES), F32),
            shape((parts.shape[0], hessian.shape[0] + EXTRA, hessian.shape[1]), BF16),
        ],
        1 << 20,
        arrays=2,
    )(parts, hessian)


def step_kernel(
    total, one_ref, one_in_ref, two_ref, two_in_ref, high_ref, low_ref, high_turned_ref,
    low_turned_ref, residual_ref, norm_ref, lifted_ref, part_ref, rough_ref,
):
    classes = residual_ref.shape[0]
    one = unpack_halves(one_ref) + unpack_halves(one_in_ref)
    two = unpack_halves(two_ref) + unpack_halves(two_in_ref)
    curve = (unpack_vector(one_ref) + unpack_vector(one_in_ref)) / total
    norm = norm_ref[:1]
    lane = lax.broadcasted_iota(jnp.int32, (1, 2 * LANES), 1)
    rough = jnp.where(lane < classes, norm / (curve + RIDGE * norm), 0.0)
    rough_ref[...] = stack_rows([rough])
    sums = jnp.concatenate([one, two], axis=1)
    old = residual_ref[...]
    image = block_products(sums, high_ref, low_ref) / total + RIDGE * old
    new = old - column(rough, classes) * image
    lifted = block_products(new, high_turned_ref, low_turned_ref).astype(BF16)
    lifted_ref[...] = lifted
    part_ref[...] = stack_rows(
        [lane_sums(old * new), lane_sums(new * new), lane_sums(jnp.abs(lifted.astype(F32)))]
    )


def step(total, sums, blocks, residual, norm):
    row = shape((8, 2 * LANES), F32)
    return call(
        functools.partial(step_kernel, total),
        "step",
        [shape(residual.shape, BF16), row, row],
        450 << 20,
        arrays=10,
    )(*sums, *blocks, residual, norm)


def curve_kernel(
    parts_ref, hessian_ref, image_ref, norm_ref, rough_ref, last_ref, scales_ref, curve_ref
):
    classes = hessian_ref.shape[0]
    last = sum_scaled(parts_ref, classes)
    last_ref[...] = last
    cross = half_vector(parts_ref, classes, 0)
    norm_rough = half_vector(parts_ref, classes, 1)
    norm = norm_ref[:1]
    lane = lax.broadcasted_iota(jnp.int32, (1, 2 * LANES), 1)
    excess = jnp.where(lane < classes, cross / (norm - cross), 0.0)
    grown = 1.0 + excess
    norm_next = grown * (grown * norm_rough - 2.0 * excess * cross) + excess * excess * norm
    ratio = jnp.where(lane < classes, norm_next / norm, 0.0)
    ridge = RIDGE * (norm_next + ratio * ratio * norm)
    scales_ref[...] = stack_rows(
        [rough_ref[:1] * grown, grown, ratio - excess, norm_next, ridge]
    )
    rows = column(grown, classes) * last + column(ratio - excess, classes) * image_ref[...]
    weighted = (hessian_ref[...] * rows).astype(BF16).astype(F32)
    curve_ref[...] = lane_sums(weighted * rows)


def last_curve(parts, hessian, image, norm, rough):
    row = shape((8, 2 * LANES), F32)
    return call(
        curve_kernel,
        "curve",
        [shape(hessian.shape, F32), row, shape((1, 2 * LANES), F32)],
        1 << 20,
        arrays=5,
    )(parts, hessian, image, norm, rough)


def margins_kernel(total, curve_ref, scales_ref, base_ref, image_ref, last_ref, margins_ref):
    classes = base_ref.shape[0]
    curve = jnp.sum(curve_ref[:, 0], axis=0, keepdims=True)
    first, grown, other = scales_ref[0:1], scales_ref[1:2], scales_ref[2:3]
    lane = lax.broadcasted_iota(jnp.int32, (1, 2 * LANES), 1)
    second = jnp.where(
        lane < classes, scales_ref[3:4] / (curve / total + scales_ref[4:5]), 0.0
    )
    margins_ref[...] = (
        base_ref[...]
        + column(first + second * other, classes) * image_ref[...]
        + column(second * grown, classes) * last_ref[...]
    )


def margins(total, curve, scales, base, image, last):
    return call(
        functools.partial(margins_kernel, total), "margins", shape(base.shape, F32), 1 << 20, arrays=5
    )(curve, scales, base, image, last)


def shards(pool, indices, labels, example_weight, centers, alpha, precond):
    n_ex, n_ctr = lax.axis_size("ex"), lax.axis_size("ctr")
    classes, count = alpha.shape
    examples = indices.shape[0]
    share = examples // n_ctr
    total = float(examples * n_ex)
    core = (lax.axis_index("ex") % 2).reshape(1)
    core_pairs = [(i, i ^ 1) for i in range(n_ex)]

    def over_y(array, flip):
        pairs = [(2 * y + c, 2 * (y ^ flip) + c) for y in range(n_ex // 2) for c in range(2)]
        return lax.ppermute(array, "ex", pairs)

    def over_cores(array):
        return lax.ppermute(array, "ex", core_pairs)

    def trade(parts):
        return lax.all_to_all(parts, "ctr", 0, 0)

    def trade_halves(parts):
        return trade(parts.astype(F16)).astype(F32)

    def swap(array, flip):
        array = lax.reduce_precision(array, 5, 10)
        return array, over_y(array.astype(F16), flip).astype(F32)

    def sum_examples(own, row, got):
        one, two = join(own, row, got)
        one, two = swap(one, 1), swap(two, 3)
        one, two = add_halves(*one), add_halves(*two)
        return *swap(one, 3), *swap(two, 1)

    offset = lax.axis_index("ctr") * share
    label = lax.dynamic_slice_in_dim(labels, offset, share, 0).reshape(1, share)
    weight = lax.dynamic_slice_in_dim(example_weight, offset, share, 0).reshape(1, share)
    index = indices.reshape(1, examples)
    sides, one_hot, chunk = prepare(index, centers, pool.shape[1])
    row_pool = trade(copies(pool, n_ctr))
    row_pool, sides, one_hot, chunk, label, weight, core = lax.optimization_barrier(
        (row_pool, sides, one_hot, chunk, label, weight, core)
    )
    tile, turned, rows = make_tile(chunk, row_pool, one_hot, sides, alpha, share)
    base = jnp.sum(trade_halves(rows), axis=0)
    hessian, send = gradient(base, label, weight, n_ctr)

    other, flat, row = backward_other(core, trade(send), turned, classes)
    got = over_cores(other)
    own = backward_own(core, flat, turned)
    got, late_core = lax.optimization_barrier((got, core))
    blocks = factors(late_core, precond)
    sums = sum_examples(own, row, got)
    residual, lifted, part = first_residual(total, sums, blocks)
    rows = forward(core, lifted, over_cores(lifted), part, over_cores(part), tile, share)
    image, norm, send = weigh(trade_halves(rows), hessian)

    other, flat, row = backward_other(core, trade(send), turned, classes)
    got = over_cores(other)
    sums = sum_examples(backward_own(core, flat, turned), row, got)
    lifted, part, rough = step(total, sums, blocks, residual, norm)
    rows = forward(core, lifted, over_cores(lifted), part, over_cores(part), tile, share)
    last, scales, curve = last_curve(trade_halves(rows), hessian, image, norm, rough)

    curve = jnp.broadcast_to(curve, (n_ex * n_ctr,) + curve.shape)
    curve = lax.all_to_all(curve, ("ex", "ctr"), 0, 0)
    return margins(total, curve, scales, base, image, last)


def solution(mesh):
    return jax.shard_map(
        shards,
        mesh=mesh,
        in_specs=(
            P(None, ("ex", "ctr")),
            P("ex"),
            P("ex"),
            P("ex"),
            P(None, "ctr"),
            P(None, "ctr"),
            P("ctr", None),
        ),
        out_specs=P(None, ("ex", "ctr")),
        check_vma=False,
    )
```

```python
import functools
import math

import jax
import jax.numpy as jnp
from jax import lax
from jax.experimental import pallas as pl
from jax.experimental.pallas import tpu as pltpu
from jax.sharding import PartitionSpec as P

RIDGE = 0.0001
F32 = jnp.float32
F16 = jnp.float16
BF16 = jnp.bfloat16
VMEM_BYTES = 24 * 1024 * 1024
DEPTH = 128
BAND = 256
EXTRA = 16
SCALARS = 8
LANES = 128
NT = (((1,), (1,)), ((), ()))
TN = (((0,), (0,)), ((), ()))


def split3(values):
    high = values.astype(BF16)
    rest = values - high.astype(F32)
    middle = rest.astype(BF16)
    low = (rest - middle.astype(F32)).astype(BF16)
    return high, middle, low


SCALAR = pl.BlockSpec(memory_space=pltpu.SMEM)
WHOLE = pl.BlockSpec(memory_space=pltpu.VMEM)
ANYWHERE = pl.BlockSpec(memory_space=pl.ANY)


def call(kernel, name, out_shape, flops, scratch=(), scalars=0, anywhere=0, arrays=0):
    shapes = out_shape if isinstance(out_shape, list) else [out_shape]
    size = sum(math.prod(s.shape) * s.dtype.itemsize for s in shapes)
    return pl.pallas_call(
        kernel,
        out_shape=out_shape,
        scratch_shapes=list(scratch),
        in_specs=[SCALAR] * scalars + [ANYWHERE] * anywhere + [WHOLE] * arrays,
        compiler_params=pltpu.CompilerParams(vmem_limit_bytes=VMEM_BYTES),
        cost_estimate=pl.CostEstimate(flops=flops, bytes_accessed=size, transcendentals=0),
        name=name,
    )


def rows_of(vectors):
    row = lax.broadcasted_iota(jnp.int32, (EXTRA, LANES), 0)
    out = jnp.zeros((EXTRA, LANES), F32)
    for k, vector in enumerate(vectors):
        for p, piece in enumerate(split3(vector)):
            for q in range(2):
                value = piece.astype(F32)[:, q * LANES : (q + 1) * LANES]
                out = jnp.where(row == 6 * k + 2 * p + q, value, out)
    return out.astype(BF16)


def read_rows(summed, k):
    halves = [
        sum(summed[6 * k + 2 * p + q : 6 * k + 2 * p + q + 1] for p in range(3)) for q in range(2)
    ]
    return jnp.concatenate(halves, axis=1)


def exponents(bounds):
    return jnp.ceil(jnp.log2(jnp.maximum(bounds, 1e-30)))


def half_pieces(powers, vectors):
    pieces = [powers]
    for vector in vectors:
        power = exponents(jnp.abs(vector)) + 1.0
        scaled = vector * jnp.exp2(-power) * 2048.0
        high = jnp.floor(scaled + 0.5)
        pieces += [power, high / 2048.0, jnp.floor((scaled - high) * 2048.0 + 0.5) / 2048.0]
    return pieces


def half_rows(powers, vectors):
    row = lax.broadcasted_iota(jnp.int32, (SCALARS, LANES), 0)
    lane = lax.broadcasted_iota(jnp.int32, (SCALARS, LANES), 1)
    out = jnp.zeros((SCALARS, LANES), F32)
    for p, piece in enumerate(half_pieces(powers, vectors)):
        out = jnp.where(row == p, piece[:, :LANES], out)
        rest = piece[:, LANES : LANES + 16]
        rest = jnp.concatenate([rest] * (LANES // 16), axis=1)
        out = jnp.where((row == SCALARS - 1) & (lane // 16 == p), rest, out)
    return out


def half_row(parts_ref, first, p):
    rest = parts_ref[:, first + SCALARS - 1, :][:, 16 * p : 16 * p + 16]
    empty = jnp.zeros((parts_ref.shape[0], LANES - 16), F32)
    return jnp.concatenate([parts_ref[:, first + p, :], rest, empty], axis=1)


def half_vector(parts_ref, first, k):
    power, high, low = (half_row(parts_ref, first, 1 + 3 * k + p) for p in range(3))
    return jnp.sum(jnp.exp2(power) * (high + low / 2048.0), axis=0, keepdims=True)


def sum_scaled(parts_ref, classes):
    scales = jnp.exp2(half_row(parts_ref, classes, 0)).T
    total = parts_ref[0, :classes] * scales[:classes, :1]
    for k in range(1, parts_ref.shape[0]):
        total = total + parts_ref[k, :classes] * scales[:classes, k : k + 1]
    return total


def column(vector, classes):
    return jnp.broadcast_to(vector, (8, vector.shape[1])).T[:classes, :1]


def lane_sums(values):
    folded = sum(values[:, k : k + LANES] for k in range(0, values.shape[1], LANES))
    empty = jnp.zeros((2 * LANES - values.shape[0], LANES), F32)
    return jnp.sum(jnp.concatenate([folded, empty], axis=0).T, axis=0, keepdims=True)


def stack_rows(vectors):
    row = lax.broadcasted_iota(jnp.int32, (8, 2 * LANES), 0)
    out = jnp.zeros((8, 2 * LANES), F32)
    for k, vector in enumerate(vectors):
        out = jnp.where(row == k, vector, out)
    return out


def sum_parts(ref):
    total = ref[0].astype(F32)
    for k in range(1, ref.shape[0]):
        total = total + ref[k].astype(F32)
    return total


def shape(dims, dtype):
    return jax.ShapeDtypeStruct(dims, dtype)


def tail(squares, first, pad):
    pieces = [p.astype(F32) for p in split3(-0.5 * squares)]
    row = lax.broadcasted_iota(jnp.int32, (pad, squares.shape[1]), 0)
    out = jnp.where((row >= 3 - first) & (row < 6 - first), 1.0, 0.0)
    for k in range(3):
        out = jnp.where(row == k + first, pieces[k], out)
    return out


def copies_kernel(block_ref, copies_ref):
    features, lanes = block_ref.shape
    for k in range(copies_ref.shape[0]):
        for q in range(lanes // LANES):
            copies_ref[k, q * features : (q + 1) * features] = block_ref[
                :, q * LANES : (q + 1) * LANES
            ]


def copies(block, number):
    out = shape((number, block.size // LANES, LANES), block.dtype)
    return call(copies_kernel, "copies", out, 1 << 20, arrays=1)(block)


def prepare_kernel(index_ref, centers_ref, sides_ref, one_hot_ref, chunk_ref):
    features, count = centers_ref.shape
    lanes = one_hot_ref.shape[0]
    center_float = centers_ref[...].astype(F32)
    center_sq = jnp.sum(center_float * center_float, axis=0, keepdims=True)
    side = jnp.concatenate([center_float, tail(center_sq, 3, DEPTH - features)], axis=0)
    sides_ref[...] = side.T.astype(BF16)
    chunk_ref[...] = index_ref[...] // lanes
    within = index_ref[...] % lanes
    row = lax.broadcasted_iota(jnp.int32, (lanes, index_ref.shape[1]), 0)
    one_hot_ref[...] = (row == within).astype(F32).astype(BF16)


def prepare(index, centers, lanes):
    features, count = centers.shape
    examples = index.shape[1]
    return call(
        prepare_kernel,
        "prepare",
        [shape((count, DEPTH), BF16), shape((lanes, examples), BF16), shape(index.shape, jnp.int32)],
        1 << 20,
        arrays=2,
    )(index, centers)


def tile_kernel(
    alpha_hbm, chunk_ref, pool_ref, one_hot_ref, sides_ref, tile_ref, turned_ref, rows_ref,
    side_ref, base_ref, alpha_ref, alpha_sem,
):
    fetch = pltpu.make_async_copy(alpha_hbm, alpha_ref, alpha_sem)
    fetch.start()
    chunks, height, _ = pool_ref.shape
    lanes = one_hot_ref.shape[0]
    features = height * LANES // lanes
    count, examples = tile_ref.shape
    share = rows_ref.shape[2]
    scale = 4.0 / features * math.log2(math.e)
    pool = jnp.concatenate(
        [
            pool_ref[:, q * features : (q + 1) * features, :].reshape(chunks * features, LANES)
            for q in range(lanes // LANES)
        ],
        axis=1,
    )
    for b in range(examples // BAND):
        here = slice(b * BAND, (b + 1) * BAND)
        chunk = chunk_ref[:, here]
        picked = jnp.dot(pool, one_hot_ref[:, here], preferred_element_type=F32)
        points = jnp.where(chunk == 0, picked[:features], 0.0)
        for k in range(1, chunks):
            points = jnp.where(chunk == k, picked[k * features : (k + 1) * features], points)
        point_sq = jnp.sum(points * points, axis=0, keepdims=True)
        side = jnp.concatenate([points, tail(point_sq, 0, DEPTH - features)], axis=0)
        side_ref[:, here] = side.astype(BF16)
    fetch.wait()
    for b in range(count // BAND):
        here = slice(b * BAND, (b + 1) * BAND)
        near = jnp.dot(sides_ref[here, :], side_ref[...], preferred_element_type=F32)
        values = jnp.exp2(near * scale).astype(BF16)
        tile_ref[here, :] = values
        turned_ref[:, here] = values.T
        rows = jnp.dot(alpha_ref[:, here], values, preferred_element_type=F32)
        base_ref[...] = rows if b == 0 else base_ref[...] + rows
    for k in range(examples // share):
        rows_ref[k] = base_ref[:, k * share : (k + 1) * share]


def make_tile(chunk, row_pool, one_hot, sides, alpha, share):
    examples, count = chunk.shape[1], sides.shape[0]
    classes = alpha.shape[0]
    return call(
        tile_kernel,
        "tile",
        [
            shape((count, examples), BF16),
            shape((examples, count), BF16),
            shape((examples // share, classes, share), F32),
        ],
        4 << 30,
        [
            pltpu.VMEM((DEPTH, examples), BF16),
            pltpu.VMEM((classes, examples), F32),
            pltpu.VMEM(alpha.shape, BF16),
            pltpu.SemaphoreType.DMA,
        ],
        anywhere=1,
        arrays=4,
    )(alpha, chunk, row_pool, one_hot, sides)


def factors_kernel(core_ref, precond_ref, high_ref, low_ref, high_turned_ref, low_turned_ref):
    order = precond_ref.shape[1]
    half = high_ref.shape[0]
    first = core_ref[0] * half
    for k in range(half // order):
        here = slice(k * order, (k + 1) * order)
        block = precond_ref[pl.ds(pl.multiple_of(first + k * order, order), order), :]
        high = block.astype(BF16)
        high_ref[here] = high
        low_ref[here] = (block - high.astype(F32)).astype(BF16)
        turned = block.T
        high = turned.astype(BF16)
        high_turned_ref[here] = high
        low_turned_ref[here] = (turned - high.astype(F32)).astype(BF16)


def factors(core, precond):
    out = shape((precond.shape[0] // 2, precond.shape[1]), BF16)
    return call(factors_kernel, "factors", [out] * 4, 1 << 20, scalars=1, arrays=1)(core, precond)


def block_products(values, high_ref, low_ref):
    order = high_ref.shape[1]
    out = []
    for k in range(high_ref.shape[0] // order):
        here = slice(k * order, (k + 1) * order)
        block = values[:, here]
        high = block.astype(BF16)
        low = (block - high.astype(F32)).astype(BF16)
        product = jnp.dot(high, high_ref[here], preferred_element_type=F32)
        product += jnp.dot(high, low_ref[here], preferred_element_type=F32)
        product += jnp.dot(low, high_ref[here], preferred_element_type=F32)
        out.append(product)
    return jnp.concatenate(out, axis=1)


def put_lifted(ref, lifted, vectors):
    classes, half = lifted.shape
    ref[:classes] = lifted
    row = lax.broadcasted_iota(jnp.int32, (EXTRA, 2 * LANES), 0)
    out = jnp.zeros((EXTRA, 2 * LANES), F32)
    for k, vector in enumerate(vectors):
        for p, piece in enumerate(split3(vector)):
            out = jnp.where(row == 3 * k + p, piece.astype(F32), out)
    ref[classes:, : 2 * LANES] = out.astype(BF16)
    ref[classes:, 2 * LANES :] = jnp.zeros((EXTRA, half - 2 * LANES), BF16)


def forward_own_kernel(core_ref, own_ref, tile_ref, first_ref):
    classes, half = first_ref.shape[0], own_ref.shape[1]
    mine = pl.ds(pl.multiple_of(core_ref[0] * half, half), half)
    for b in range(first_ref.shape[1] // BAND):
        here = slice(b * BAND, (b + 1) * BAND)
        first_ref[:, here] = jnp.dot(
            own_ref[:classes], tile_ref[mine, here], preferred_element_type=F32
        )


def forward_kernel(core_ref, first_ref, own_ref, other_ref, tile_ref, rows_ref):
    classes, half = first_ref.shape[0], other_ref.shape[1]
    share = rows_ref.shape[2]
    examples = tile_ref.shape[1]
    theirs = pl.ds(pl.multiple_of((1 - core_ref[0]) * half, half), half)
    part = [ref[classes:, : 2 * LANES].astype(F32) for ref in (own_ref, other_ref)]
    part = part[0] + part[1]
    part = [part[3 * k : 3 * k + 1] + part[3 * k + 1 : 3 * k + 2] + part[3 * k + 2 : 3 * k + 3] for k in range(3)]
    powers = exponents(part[2]) - 14.0
    extra = half_rows(powers, part[:2])
    scales = column(jnp.exp2(-powers), classes)
    for b in range(examples // BAND):
        here = slice(b * BAND, (b + 1) * BAND)
        rows = jnp.dot(other_ref[:classes], tile_ref[theirs, here], preferred_element_type=F32)
        rows = (rows + first_ref[:, here]) * scales
        for k in range(BAND // share):
            at = b * (BAND // share) + k
            rows_ref[at, :classes] = rows[:, k * share : (k + 1) * share]
            rows_ref[at, classes:] = extra


def forward(core, lifted, other, tile, share):
    classes = lifted.shape[0] - EXTRA
    examples = tile.shape[1]
    first = call(
        forward_own_kernel,
        "forward_own",
        shape((classes, examples), F32),
        604 << 20,
        scalars=1,
        arrays=2,
    )(core, lifted, tile)
    return call(
        forward_kernel,
        "forward",
        shape((examples // share, classes + SCALARS, share), F32),
        604 << 20,
        scalars=1,
        arrays=4,
    )(core, first, lifted, other, tile)


def backward_other_kernel(core_ref, values_ref, turned_ref, other_ref, flat_ref, row_ref):
    shares, height, share = values_ref.shape
    classes, examples = flat_ref.shape
    half = other_ref.shape[1]
    for k in range(shares):
        flat_ref[:, k * share : (k + 1) * share] = values_ref[k, :classes]
    row = jnp.zeros((8, 2 * LANES), F32)
    if height > classes:
        total = values_ref[0, classes:].astype(F32)
        for k in range(1, shares):
            total = total + values_ref[k, classes:].astype(F32)
        row = jnp.broadcast_to(read_rows(total, 0), (8, 2 * LANES))
    row_ref[...] = row
    other_ref[classes:, : 2 * LANES] = row
    other_ref[classes:, 2 * LANES :] = jnp.zeros((8, half - 2 * LANES), F32)
    for b in range(half // BAND):
        there = pl.ds(pl.multiple_of((1 - core_ref[0]) * half + b * BAND, BAND), BAND)
        other_ref[:classes, b * BAND : (b + 1) * BAND] = jnp.dot(
            flat_ref[...], turned_ref[:, there], preferred_element_type=F32
        )


def backward_own_kernel(core_ref, flat_ref, turned_ref, own_ref):
    half = own_ref.shape[1]
    for b in range(half // BAND):
        there = pl.ds(pl.multiple_of(core_ref[0] * half + b * BAND, BAND), BAND)
        own_ref[:, b * BAND : (b + 1) * BAND] = jnp.dot(
            flat_ref[...], turned_ref[:, there], preferred_element_type=F32
        )


def backward_other(core, values, turned, classes):
    examples, count = turned.shape
    return call(
        backward_other_kernel,
        "backward_other",
        [
            shape((classes + 8, count // 2), F32),
            shape((classes, examples), BF16),
            shape((8, 2 * LANES), F32),
        ],
        604 << 20,
        scalars=1,
        arrays=2,
    )(core, values, turned)


def backward_own(core, flat, turned):
    return call(
        backward_own_kernel,
        "backward_own",
        shape((flat.shape[0], turned.shape[1] // 2), F32),
        604 << 20,
        scalars=1,
        arrays=2,
    )(core, flat, turned)


def pack_halves(ref, values, vectors):
    classes, wide = values.shape
    size = jnp.max(jnp.abs(values), axis=1, keepdims=True)
    powers = exponents(size) - 14.0
    ref[:classes] = values * jnp.exp2(-powers)
    empty = jnp.zeros((2 * LANES - classes, LANES), F32)
    powers = jnp.concatenate([jnp.broadcast_to(powers, (classes, LANES)), empty], axis=0).T[:1]
    row = lax.broadcasted_iota(jnp.int32, (SCALARS, 2 * LANES), 0)
    out = jnp.zeros((SCALARS, 2 * LANES), F32)
    for p, piece in enumerate(half_pieces(powers, vectors)):
        out = jnp.where(row == p, piece, out)
    ref[classes:, : 2 * LANES] = out
    ref[classes:, 2 * LANES :] = jnp.zeros((SCALARS, wide - 2 * LANES), F32)


def unpack_halves(ref):
    classes = ref.shape[0] - SCALARS
    return ref[:classes] * column(jnp.exp2(ref[classes : classes + 1, : 2 * LANES]), classes)


def unpack_vector(ref):
    classes = ref.shape[0] - SCALARS
    power, high, low = (ref[classes + p : classes + p + 1, : 2 * LANES] for p in range(1, 4))
    return jnp.exp2(power) * (high + low / 2048.0)


def join_kernel(own_ref, row_ref, got_ref, one_ref, two_ref):
    classes, wide = own_ref.shape[0], one_ref.shape[1]
    for k, ref in enumerate((one_ref, two_ref)):
        here = slice(k * wide, (k + 1) * wide)
        vectors = [row_ref[:1] + got_ref[classes : classes + 1, : 2 * LANES]] if k == 0 else []
        pack_halves(ref, own_ref[:, here] + got_ref[:classes, here], vectors)


def join(own, row, got):
    half = shape((own.shape[0] + SCALARS, own.shape[1] // 2), F32)
    return call(join_kernel, "join", [half, half], 1 << 20, arrays=3)(own, row, got)


def add_kernel(own_ref, got_ref, sum_ref):
    vector = unpack_vector(own_ref) + unpack_vector(got_ref)
    pack_halves(sum_ref, unpack_halves(own_ref) + unpack_halves(got_ref), [vector])


def add_halves(own, got):
    return call(add_kernel, "add", shape(own.shape, F32), 1 << 20, arrays=2)(own, got)


def gradient_kernel(base_ref, label_ref, weight_ref, hessian_ref, send_ref):
    classes, share = base_ref.shape
    base = base_ref[...]
    probability = jax.nn.sigmoid(base)
    row = lax.broadcasted_iota(jnp.int32, (classes, share), 0)
    target = jnp.where(row == label_ref[...], 1.0, 0.0)
    hessian_ref[...] = weight_ref[...] * probability * (1.0 - probability)
    gradient = (weight_ref[...] * (probability - target)).astype(BF16)
    for k in range(send_ref.shape[0]):
        send_ref[k] = gradient


def gradient(base, label, weight, shares):
    return call(
        gradient_kernel,
        "gradient",
        [shape(base.shape, F32), shape((shares,) + base.shape, BF16)],
        1 << 20,
        arrays=3,
    )(base, label, weight)


def residual_kernel(
    total, one_ref, one_in_ref, two_ref, two_in_ref, high_ref, low_ref, high_turned_ref,
    low_turned_ref, residual_ref, lifted_ref,
):
    one = unpack_halves(one_ref) + unpack_halves(one_in_ref)
    two = unpack_halves(two_ref) + unpack_halves(two_in_ref)
    sums = jnp.concatenate([one, two], axis=1)
    residual = block_products(sums, high_ref, low_ref) * (-1.0 / total)
    residual_ref[...] = residual
    lifted = block_products(residual, high_turned_ref, low_turned_ref).astype(BF16)
    zero = jnp.zeros((1, 2 * LANES), F32)
    sizes = lane_sums(jnp.abs(lifted.astype(F32)))
    put_lifted(lifted_ref, lifted, [lane_sums(residual * residual), zero, sizes])


def first_residual(total, sums, blocks):
    classes, wide = sums[2].shape[0] - SCALARS, sums[2].shape[1]
    return call(
        functools.partial(residual_kernel, total),
        "residual",
        [
            shape((classes, 2 * wide), F32),
            shape((classes + EXTRA, 2 * wide), BF16),
        ],
        450 << 20,
        arrays=8,
    )(*sums, *blocks)


def weigh_kernel(parts_ref, hessian_ref, image_ref, norm_ref, send_ref):
    classes = hessian_ref.shape[0]
    image = sum_scaled(parts_ref, classes)
    image_ref[...] = image
    norm_ref[...] = stack_rows([half_vector(parts_ref, classes, 0)])
    weighted = (hessian_ref[...] * image).astype(BF16)
    extra = rows_of([lane_sums(weighted.astype(F32) * image)])
    for k in range(send_ref.shape[0]):
        send_ref[k, :classes] = weighted
        send_ref[k, classes:] = extra


def weigh(parts, hessian):
    return call(
        weigh_kernel,
        "weigh",
        [
            shape(hessian.shape, F32),
            shape((8, 2 * LANES), F32),
            shape((parts.shape[0], hessian.shape[0] + EXTRA, hessian.shape[1]), BF16),
        ],
        1 << 20,
        arrays=2,
    )(parts, hessian)


def step_kernel(
    total, one_ref, one_in_ref, two_ref, two_in_ref, high_ref, low_ref, high_turned_ref,
    low_turned_ref, residual_ref, norm_ref, lifted_ref, rough_ref,
):
    classes = residual_ref.shape[0]
    one = unpack_halves(one_ref) + unpack_halves(one_in_ref)
    two = unpack_halves(two_ref) + unpack_halves(two_in_ref)
    curve = (unpack_vector(one_ref) + unpack_vector(one_in_ref)) / total
    norm = norm_ref[:1]
    lane = lax.broadcasted_iota(jnp.int32, (1, 2 * LANES), 1)
    rough = jnp.where(lane < classes, norm / (curve + RIDGE * norm), 0.0)
    rough_ref[...] = stack_rows([rough])
    sums = jnp.concatenate([one, two], axis=1)
    old = residual_ref[...]
    image = block_products(sums, high_ref, low_ref) / total + RIDGE * old
    new = old - column(rough, classes) * image
    lifted = block_products(new, high_turned_ref, low_turned_ref).astype(BF16)
    sizes = lane_sums(jnp.abs(lifted.astype(F32)))
    put_lifted(lifted_ref, lifted, [lane_sums(old * new), lane_sums(new * new), sizes])


def step(total, sums, blocks, residual, norm):
    classes, half = residual.shape
    return call(
        functools.partial(step_kernel, total),
        "step",
        [shape((classes + EXTRA, half), BF16), shape((8, 2 * LANES), F32)],
        450 << 20,
        arrays=10,
    )(*sums, *blocks, residual, norm)


def curve_kernel(
    parts_ref, hessian_ref, image_ref, norm_ref, rough_ref, last_ref, scales_ref, curve_ref
):
    classes = hessian_ref.shape[0]
    last = sum_scaled(parts_ref, classes)
    last_ref[...] = last
    cross = half_vector(parts_ref, classes, 0)
    norm_rough = half_vector(parts_ref, classes, 1)
    norm = norm_ref[:1]
    lane = lax.broadcasted_iota(jnp.int32, (1, 2 * LANES), 1)
    excess = jnp.where(lane < classes, cross / (norm - cross), 0.0)
    grown = 1.0 + excess
    norm_next = grown * (grown * norm_rough - 2.0 * excess * cross) + excess * excess * norm
    ratio = jnp.where(lane < classes, norm_next / norm, 0.0)
    ridge = RIDGE * (norm_next + ratio * ratio * norm)
    scales_ref[...] = stack_rows(
        [rough_ref[:1] * grown, grown, ratio - excess, norm_next, ridge]
    )
    rows = column(grown, classes) * last + column(ratio - excess, classes) * image_ref[...]
    weighted = (hessian_ref[...] * rows).astype(BF16).astype(F32)
    curve_ref[...] = lane_sums(weighted * rows)


def last_curve(parts, hessian, image, norm, rough):
    row = shape((8, 2 * LANES), F32)
    return call(
        curve_kernel,
        "curve",
        [shape(hessian.shape, F32), row, shape((1, 2 * LANES), F32)],
        1 << 20,
        arrays=5,
    )(parts, hessian, image, norm, rough)


def margins_kernel(total, curve_ref, scales_ref, base_ref, image_ref, last_ref, margins_ref):
    classes = base_ref.shape[0]
    curve = jnp.sum(curve_ref[:, 0], axis=0, keepdims=True)
    first, grown, other = scales_ref[0:1], scales_ref[1:2], scales_ref[2:3]
    lane = lax.broadcasted_iota(jnp.int32, (1, 2 * LANES), 1)
    second = jnp.where(
        lane < classes, scales_ref[3:4] / (curve / total + scales_ref[4:5]), 0.0
    )
    margins_ref[...] = (
        base_ref[...]
        + column(first + second * other, classes) * image_ref[...]
        + column(second * grown, classes) * last_ref[...]
    )


def margins(total, curve, scales, base, image, last):
    return call(
        functools.partial(margins_kernel, total), "margins", shape(base.shape, F32), 1 << 20, arrays=5
    )(curve, scales, base, image, last)


def shards(pool, indices, labels, example_weight, centers, alpha, precond):
    n_ex, n_ctr = lax.axis_size("ex"), lax.axis_size("ctr")
    classes, count = alpha.shape
    examples = indices.shape[0]
    share = examples // n_ctr
    total = float(examples * n_ex)
    core = (lax.axis_index("ex") % 2).reshape(1)
    core_pairs = [(i, i ^ 1) for i in range(n_ex)]

    def over_y(array, flip):
        pairs = [(2 * y + c, 2 * (y ^ flip) + c) for y in range(n_ex // 2) for c in range(2)]
        return lax.ppermute(array, "ex", pairs)

    def over_cores(array):
        return lax.ppermute(array, "ex", core_pairs)

    def trade(parts):
        return lax.all_to_all(parts, "ctr", 0, 0)

    def trade_halves(parts):
        return trade(parts.astype(F16)).astype(F32)

    def swap(array, flip):
        array = lax.reduce_precision(array, 5, 10)
        return array, over_y(array.astype(F16), flip).astype(F32)

    def sum_examples(own, row, got):
        one, two = join(own, row, got)
        one, two = swap(one, 1), swap(two, 3)
        one, two = add_halves(*one), add_halves(*two)
        return *swap(one, 3), *swap(two, 1)

    offset = lax.axis_index("ctr") * share
    label = lax.dynamic_slice_in_dim(labels, offset, share, 0).reshape(1, share)
    weight = lax.dynamic_slice_in_dim(example_weight, offset, share, 0).reshape(1, share)
    index = indices.reshape(1, examples)
    sides, one_hot, chunk = prepare(index, centers, pool.shape[1])
    row_pool = trade(copies(pool, n_ctr))
    row_pool, sides, one_hot, chunk, label, weight, core = lax.optimization_barrier(
        (row_pool, sides, one_hot, chunk, label, weight, core)
    )
    tile, turned, rows = make_tile(chunk, row_pool, one_hot, sides, alpha, share)
    base = jnp.sum(trade_halves(rows), axis=0)
    hessian, send = gradient(base, label, weight, n_ctr)

    other, flat, row = backward_other(core, trade(send), turned, classes)
    got = over_cores(other)
    own = backward_own(core, flat, turned)
    got, late_core = lax.optimization_barrier((got, core))
    blocks = factors(late_core, precond)
    sums = sum_examples(own, row, got)
    residual, lifted = first_residual(total, sums, blocks)
    rows = forward(core, lifted, over_cores(lifted), tile, share)
    image, norm, send = weigh(trade_halves(rows), hessian)

    other, flat, row = backward_other(core, trade(send), turned, classes)
    got = over_cores(other)
    sums = sum_examples(backward_own(core, flat, turned), row, got)
    lifted, rough = step(total, sums, blocks, residual, norm)
    rows = forward(core, lifted, over_cores(lifted), tile, share)
    last, scales, curve = last_curve(trade_halves(rows), hessian, image, norm, rough)

    curve = jnp.broadcast_to(curve, (n_ex * n_ctr,) + curve.shape)
    curve = lax.all_to_all(curve, ("ex", "ctr"), 0, 0)
    return margins(total, curve, scales, base, image, last)


def solution(mesh):
    return jax.shard_map(
        shards,
        mesh=mesh,
        in_specs=(
            P(None, ("ex", "ctr")),
            P("ex"),
            P("ex"),
            P("ex"),
            P(None, "ctr"),
            P(None, "ctr"),
            P("ctr", None),
        ),
        out_specs=P(None, ("ex", "ctr")),
        check_vma=False,
    )
```

```python
import functools
import math

import jax
import jax.numpy as jnp
from jax import lax
from jax.experimental import pallas as pl
from jax.experimental.pallas import tpu as pltpu
from jax.sharding import PartitionSpec as P

RIDGE = 0.0001
F32 = jnp.float32
F16 = jnp.float16
BF16 = jnp.bfloat16
VMEM_BYTES = 24 * 1024 * 1024
DEPTH = 128
BAND = 256
EXTRA = 16
SCALARS = 8
LANES = 128
NT = (((1,), (1,)), ((), ()))
TN = (((0,), (0,)), ((), ()))


def split3(values):
    high = values.astype(BF16)
    rest = values - high.astype(F32)
    middle = rest.astype(BF16)
    low = (rest - middle.astype(F32)).astype(BF16)
    return high, middle, low


SCALAR = pl.BlockSpec(memory_space=pltpu.SMEM)
WHOLE = pl.BlockSpec(memory_space=pltpu.VMEM)
ANYWHERE = pl.BlockSpec(memory_space=pl.ANY)


def call(kernel, name, out_shape, flops, scratch=(), scalars=0, anywhere=0, arrays=0):
    shapes = out_shape if isinstance(out_shape, list) else [out_shape]
    size = sum(math.prod(s.shape) * s.dtype.itemsize for s in shapes)
    return pl.pallas_call(
        kernel,
        out_shape=out_shape,
        scratch_shapes=list(scratch),
        in_specs=[SCALAR] * scalars + [ANYWHERE] * anywhere + [WHOLE] * arrays,
        compiler_params=pltpu.CompilerParams(vmem_limit_bytes=VMEM_BYTES),
        cost_estimate=pl.CostEstimate(flops=flops, bytes_accessed=size, transcendentals=0),
        name=name,
    )


def rows_of(vectors):
    row = lax.broadcasted_iota(jnp.int32, (EXTRA, LANES), 0)
    out = jnp.zeros((EXTRA, LANES), F32)
    for k, vector in enumerate(vectors):
        for p, piece in enumerate(split3(vector)):
            for q in range(2):
                value = piece.astype(F32)[:, q * LANES : (q + 1) * LANES]
                out = jnp.where(row == 6 * k + 2 * p + q, value, out)
    return out.astype(BF16)


def read_rows(summed, k):
    halves = [
        sum(summed[6 * k + 2 * p + q : 6 * k + 2 * p + q + 1] for p in range(3)) for q in range(2)
    ]
    return jnp.concatenate(halves, axis=1)


def exponents(bounds):
    return jnp.ceil(jnp.log2(jnp.maximum(bounds, 1e-30)))


def half_pieces(powers, vectors):
    pieces = [powers]
    for vector in vectors:
        power = exponents(jnp.abs(vector)) + 1.0
        scaled = vector * jnp.exp2(-power) * 2048.0
        high = jnp.floor(scaled + 0.5)
        pieces += [power, high / 2048.0, jnp.floor((scaled - high) * 2048.0 + 0.5) / 2048.0]
    return pieces


def half_rows(powers, vectors):
    row = lax.broadcasted_iota(jnp.int32, (SCALARS, LANES), 0)
    lane = lax.broadcasted_iota(jnp.int32, (SCALARS, LANES), 1)
    out = jnp.zeros((SCALARS, LANES), F32)
    for p, piece in enumerate(half_pieces(powers, vectors)):
        out = jnp.where(row == p, piece[:, :LANES], out)
        rest = piece[:, LANES : LANES + 16]
        rest = jnp.concatenate([rest] * (LANES // 16), axis=1)
        out = jnp.where((row == SCALARS - 1) & (lane // 16 == p), rest, out)
    return out


def half_row(parts_ref, first, p):
    rest = parts_ref[:, first + SCALARS - 1, :][:, 16 * p : 16 * p + 16]
    empty = jnp.zeros((parts_ref.shape[0], LANES - 16), F32)
    return jnp.concatenate([parts_ref[:, first + p, :], rest, empty], axis=1)


def half_vector(parts_ref, first, k):
    power, high, low = (half_row(parts_ref, first, 1 + 3 * k + p) for p in range(3))
    return jnp.sum(jnp.exp2(power) * (high + low / 2048.0), axis=0, keepdims=True)


def sum_scaled(parts_ref, classes):
    scales = jnp.exp2(half_row(parts_ref, classes, 0)).T
    total = parts_ref[0, :classes] * scales[:classes, :1]
    for k in range(1, parts_ref.shape[0]):
        total = total + parts_ref[k, :classes] * scales[:classes, k : k + 1]
    return total


def column(vector, classes):
    return jnp.broadcast_to(vector, (8, vector.shape[1])).T[:classes, :1]


def lane_sums(values):
    folded = sum(values[:, k : k + LANES] for k in range(0, values.shape[1], LANES))
    empty = jnp.zeros((2 * LANES - values.shape[0], LANES), F32)
    return jnp.sum(jnp.concatenate([folded, empty], axis=0).T, axis=0, keepdims=True)


def stack_rows(vectors):
    row = lax.broadcasted_iota(jnp.int32, (8, 2 * LANES), 0)
    out = jnp.zeros((8, 2 * LANES), F32)
    for k, vector in enumerate(vectors):
        out = jnp.where(row == k, vector, out)
    return out


def sum_parts(ref):
    total = ref[0].astype(F32)
    for k in range(1, ref.shape[0]):
        total = total + ref[k].astype(F32)
    return total


def shape(dims, dtype):
    return jax.ShapeDtypeStruct(dims, dtype)


def tail(squares, first, pad):
    pieces = [p.astype(F32) for p in split3(-0.5 * squares)]
    row = lax.broadcasted_iota(jnp.int32, (pad, squares.shape[1]), 0)
    out = jnp.where((row >= 3 - first) & (row < 6 - first), 1.0, 0.0)
    for k in range(3):
        out = jnp.where(row == k + first, pieces[k], out)
    return out


def copies_kernel(block_ref, copies_ref):
    features, lanes = block_ref.shape
    for k in range(copies_ref.shape[0]):
        for q in range(lanes // LANES):
            copies_ref[k, q * features : (q + 1) * features] = block_ref[
                :, q * LANES : (q + 1) * LANES
            ]


def copies(block, number):
    out = shape((number, block.size // LANES, LANES), block.dtype)
    return call(copies_kernel, "copies", out, 1 << 20, arrays=1)(block)


def prepare_kernel(index_ref, centers_ref, sides_ref, one_hot_ref, chunk_ref):
    features, count = centers_ref.shape
    lanes = one_hot_ref.shape[0]
    center_float = centers_ref[...].astype(F32)
    center_sq = jnp.sum(center_float * center_float, axis=0, keepdims=True)
    side = jnp.concatenate([center_float, tail(center_sq, 3, DEPTH - features)], axis=0)
    sides_ref[...] = side.T.astype(BF16)
    chunk_ref[...] = index_ref[...] // lanes
    within = index_ref[...] % lanes
    row = lax.broadcasted_iota(jnp.int32, (lanes, index_ref.shape[1]), 0)
    one_hot_ref[...] = (row == within).astype(F32).astype(BF16)


def prepare(index, centers, lanes):
    features, count = centers.shape
    examples = index.shape[1]
    return call(
        prepare_kernel,
        "prepare",
        [shape((count, DEPTH), BF16), shape((lanes, examples), BF16), shape(index.shape, jnp.int32)],
        1 << 20,
        arrays=2,
    )(index, centers)


def tile_kernel(
    alpha_hbm, chunk_ref, pool_ref, one_hot_ref, sides_ref, tile_ref, turned_ref, rows_ref,
    side_ref, base_ref, alpha_ref, alpha_sem,
):
    fetch = pltpu.make_async_copy(alpha_hbm, alpha_ref, alpha_sem)
    fetch.start()
    chunks, height, _ = pool_ref.shape
    lanes = one_hot_ref.shape[0]
    features = height * LANES // lanes
    count, examples = tile_ref.shape
    share = rows_ref.shape[2]
    scale = 4.0 / features * math.log2(math.e)
    pool = jnp.concatenate(
        [
            pool_ref[:, q * features : (q + 1) * features, :].reshape(chunks * features, LANES)
            for q in range(lanes // LANES)
        ],
        axis=1,
    )
    for b in range(examples // BAND):
        here = slice(b * BAND, (b + 1) * BAND)
        chunk = chunk_ref[:, here]
        picked = jnp.dot(pool, one_hot_ref[:, here], preferred_element_type=F32)
        points = jnp.where(chunk == 0, picked[:features], 0.0)
        for k in range(1, chunks):
            points = jnp.where(chunk == k, picked[k * features : (k + 1) * features], points)
        point_sq = jnp.sum(points * points, axis=0, keepdims=True)
        side = jnp.concatenate([points, tail(point_sq, 0, DEPTH - features)], axis=0)
        side_ref[:, here] = side.astype(BF16)
    fetch.wait()
    for b in range(count // BAND):
        here = slice(b * BAND, (b + 1) * BAND)
        near = jnp.dot(sides_ref[here, :], side_ref[...], preferred_element_type=F32)
        values = jnp.exp2(near * scale).astype(BF16)
        tile_ref[here, :] = values
        turned_ref[:, here] = values.T
        rows = jnp.dot(alpha_ref[:, here], values, preferred_element_type=F32)
        base_ref[...] = rows if b == 0 else base_ref[...] + rows
    for k in range(examples // share):
        rows_ref[k] = base_ref[:, k * share : (k + 1) * share]


def make_tile(chunk, row_pool, one_hot, sides, alpha, share):
    examples, count = chunk.shape[1], sides.shape[0]
    classes = alpha.shape[0]
    return call(
        tile_kernel,
        "tile",
        [
            shape((count, examples), BF16),
            shape((examples, count), BF16),
            shape((examples // share, classes, share), F32),
        ],
        4 << 30,
        [
            pltpu.VMEM((DEPTH, examples), BF16),
            pltpu.VMEM((classes, examples), F32),
            pltpu.VMEM(alpha.shape, BF16),
            pltpu.SemaphoreType.DMA,
        ],
        anywhere=1,
        arrays=4,
    )(alpha, chunk, row_pool, one_hot, sides)


def factors_kernel(core_ref, precond_ref, high_ref, low_ref, high_turned_ref, low_turned_ref):
    order = precond_ref.shape[1]
    half = high_ref.shape[0]
    first = core_ref[0] * half
    for k in range(half // order):
        here = slice(k * order, (k + 1) * order)
        block = precond_ref[pl.ds(pl.multiple_of(first + k * order, order), order), :]
        high = block.astype(BF16)
        high_ref[here] = high
        low_ref[here] = (block - high.astype(F32)).astype(BF16)
        turned = block.T
        high = turned.astype(BF16)
        high_turned_ref[here] = high
        low_turned_ref[here] = (turned - high.astype(F32)).astype(BF16)


def factors(core, precond):
    out = shape((precond.shape[0] // 2, precond.shape[1]), BF16)
    return call(factors_kernel, "factors", [out] * 4, 1 << 20, scalars=1, arrays=1)(core, precond)


def block_products(values, high_ref, low_ref):
    order = high_ref.shape[1]
    out = []
    for k in range(high_ref.shape[0] // order):
        here = slice(k * order, (k + 1) * order)
        block = values[:, here]
        high = block.astype(BF16)
        low = (block - high.astype(F32)).astype(BF16)
        product = jnp.dot(high, high_ref[here], preferred_element_type=F32)
        product += jnp.dot(high, low_ref[here], preferred_element_type=F32)
        product += jnp.dot(low, high_ref[here], preferred_element_type=F32)
        out.append(product)
    return jnp.concatenate(out, axis=1)


def put_lifted(ref, lifted, vectors):
    classes, half = lifted.shape
    ref[:classes] = lifted
    row = lax.broadcasted_iota(jnp.int32, (EXTRA, 2 * LANES), 0)
    out = jnp.zeros((EXTRA, 2 * LANES), F32)
    for k, vector in enumerate(vectors):
        for p, piece in enumerate(split3(vector)):
            out = jnp.where(row == 3 * k + p, piece.astype(F32), out)
    ref[classes:, : 2 * LANES] = out.astype(BF16)
    ref[classes:, 2 * LANES :] = jnp.zeros((EXTRA, half - 2 * LANES), BF16)


def forward_own_kernel(core_ref, own_ref, tile_ref, first_ref):
    classes, half = first_ref.shape[0], own_ref.shape[1]
    mine = pl.ds(pl.multiple_of(core_ref[0] * half, half), half)
    for b in range(first_ref.shape[1] // BAND):
        here = slice(b * BAND, (b + 1) * BAND)
        first_ref[:, here] = jnp.dot(
            own_ref[:classes], tile_ref[mine, here], preferred_element_type=F32
        )


def forward_kernel(core_ref, first_ref, own_ref, other_ref, tile_ref, rows_ref):
    classes, half = first_ref.shape[0], other_ref.shape[1]
    share = rows_ref.shape[2]
    examples = tile_ref.shape[1]
    theirs = pl.ds(pl.multiple_of((1 - core_ref[0]) * half, half), half)
    part = [ref[classes:, : 2 * LANES].astype(F32) for ref in (own_ref, other_ref)]
    part = part[0] + part[1]
    part = [part[3 * k : 3 * k + 1] + part[3 * k + 1 : 3 * k + 2] + part[3 * k + 2 : 3 * k + 3] for k in range(3)]
    powers = exponents(part[2]) - 14.0
    extra = half_rows(powers, part[:2])
    scales = column(jnp.exp2(-powers), classes)
    for b in range(examples // BAND):
        here = slice(b * BAND, (b + 1) * BAND)
        rows = jnp.dot(other_ref[:classes], tile_ref[theirs, here], preferred_element_type=F32)
        rows = (rows + first_ref[:, here]) * scales
        for k in range(BAND // share):
            at = b * (BAND // share) + k
            rows_ref[at, :classes] = rows[:, k * share : (k + 1) * share]
            rows_ref[at, classes:] = extra


def forward(core, lifted, other, tile, share):
    classes = lifted.shape[0] - EXTRA
    examples = tile.shape[1]
    first = call(
        forward_own_kernel,
        "forward_own",
        shape((classes, examples), F32),
        604 << 20,
        scalars=1,
        arrays=2,
    )(core, lifted, tile)
    return call(
        forward_kernel,
        "forward",
        shape((examples // share, classes + SCALARS, share), F32),
        604 << 20,
        scalars=1,
        arrays=4,
    )(core, first, lifted, other, tile)


def backward_other_kernel(
    core_ref, values_ref, turned_ref, first_ref, second_ref, flat_ref, row_ref
):
    shares, height, share = values_ref.shape
    classes, examples = flat_ref.shape
    wide = first_ref.shape[1]
    for k in range(shares):
        flat_ref[:, k * share : (k + 1) * share] = values_ref[k, :classes]
    row = jnp.zeros((8, 2 * LANES), F32)
    if height > classes:
        total = values_ref[0, classes:].astype(F32)
        for k in range(1, shares):
            total = total + values_ref[k, classes:].astype(F32)
        row = jnp.broadcast_to(read_rows(total, 0), (8, 2 * LANES))
    row_ref[...] = row
    first_ref[classes:, : 2 * LANES] = row
    first_ref[classes:, 2 * LANES :] = jnp.zeros((8, wide - 2 * LANES), F32)
    for k, ref in enumerate((first_ref, second_ref)):
        for b in range(wide // BAND):
            there = (1 - core_ref[0]) * (2 * wide) + k * wide + b * BAND
            ref[:classes, b * BAND : (b + 1) * BAND] = jnp.dot(
                flat_ref[...],
                turned_ref[:, pl.ds(pl.multiple_of(there, BAND), BAND)],
                preferred_element_type=F32,
            )


def backward_own_kernel(core_ref, flat_ref, turned_ref, own_ref):
    half = own_ref.shape[1]
    for b in range(half // BAND):
        there = pl.ds(pl.multiple_of(core_ref[0] * half + b * BAND, BAND), BAND)
        own_ref[:, b * BAND : (b + 1) * BAND] = jnp.dot(
            flat_ref[...], turned_ref[:, there], preferred_element_type=F32
        )


def backward_other(core, values, turned, classes):
    examples, count = turned.shape
    return call(
        backward_other_kernel,
        "backward_other",
        [
            shape((classes + SCALARS, count // 4), F32),
            shape((classes, count // 4), F32),
            shape((classes, examples), BF16),
            shape((8, 2 * LANES), F32),
        ],
        604 << 20,
        scalars=1,
        arrays=2,
    )(core, values, turned)


def backward_own(core, flat, turned):
    return call(
        backward_own_kernel,
        "backward_own",
        shape((flat.shape[0], turned.shape[1] // 2), F32),
        604 << 20,
        scalars=1,
        arrays=2,
    )(core, flat, turned)


def pack_halves(ref, values, vectors):
    classes, wide = values.shape
    size = jnp.max(jnp.abs(values), axis=1, keepdims=True)
    powers = exponents(size) - 14.0
    ref[:classes] = values * jnp.exp2(-powers)
    empty = jnp.zeros((2 * LANES - classes, LANES), F32)
    powers = jnp.concatenate([jnp.broadcast_to(powers, (classes, LANES)), empty], axis=0).T[:1]
    row = lax.broadcasted_iota(jnp.int32, (SCALARS, 2 * LANES), 0)
    out = jnp.zeros((SCALARS, 2 * LANES), F32)
    for p, piece in enumerate(half_pieces(powers, vectors)):
        out = jnp.where(row == p, piece, out)
    ref[classes:, : 2 * LANES] = out
    ref[classes:, 2 * LANES :] = jnp.zeros((SCALARS, wide - 2 * LANES), F32)


def unpack_halves(ref):
    classes = ref.shape[0] - SCALARS
    return ref[:classes] * column(jnp.exp2(ref[classes : classes + 1, : 2 * LANES]), classes)


def unpack_vector(ref):
    classes = ref.shape[0] - SCALARS
    power, high, low = (ref[classes + p : classes + p + 1, : 2 * LANES] for p in range(1, 4))
    return jnp.exp2(power) * (high + low / 2048.0)


def join_first_kernel(own_ref, row_ref, got_ref, sum_ref):
    classes, wide = own_ref.shape[0], sum_ref.shape[1]
    vector = row_ref[:1] + got_ref[classes : classes + 1, : 2 * LANES]
    pack_halves(sum_ref, own_ref[:, :wide] + got_ref[:classes], [vector])


def join_second_kernel(own_ref, got_ref, sum_ref):
    pack_halves(sum_ref, own_ref[:, sum_ref.shape[1] :] + got_ref[...], [])


def join(own, row, first, second):
    half = shape((own.shape[0] + SCALARS, own.shape[1] // 2), F32)
    return (
        call(join_first_kernel, "join_first", half, 1 << 20, arrays=3)(own, row, first),
        call(join_second_kernel, "join_second", half, 1 << 20, arrays=2)(own, second),
    )


def add_kernel(own_ref, got_ref, sum_ref):
    vector = unpack_vector(own_ref) + unpack_vector(got_ref)
    pack_halves(sum_ref, unpack_halves(own_ref) + unpack_halves(got_ref), [vector])


def add_halves(own, got):
    return call(add_kernel, "add", shape(own.shape, F32), 1 << 20, arrays=2)(own, got)


def gradient_kernel(base_ref, label_ref, weight_ref, hessian_ref, send_ref):
    classes, share = base_ref.shape
    base = base_ref[...]
    probability = jax.nn.sigmoid(base)
    row = lax.broadcasted_iota(jnp.int32, (classes, share), 0)
    target = jnp.where(row == label_ref[...], 1.0, 0.0)
    hessian_ref[...] = weight_ref[...] * probability * (1.0 - probability)
    gradient = (weight_ref[...] * (probability - target)).astype(BF16)
    for k in range(send_ref.shape[0]):
        send_ref[k] = gradient


def gradient(base, label, weight, shares):
    return call(
        gradient_kernel,
        "gradient",
        [shape(base.shape, F32), shape((shares,) + base.shape, BF16)],
        1 << 20,
        arrays=3,
    )(base, label, weight)


def residual_kernel(
    total, one_ref, one_in_ref, two_ref, two_in_ref, high_ref, low_ref, high_turned_ref,
    low_turned_ref, residual_ref, lifted_ref,
):
    one = unpack_halves(one_ref) + unpack_halves(one_in_ref)
    two = unpack_halves(two_ref) + unpack_halves(two_in_ref)
    sums = jnp.concatenate([one, two], axis=1)
    residual = block_products(sums, high_ref, low_ref) * (-1.0 / total)
    residual_ref[...] = residual
    lifted = block_products(residual, high_turned_ref, low_turned_ref).astype(BF16)
    zero = jnp.zeros((1, 2 * LANES), F32)
    sizes = lane_sums(jnp.abs(lifted.astype(F32)))
    put_lifted(lifted_ref, lifted, [lane_sums(residual * residual), zero, sizes])


def first_residual(total, sums, blocks):
    classes, wide = sums[2].shape[0] - SCALARS, sums[2].shape[1]
    return call(
        functools.partial(residual_kernel, total),
        "residual",
        [
            shape((classes, 2 * wide), F32),
            shape((classes + EXTRA, 2 * wide), BF16),
        ],
        450 << 20,
        arrays=8,
    )(*sums, *blocks)


def weigh_kernel(parts_ref, hessian_ref, image_ref, norm_ref, send_ref):
    classes = hessian_ref.shape[0]
    image = sum_scaled(parts_ref, classes)
    image_ref[...] = image
    norm_ref[...] = stack_rows([half_vector(parts_ref, classes, 0)])
    weighted = (hessian_ref[...] * image).astype(BF16)
    extra = rows_of([lane_sums(weighted.astype(F32) * image)])
    for k in range(send_ref.shape[0]):
        send_ref[k, :classes] = weighted
        send_ref[k, classes:] = extra


def weigh(parts, hessian):
    return call(
        weigh_kernel,
        "weigh",
        [
            shape(hessian.shape, F32),
            shape((8, 2 * LANES), F32),
            shape((parts.shape[0], hessian.shape[0] + EXTRA, hessian.shape[1]), BF16),
        ],
        1 << 20,
        arrays=2,
    )(parts, hessian)


def step_kernel(
    total, one_ref, one_in_ref, two_ref, two_in_ref, high_ref, low_ref, high_turned_ref,
    low_turned_ref, residual_ref, norm_ref, lifted_ref, rough_ref,
):
    classes = residual_ref.shape[0]
    one = unpack_halves(one_ref) + unpack_halves(one_in_ref)
    two = unpack_halves(two_ref) + unpack_halves(two_in_ref)
    curve = (unpack_vector(one_ref) + unpack_vector(one_in_ref)) / total
    norm = norm_ref[:1]
    lane = lax.broadcasted_iota(jnp.int32, (1, 2 * LANES), 1)
    rough = jnp.where(lane < classes, norm / (curve + RIDGE * norm), 0.0)
    rough_ref[...] = stack_rows([rough])
    sums = jnp.concatenate([one, two], axis=1)
    old = residual_ref[...]
    image = block_products(sums, high_ref, low_ref) / total + RIDGE * old
    new = old - column(rough, classes) * image
    lifted = block_products(new, high_turned_ref, low_turned_ref).astype(BF16)
    sizes = lane_sums(jnp.abs(lifted.astype(F32)))
    put_lifted(lifted_ref, lifted, [lane_sums(old * new), lane_sums(new * new), sizes])


def step(total, sums, blocks, residual, norm):
    classes, half = residual.shape
    return call(
        functools.partial(step_kernel, total),
        "step",
        [shape((classes + EXTRA, half), BF16), shape((8, 2 * LANES), F32)],
        450 << 20,
        arrays=10,
    )(*sums, *blocks, residual, norm)


def curve_kernel(
    parts_ref, hessian_ref, image_ref, norm_ref, rough_ref, last_ref, scales_ref, curve_ref
):
    classes = hessian_ref.shape[0]
    last = sum_scaled(parts_ref, classes)
    last_ref[...] = last
    cross = half_vector(parts_ref, classes, 0)
    norm_rough = half_vector(parts_ref, classes, 1)
    norm = norm_ref[:1]
    lane = lax.broadcasted_iota(jnp.int32, (1, 2 * LANES), 1)
    excess = jnp.where(lane < classes, cross / (norm - cross), 0.0)
    grown = 1.0 + excess
    norm_next = grown * (grown * norm_rough - 2.0 * excess * cross) + excess * excess * norm
    ratio = jnp.where(lane < classes, norm_next / norm, 0.0)
    ridge = RIDGE * (norm_next + ratio * ratio * norm)
    scales_ref[...] = stack_rows(
        [rough_ref[:1] * grown, grown, ratio - excess, norm_next, ridge]
    )
    rows = column(grown, classes) * last + column(ratio - excess, classes) * image_ref[...]
    weighted = (hessian_ref[...] * rows).astype(BF16).astype(F32)
    curve_ref[...] = lane_sums(weighted * rows)


def last_curve(parts, hessian, image, norm, rough):
    row = shape((8, 2 * LANES), F32)
    return call(
        curve_kernel,
        "curve",
        [shape(hessian.shape, F32), row, shape((1, 2 * LANES), F32)],
        1 << 20,
        arrays=5,
    )(parts, hessian, image, norm, rough)


def margins_kernel(total, curve_ref, scales_ref, base_ref, image_ref, last_ref, margins_ref):
    classes = base_ref.shape[0]
    curve = jnp.sum(curve_ref[:, 0], axis=0, keepdims=True)
    first, grown, other = scales_ref[0:1], scales_ref[1:2], scales_ref[2:3]
    lane = lax.broadcasted_iota(jnp.int32, (1, 2 * LANES), 1)
    second = jnp.where(
        lane < classes, scales_ref[3:4] / (curve / total + scales_ref[4:5]), 0.0
    )
    margins_ref[...] = (
        base_ref[...]
        + column(first + second * other, classes) * image_ref[...]
        + column(second * grown, classes) * last_ref[...]
    )


def margins(total, curve, scales, base, image, last):
    return call(
        functools.partial(margins_kernel, total), "margins", shape(base.shape, F32), 1 << 20, arrays=5
    )(curve, scales, base, image, last)


def shards(pool, indices, labels, example_weight, centers, alpha, precond):
    n_ex, n_ctr = lax.axis_size("ex"), lax.axis_size("ctr")
    classes, count = alpha.shape
    examples = indices.shape[0]
    share = examples // n_ctr
    total = float(examples * n_ex)
    core = (lax.axis_index("ex") % 2).reshape(1)
    core_pairs = [(i, i ^ 1) for i in range(n_ex)]

    def over_y(array, flip):
        pairs = [(2 * y + c, 2 * (y ^ flip) + c) for y in range(n_ex // 2) for c in range(2)]
        return lax.ppermute(array, "ex", pairs)

    def over_cores(array):
        return lax.ppermute(array, "ex", core_pairs)

    def trade(parts):
        return lax.all_to_all(parts, "ctr", 0, 0)

    def trade_halves(parts):
        return trade(parts.astype(F16)).astype(F32)

    def swap(array, flip):
        array = lax.reduce_precision(array, 5, 10)
        return array, over_y(array.astype(F16), flip).astype(F32)

    def sum_examples(send):
        first, second, flat, row = backward_other(core, trade(send), turned, classes)
        got = over_cores(first), over_cores(second)
        one, two = join(backward_own(core, flat, turned), row, *got)
        one, two = swap(one, 3), swap(two, 1)
        one, two = add_halves(*one), add_halves(*two)
        return (*swap(one, 1), *swap(two, 3)), got[0]

    offset = lax.axis_index("ctr") * share
    label = lax.dynamic_slice_in_dim(labels, offset, share, 0).reshape(1, share)
    weight = lax.dynamic_slice_in_dim(example_weight, offset, share, 0).reshape(1, share)
    index = indices.reshape(1, examples)
    sides, one_hot, chunk = prepare(index, centers, pool.shape[1])
    row_pool = trade(copies(pool, n_ctr))
    row_pool, sides, one_hot, chunk, label, weight, core = lax.optimization_barrier(
        (row_pool, sides, one_hot, chunk, label, weight, core)
    )
    tile, turned, rows = make_tile(chunk, row_pool, one_hot, sides, alpha, share)
    base = jnp.sum(trade_halves(rows), axis=0)
    hessian, send = gradient(base, label, weight, n_ctr)

    sums, got = sum_examples(send)
    got, late_core = lax.optimization_barrier((got, core))
    blocks = factors(late_core, precond)
    residual, lifted = first_residual(total, sums, blocks)
    rows = forward(core, lifted, over_cores(lifted), tile, share)
    image, norm, send = weigh(trade_halves(rows), hessian)

    sums, _ = sum_examples(send)
    lifted, rough = step(total, sums, blocks, residual, norm)
    rows = forward(core, lifted, over_cores(lifted), tile, share)
    last, scales, curve = last_curve(trade_halves(rows), hessian, image, norm, rough)

    curve = jnp.broadcast_to(curve, (n_ex * n_ctr,) + curve.shape)
    curve = lax.all_to_all(curve, ("ex", "ctr"), 0, 0)
    return margins(total, curve, scales, base, image, last)


def solution(mesh):
    return jax.shard_map(
        shards,
        mesh=mesh,
        in_specs=(
            P(None, ("ex", "ctr")),
            P("ex"),
            P("ex"),
            P("ex"),
            P(None, "ctr"),
            P(None, "ctr"),
            P("ctr", None),
        ),
        out_specs=P(None, ("ex", "ctr")),
        check_vma=False,
    )
```

```python
import functools
import math

import jax
import jax.numpy as jnp
from jax import lax
from jax.experimental import pallas as pl
from jax.experimental.pallas import tpu as pltpu
from jax.sharding import PartitionSpec as P

RIDGE = 0.0001
F32 = jnp.float32
F16 = jnp.float16
BF16 = jnp.bfloat16
VMEM_BYTES = 24 * 1024 * 1024
DEPTH = 128
BAND = 256
EXTRA = 16
SCALARS = 8
LANES = 128
NT = (((1,), (1,)), ((), ()))
TN = (((0,), (0,)), ((), ()))


def split3(values):
    high = values.astype(BF16)
    rest = values - high.astype(F32)
    middle = rest.astype(BF16)
    low = (rest - middle.astype(F32)).astype(BF16)
    return high, middle, low


SCALAR = pl.BlockSpec(memory_space=pltpu.SMEM)
WHOLE = pl.BlockSpec(memory_space=pltpu.VMEM)
ANYWHERE = pl.BlockSpec(memory_space=pl.ANY)


def call(kernel, name, out_shape, flops, scratch=(), scalars=0, anywhere=0, arrays=0):
    shapes = out_shape if isinstance(out_shape, list) else [out_shape]
    size = sum(math.prod(s.shape) * s.dtype.itemsize for s in shapes)
    return pl.pallas_call(
        kernel,
        out_shape=out_shape,
        scratch_shapes=list(scratch),
        in_specs=[SCALAR] * scalars + [ANYWHERE] * anywhere + [WHOLE] * arrays,
        compiler_params=pltpu.CompilerParams(vmem_limit_bytes=VMEM_BYTES),
        cost_estimate=pl.CostEstimate(flops=flops, bytes_accessed=size, transcendentals=0),
        name=name,
    )


def rows_of(vectors):
    row = lax.broadcasted_iota(jnp.int32, (EXTRA, LANES), 0)
    out = jnp.zeros((EXTRA, LANES), F32)
    for k, vector in enumerate(vectors):
        for p, piece in enumerate(split3(vector)):
            for q in range(2):
                value = piece.astype(F32)[:, q * LANES : (q + 1) * LANES]
                out = jnp.where(row == 6 * k + 2 * p + q, value, out)
    return out.astype(BF16)


def read_rows(summed, k):
    halves = [
        sum(summed[6 * k + 2 * p + q : 6 * k + 2 * p + q + 1] for p in range(3)) for q in range(2)
    ]
    return jnp.concatenate(halves, axis=1)


def exponents(bounds):
    return jnp.ceil(jnp.log2(jnp.maximum(bounds, 1e-30)))


def half_pieces(powers, vectors):
    pieces = [powers]
    for vector in vectors:
        power = exponents(jnp.abs(vector)) + 1.0
        scaled = vector * jnp.exp2(-power) * 2048.0
        high = jnp.floor(scaled + 0.5)
        pieces += [power, high / 2048.0, jnp.floor((scaled - high) * 2048.0 + 0.5) / 2048.0]
    return pieces


def half_rows(powers, vectors):
    row = lax.broadcasted_iota(jnp.int32, (SCALARS, LANES), 0)
    lane = lax.broadcasted_iota(jnp.int32, (SCALARS, LANES), 1)
    out = jnp.zeros((SCALARS, LANES), F32)
    for p, piece in enumerate(half_pieces(powers, vectors)):
        out = jnp.where(row == p, piece[:, :LANES], out)
        rest = piece[:, LANES : LANES + 16]
        rest = jnp.concatenate([rest] * (LANES // 16), axis=1)
        out = jnp.where((row == SCALARS - 1) & (lane // 16 == p), rest, out)
    return out


def half_row(parts_ref, first, p):
    rest = parts_ref[:, first + SCALARS - 1, :][:, 16 * p : 16 * p + 16]
    empty = jnp.zeros((parts_ref.shape[0], LANES - 16), F32)
    return jnp.concatenate([parts_ref[:, first + p, :], rest, empty], axis=1)


def half_vector(parts_ref, first, k):
    power, high, low = (half_row(parts_ref, first, 1 + 3 * k + p) for p in range(3))
    return jnp.sum(jnp.exp2(power) * (high + low / 2048.0), axis=0, keepdims=True)


def sum_scaled(parts_ref, classes):
    scales = jnp.exp2(half_row(parts_ref, classes, 0)).T
    total = parts_ref[0, :classes] * scales[:classes, :1]
    for k in range(1, parts_ref.shape[0]):
        total = total + parts_ref[k, :classes] * scales[:classes, k : k + 1]
    return total


def columns(vectors, classes):
    turned = stack_rows(vectors).T
    return [turned[:classes, k : k + 1] for k in range(len(vectors))]


def column(vector, classes):
    return jnp.broadcast_to(vector, (8, vector.shape[1])).T[:classes, :1]


def lane_sums(values):
    folded = sum(values[:, k : k + LANES] for k in range(0, values.shape[1], LANES))
    empty = jnp.zeros((2 * LANES - values.shape[0], LANES), F32)
    return jnp.sum(jnp.concatenate([folded, empty], axis=0).T, axis=0, keepdims=True)


def stack_rows(vectors):
    row = lax.broadcasted_iota(jnp.int32, (8, 2 * LANES), 0)
    out = jnp.zeros((8, 2 * LANES), F32)
    for k, vector in enumerate(vectors):
        out = jnp.where(row == k, vector, out)
    return out


def shape(dims, dtype):
    return jax.ShapeDtypeStruct(dims, dtype)


def tail(squares, first, pad):
    pieces = [p.astype(F32) for p in split3(-0.5 * squares)]
    row = lax.broadcasted_iota(jnp.int32, (pad, squares.shape[1]), 0)
    out = jnp.where((row >= 3 - first) & (row < 6 - first), 1.0, 0.0)
    for k in range(3):
        out = jnp.where(row == k + first, pieces[k], out)
    return out


def copies_kernel(block_ref, copies_ref):
    features, lanes = block_ref.shape
    for k in range(copies_ref.shape[0]):
        for q in range(lanes // LANES):
            copies_ref[k, q * features : (q + 1) * features] = block_ref[
                :, q * LANES : (q + 1) * LANES
            ]


def copies(block, number):
    out = shape((number, block.size // LANES, LANES), block.dtype)
    return call(copies_kernel, "copies", out, 1 << 20, arrays=1)(block)


def prepare_kernel(index_ref, centers_ref, sides_ref, one_hot_ref, chunk_ref):
    features, count = centers_ref.shape
    lanes = one_hot_ref.shape[0]
    center_float = centers_ref[...].astype(F32)
    center_sq = jnp.sum(center_float * center_float, axis=0, keepdims=True)
    side = jnp.concatenate([center_float, tail(center_sq, 3, DEPTH - features)], axis=0)
    sides_ref[...] = side.T.astype(BF16)
    chunk_ref[...] = index_ref[...] // lanes
    within = index_ref[...] % lanes
    row = lax.broadcasted_iota(jnp.int32, (lanes, index_ref.shape[1]), 0)
    one_hot_ref[...] = (row == within).astype(F32).astype(BF16)


def prepare(index, centers, lanes):
    features, count = centers.shape
    examples = index.shape[1]
    return call(
        prepare_kernel,
        "prepare",
        [shape((count, DEPTH), BF16), shape((lanes, examples), BF16), shape(index.shape, jnp.int32)],
        1 << 20,
        arrays=2,
    )(index, centers)


def tile_kernel(
    alpha_hbm, chunk_ref, pool_ref, one_hot_ref, sides_ref, tile_ref, turned_ref, rows_ref,
    side_ref, base_ref, alpha_ref, alpha_sem,
):
    fetch = pltpu.make_async_copy(alpha_hbm, alpha_ref, alpha_sem)
    fetch.start()
    chunks, height, _ = pool_ref.shape
    lanes = one_hot_ref.shape[0]
    features = height * LANES // lanes
    count, examples = tile_ref.shape
    share = rows_ref.shape[2]
    scale = 4.0 / features * math.log2(math.e)
    pool = jnp.concatenate(
        [
            pool_ref[:, q * features : (q + 1) * features, :].reshape(chunks * features, LANES)
            for q in range(lanes // LANES)
        ],
        axis=1,
    )
    for b in range(examples // BAND):
        here = slice(b * BAND, (b + 1) * BAND)
        chunk = chunk_ref[:, here]
        picked = jnp.dot(pool, one_hot_ref[:, here], preferred_element_type=F32)
        points = jnp.where(chunk == 0, picked[:features], 0.0)
        for k in range(1, chunks):
            points = jnp.where(chunk == k, picked[k * features : (k + 1) * features], points)
        point_sq = jnp.sum(points * points, axis=0, keepdims=True)
        side = jnp.concatenate([points, tail(point_sq, 0, DEPTH - features)], axis=0)
        side_ref[:, here] = side.astype(BF16)
    fetch.wait()
    for b in range(count // BAND):
        here = slice(b * BAND, (b + 1) * BAND)
        near = jnp.dot(sides_ref[here, :], side_ref[...], preferred_element_type=F32)
        values = jnp.exp2(near * scale).astype(BF16)
        tile_ref[here, :] = values
        turned_ref[:, here] = values.T
        rows = jnp.dot(alpha_ref[:, here], values, preferred_element_type=F32)
        base_ref[...] = rows if b == 0 else base_ref[...] + rows
    for k in range(examples // share):
        rows_ref[k] = base_ref[:, k * share : (k + 1) * share]


def make_tile(chunk, row_pool, one_hot, sides, alpha, share):
    examples, count = chunk.shape[1], sides.shape[0]
    classes = alpha.shape[0]
    return call(
        tile_kernel,
        "tile",
        [
            shape((count, examples), BF16),
            shape((examples, count), BF16),
            shape((examples // share, classes, share), F32),
        ],
        4 << 30,
        [
            pltpu.VMEM((DEPTH, examples), BF16),
            pltpu.VMEM((classes, examples), F32),
            pltpu.VMEM(alpha.shape, BF16),
            pltpu.SemaphoreType.DMA,
        ],
        anywhere=1,
        arrays=4,
    )(alpha, chunk, row_pool, one_hot, sides)


def factors_kernel(core_ref, precond_ref, high_ref, low_ref, high_turned_ref, low_turned_ref):
    order = precond_ref.shape[1]
    half = high_ref.shape[0]
    first = core_ref[0] * half
    for k in range(half // order):
        here = slice(k * order, (k + 1) * order)
        block = precond_ref[pl.ds(pl.multiple_of(first + k * order, order), order), :]
        high = block.astype(BF16)
        high_ref[here] = high
        low_ref[here] = (block - high.astype(F32)).astype(BF16)
        turned = block.T
        high = turned.astype(BF16)
        high_turned_ref[here] = high
        low_turned_ref[here] = (turned - high.astype(F32)).astype(BF16)


def factors(core, precond):
    out = shape((precond.shape[0] // 2, precond.shape[1]), BF16)
    return call(factors_kernel, "factors", [out] * 4, 1 << 20, scalars=1, arrays=1)(core, precond)


def block_products(values, high_ref, low_ref):
    order = high_ref.shape[1]
    out = []
    for k in range(high_ref.shape[0] // order):
        here = slice(k * order, (k + 1) * order)
        block = values[:, here]
        high = block.astype(BF16)
        low = (block - high.astype(F32)).astype(BF16)
        product = jnp.dot(high, high_ref[here], preferred_element_type=F32)
        product += jnp.dot(high, low_ref[here], preferred_element_type=F32)
        product += jnp.dot(low, high_ref[here], preferred_element_type=F32)
        out.append(product)
    return jnp.concatenate(out, axis=1)


def put_lifted(ref, lifted, vectors):
    classes, half = lifted.shape
    ref[:classes] = lifted
    row = lax.broadcasted_iota(jnp.int32, (EXTRA, 2 * LANES), 0)
    out = jnp.zeros((EXTRA, 2 * LANES), F32)
    for k, vector in enumerate(vectors):
        for p, piece in enumerate(split3(vector)):
            out = jnp.where(row == 3 * k + p, piece.astype(F32), out)
    ref[classes:, : 2 * LANES] = out.astype(BF16)
    ref[classes:, 2 * LANES :] = jnp.zeros((EXTRA, half - 2 * LANES), BF16)


def forward_own_kernel(core_ref, own_ref, tile_ref, first_ref):
    classes, half = first_ref.shape[0], own_ref.shape[1]
    mine = pl.ds(pl.multiple_of(core_ref[0] * half, half), half)
    for b in range(first_ref.shape[1] // BAND):
        here = slice(b * BAND, (b + 1) * BAND)
        first_ref[:, here] = jnp.dot(
            own_ref[:classes], tile_ref[mine, here], preferred_element_type=F32
        )


def forward_kernel(core_ref, first_ref, own_ref, other_ref, tile_ref, rows_ref):
    classes, half = first_ref.shape[0], other_ref.shape[1]
    share = rows_ref.shape[2]
    examples = tile_ref.shape[1]
    theirs = pl.ds(pl.multiple_of((1 - core_ref[0]) * half, half), half)
    part = [ref[classes:, : 2 * LANES].astype(F32) for ref in (own_ref, other_ref)]
    part = part[0] + part[1]
    part = [part[3 * k : 3 * k + 1] + part[3 * k + 1 : 3 * k + 2] + part[3 * k + 2 : 3 * k + 3] for k in range(3)]
    powers = exponents(part[2]) - 14.0
    extra = half_rows(powers, part[:2])
    scales = column(jnp.exp2(-powers), classes)
    for b in range(examples // BAND):
        here = slice(b * BAND, (b + 1) * BAND)
        rows = jnp.dot(other_ref[:classes], tile_ref[theirs, here], preferred_element_type=F32)
        rows = (rows + first_ref[:, here]) * scales
        for k in range(BAND // share):
            at = b * (BAND // share) + k
            rows_ref[at, :classes] = rows[:, k * share : (k + 1) * share]
            rows_ref[at, classes:] = extra


def forward(core, lifted, other, tile, share):
    classes = lifted.shape[0] - EXTRA
    examples = tile.shape[1]
    first = call(
        forward_own_kernel,
        "forward_own",
        shape((classes, examples), F32),
        604 << 20,
        scalars=1,
        arrays=2,
    )(core, lifted, tile)
    return call(
        forward_kernel,
        "forward",
        shape((examples // share, classes + SCALARS, share), F32),
        604 << 20,
        scalars=1,
        arrays=4,
    )(core, first, lifted, other, tile)


def backward_other_kernel(
    core_ref, values_ref, turned_ref, first_ref, second_ref, flat_ref, row_ref
):
    shares, height, share = values_ref.shape
    classes, examples = flat_ref.shape
    wide = first_ref.shape[1]
    for k in range(shares):
        flat_ref[:, k * share : (k + 1) * share] = values_ref[k, :classes]
    row = jnp.zeros((8, 2 * LANES), F32)
    if height > classes:
        total = values_ref[0, classes:].astype(F32)
        for k in range(1, shares):
            total = total + values_ref[k, classes:].astype(F32)
        row = jnp.broadcast_to(read_rows(total, 0), (8, 2 * LANES))
    row_ref[...] = row
    first_ref[classes:, : 2 * LANES] = row
    first_ref[classes:, 2 * LANES :] = jnp.zeros((8, wide - 2 * LANES), F32)
    for k, ref in enumerate((first_ref, second_ref)):
        for b in range(wide // BAND):
            there = (1 - core_ref[0]) * (2 * wide) + k * wide + b * BAND
            ref[:classes, b * BAND : (b + 1) * BAND] = jnp.dot(
                flat_ref[...],
                turned_ref[:, pl.ds(pl.multiple_of(there, BAND), BAND)],
                preferred_element_type=F32,
            )


def backward_own_kernel(core_ref, flat_ref, turned_ref, own_ref):
    half = own_ref.shape[1]
    for b in range(half // BAND):
        there = pl.ds(pl.multiple_of(core_ref[0] * half + b * BAND, BAND), BAND)
        own_ref[:, b * BAND : (b + 1) * BAND] = jnp.dot(
            flat_ref[...], turned_ref[:, there], preferred_element_type=F32
        )


def backward_other(core, values, turned, classes):
    examples, count = turned.shape
    return call(
        backward_other_kernel,
        "backward_other",
        [
            shape((classes + SCALARS, count // 4), F32),
            shape((classes, count // 4), F32),
            shape((classes, examples), BF16),
            shape((8, 2 * LANES), F32),
        ],
        604 << 20,
        scalars=1,
        arrays=2,
    )(core, values, turned)


def backward_own(core, flat, turned):
    return call(
        backward_own_kernel,
        "backward_own",
        shape((flat.shape[0], turned.shape[1] // 2), F32),
        604 << 20,
        scalars=1,
        arrays=2,
    )(core, flat, turned)


def put_halves(ref, values, powers, vectors):
    classes, wide = values.shape
    ref[:classes] = values
    row = lax.broadcasted_iota(jnp.int32, (SCALARS, 2 * LANES), 0)
    out = jnp.zeros((SCALARS, 2 * LANES), F32)
    for p, piece in enumerate(half_pieces(powers, vectors)):
        out = jnp.where(row == p, piece, out)
    ref[classes:, : 2 * LANES] = out
    ref[classes:, 2 * LANES :] = jnp.zeros((SCALARS, wide - 2 * LANES), F32)


def pack_halves(ref, values, vectors):
    classes = values.shape[0]
    size = jnp.max(jnp.abs(values), axis=1, keepdims=True)
    powers = exponents(size) - 14.0
    empty = jnp.zeros((2 * LANES - classes, LANES), F32)
    row = jnp.concatenate([jnp.broadcast_to(powers, (classes, LANES)), empty], axis=0).T[:1]
    put_halves(ref, values * jnp.exp2(-powers), row, vectors)


def powers_of(ref):
    classes = ref.shape[0] - SCALARS
    return ref[classes : classes + 1, : 2 * LANES]


def unpack_pairs(pairs):
    refs = [ref for pair in pairs for ref in pair]
    classes = refs[0].shape[0] - SCALARS
    scales = columns([jnp.exp2(powers_of(ref)) for ref in refs], classes)
    values = [ref[:classes] * scale for ref, scale in zip(refs, scales)]
    return [values[2 * k] + values[2 * k + 1] for k in range(len(pairs))]


def unpack_vector(ref):
    classes = ref.shape[0] - SCALARS
    power, high, low = (ref[classes + p : classes + p + 1, : 2 * LANES] for p in range(1, 4))
    return jnp.exp2(power) * (high + low / 2048.0)


def join_first_kernel(own_ref, row_ref, got_ref, sum_ref):
    classes, wide = own_ref.shape[0], sum_ref.shape[1]
    vector = row_ref[:1] + got_ref[classes : classes + 1, : 2 * LANES]
    pack_halves(sum_ref, own_ref[:, :wide] + got_ref[:classes], [vector])


def join_second_kernel(own_ref, got_ref, sum_ref):
    pack_halves(sum_ref, own_ref[:, sum_ref.shape[1] :] + got_ref[...], [])


def join(own, row, first, second):
    half = shape((own.shape[0] + SCALARS, own.shape[1] // 2), F32)
    return (
        call(join_first_kernel, "join_first", half, 1 << 20, arrays=3)(own, row, first),
        call(join_second_kernel, "join_second", half, 1 << 20, arrays=2)(own, second),
    )


def add_kernel(own_ref, got_ref, sum_ref):
    classes = own_ref.shape[0] - SCALARS
    powers = jnp.maximum(powers_of(own_ref), powers_of(got_ref)) + 1.0
    own, got = columns(
        [jnp.exp2(powers_of(own_ref) - powers), jnp.exp2(powers_of(got_ref) - powers)], classes
    )
    vector = unpack_vector(own_ref) + unpack_vector(got_ref)
    put_halves(sum_ref, own_ref[:classes] * own + got_ref[:classes] * got, powers, [vector])


def add_halves(own, got):
    return call(add_kernel, "add", shape(own.shape, F32), 1 << 20, arrays=2)(own, got)


def gradient_kernel(base_ref, label_ref, weight_ref, hessian_ref, send_ref):
    classes, share = base_ref.shape
    base = base_ref[...]
    probability = jax.nn.sigmoid(base)
    row = lax.broadcasted_iota(jnp.int32, (classes, share), 0)
    target = jnp.where(row == label_ref[...], 1.0, 0.0)
    hessian_ref[...] = weight_ref[...] * probability * (1.0 - probability)
    gradient = (weight_ref[...] * (probability - target)).astype(BF16)
    for k in range(send_ref.shape[0]):
        send_ref[k] = gradient


def gradient(base, label, weight, shares):
    return call(
        gradient_kernel,
        "gradient",
        [shape(base.shape, F32), shape((shares,) + base.shape, BF16)],
        1 << 20,
        arrays=3,
    )(base, label, weight)


def residual_kernel(
    total, one_ref, one_in_ref, two_ref, two_in_ref, high_ref, low_ref, high_turned_ref,
    low_turned_ref, residual_ref, lifted_ref,
):
    one, two = unpack_pairs(((one_ref, one_in_ref), (two_ref, two_in_ref)))
    sums = jnp.concatenate([one, two], axis=1)
    residual = block_products(sums, high_ref, low_ref) * (-1.0 / total)
    residual_ref[...] = residual
    lifted = block_products(residual, high_turned_ref, low_turned_ref).astype(BF16)
    zero = jnp.zeros((1, 2 * LANES), F32)
    sizes = lane_sums(jnp.abs(lifted.astype(F32)))
    put_lifted(lifted_ref, lifted, [lane_sums(residual * residual), zero, sizes])


def first_residual(total, sums, blocks):
    classes, wide = sums[2].shape[0] - SCALARS, sums[2].shape[1]
    return call(
        functools.partial(residual_kernel, total),
        "residual",
        [
            shape((classes, 2 * wide), F32),
            shape((classes + EXTRA, 2 * wide), BF16),
        ],
        450 << 20,
        arrays=8,
    )(*sums, *blocks)


def weigh_kernel(parts_ref, hessian_ref, image_ref, norm_ref, send_ref):
    classes = hessian_ref.shape[0]
    image = sum_scaled(parts_ref, classes)
    image_ref[...] = image
    norm_ref[...] = stack_rows([half_vector(parts_ref, classes, 0)])
    weighted = (hessian_ref[...] * image).astype(BF16)
    extra = rows_of([lane_sums(weighted.astype(F32) * image)])
    for k in range(send_ref.shape[0]):
        send_ref[k, :classes] = weighted
        send_ref[k, classes:] = extra


def weigh(parts, hessian):
    return call(
        weigh_kernel,
        "weigh",
        [
            shape(hessian.shape, F32),
            shape((8, 2 * LANES), F32),
            shape((parts.shape[0], hessian.shape[0] + EXTRA, hessian.shape[1]), BF16),
        ],
        1 << 20,
        arrays=2,
    )(parts, hessian)


def step_kernel(
    total, one_ref, one_in_ref, two_ref, two_in_ref, high_ref, low_ref, high_turned_ref,
    low_turned_ref, residual_ref, norm_ref, lifted_ref, rough_ref,
):
    classes = residual_ref.shape[0]
    one, two = unpack_pairs(((one_ref, one_in_ref), (two_ref, two_in_ref)))
    curve = (unpack_vector(one_ref) + unpack_vector(one_in_ref)) / total
    norm = norm_ref[:1]
    lane = lax.broadcasted_iota(jnp.int32, (1, 2 * LANES), 1)
    rough = jnp.where(lane < classes, norm / (curve + RIDGE * norm), 0.0)
    rough_ref[...] = stack_rows([rough])
    sums = jnp.concatenate([one, two], axis=1)
    old = residual_ref[...]
    image = block_products(sums, high_ref, low_ref) / total + RIDGE * old
    new = old - column(rough, classes) * image
    lifted = block_products(new, high_turned_ref, low_turned_ref).astype(BF16)
    sizes = lane_sums(jnp.abs(lifted.astype(F32)))
    put_lifted(lifted_ref, lifted, [lane_sums(old * new), lane_sums(new * new), sizes])


def step(total, sums, blocks, residual, norm):
    classes, half = residual.shape
    return call(
        functools.partial(step_kernel, total),
        "step",
        [shape((classes + EXTRA, half), BF16), shape((8, 2 * LANES), F32)],
        450 << 20,
        arrays=10,
    )(*sums, *blocks, residual, norm)


def curve_kernel(
    parts_ref, hessian_ref, image_ref, norm_ref, rough_ref, last_ref, scales_ref, curve_ref
):
    classes = hessian_ref.shape[0]
    last = sum_scaled(parts_ref, classes)
    last_ref[...] = last
    cross = half_vector(parts_ref, classes, 0)
    norm_rough = half_vector(parts_ref, classes, 1)
    norm = norm_ref[:1]
    lane = lax.broadcasted_iota(jnp.int32, (1, 2 * LANES), 1)
    excess = jnp.where(lane < classes, cross / (norm - cross), 0.0)
    grown = 1.0 + excess
    norm_next = grown * (grown * norm_rough - 2.0 * excess * cross) + excess * excess * norm
    ratio = jnp.where(lane < classes, norm_next / norm, 0.0)
    ridge = RIDGE * (norm_next + ratio * ratio * norm)
    scales_ref[...] = stack_rows(
        [rough_ref[:1] * grown, grown, ratio - excess, norm_next, ridge]
    )
    scale, other = columns([grown, ratio - excess], classes)
    rows = scale * last + other * image_ref[...]
    weighted = (hessian_ref[...] * rows).astype(BF16).astype(F32)
    curve_ref[...] = lane_sums(weighted * rows)


def last_curve(parts, hessian, image, norm, rough):
    row = shape((8, 2 * LANES), F32)
    return call(
        curve_kernel,
        "curve",
        [shape(hessian.shape, F32), row, shape((1, 2 * LANES), F32)],
        1 << 20,
        arrays=5,
    )(parts, hessian, image, norm, rough)


def margins_kernel(total, curve_ref, scales_ref, base_ref, image_ref, last_ref, margins_ref):
    classes = base_ref.shape[0]
    curve = jnp.sum(curve_ref[:, 0], axis=0, keepdims=True)
    first, grown, other = scales_ref[0:1], scales_ref[1:2], scales_ref[2:3]
    lane = lax.broadcasted_iota(jnp.int32, (1, 2 * LANES), 1)
    second = jnp.where(
        lane < classes, scales_ref[3:4] / (curve / total + scales_ref[4:5]), 0.0
    )
    image_scale, last_scale = columns([first + second * other, second * grown], classes)
    margins_ref[...] = base_ref[...] + image_scale * image_ref[...] + last_scale * last_ref[...]


def margins(total, curve, scales, base, image, last):
    return call(
        functools.partial(margins_kernel, total), "margins", shape(base.shape, F32), 1 << 20, arrays=5
    )(curve, scales, base, image, last)


def shards(pool, indices, labels, example_weight, centers, alpha, precond):
    n_ex, n_ctr = lax.axis_size("ex"), lax.axis_size("ctr")
    classes, count = alpha.shape
    examples = indices.shape[0]
    share = examples // n_ctr
    total = float(examples * n_ex)
    core = (lax.axis_index("ex") % 2).reshape(1)
    core_pairs = [(i, i ^ 1) for i in range(n_ex)]

    def over_y(array, flip):
        pairs = [(2 * y + c, 2 * (y ^ flip) + c) for y in range(n_ex // 2) for c in range(2)]
        return lax.ppermute(array, "ex", pairs)

    def over_cores(array):
        return lax.ppermute(array, "ex", core_pairs)

    def trade(parts):
        return lax.all_to_all(parts, "ctr", 0, 0)

    def trade_halves(parts):
        return trade(parts.astype(F16)).astype(F32)

    def swap(array, flip):
        array = lax.reduce_precision(array, 5, 10)
        return array, over_y(array.astype(F16), flip).astype(F32)

    def sum_examples(send):
        first, second, flat, row = backward_other(core, trade(send), turned, classes)
        got = over_cores(first), over_cores(second)
        one, two = join(backward_own(core, flat, turned), row, *got)
        one, two = swap(one, 3), swap(two, 1)
        one, two = add_halves(*one), add_halves(*two)
        return (*swap(one, 1), *swap(two, 3)), got[0]

    offset = lax.axis_index("ctr") * share
    label = lax.dynamic_slice_in_dim(labels, offset, share, 0).reshape(1, share)
    weight = lax.dynamic_slice_in_dim(example_weight, offset, share, 0).reshape(1, share)
    index = indices.reshape(1, examples)
    sides, one_hot, chunk = prepare(index, centers, pool.shape[1])
    row_pool = trade(copies(pool, n_ctr))
    row_pool, sides, one_hot, chunk, label, weight, core = lax.optimization_barrier(
        (row_pool, sides, one_hot, chunk, label, weight, core)
    )
    tile, turned, rows = make_tile(chunk, row_pool, one_hot, sides, alpha, share)
    base = jnp.sum(trade_halves(rows), axis=0)
    hessian, send = gradient(base, label, weight, n_ctr)

    sums, got = sum_examples(send)
    got, late_core = lax.optimization_barrier((got, core))
    blocks = factors(late_core, precond)
    residual, lifted = first_residual(total, sums, blocks)
    rows = forward(core, lifted, over_cores(lifted), tile, share)
    image, norm, send = weigh(trade_halves(rows), hessian)

    sums, _ = sum_examples(send)
    lifted, rough = step(total, sums, blocks, residual, norm)
    rows = forward(core, lifted, over_cores(lifted), tile, share)
    last, scales, curve = last_curve(trade_halves(rows), hessian, image, norm, rough)

    curve = jnp.broadcast_to(curve, (n_ex * n_ctr,) + curve.shape)
    curve = lax.all_to_all(curve, ("ex", "ctr"), 0, 0)
    return margins(total, curve, scales, base, image, last)


def solution(mesh):
    return jax.shard_map(
        shards,
        mesh=mesh,
        in_specs=(
            P(None, ("ex", "ctr")),
            P("ex"),
            P("ex"),
            P("ex"),
            P(None, "ctr"),
            P(None, "ctr"),
            P("ctr", None),
        ),
        out_specs=P(None, ("ex", "ctr")),
        check_vma=False,
    )
```

```python
import functools
import math

import jax
import jax.numpy as jnp
from jax import lax
from jax.experimental import pallas as pl
from jax.experimental.pallas import tpu as pltpu
from jax.sharding import PartitionSpec as P

RIDGE = 0.0001
F32 = jnp.float32
F16 = jnp.float16
BF16 = jnp.bfloat16
VMEM_BYTES = 24 * 1024 * 1024
DEPTH = 128
BAND = 256
EXTRA = 16
SCALARS = 8
LANES = 128
NT = (((1,), (1,)), ((), ()))
TN = (((0,), (0,)), ((), ()))


def split3(values):
    high = values.astype(BF16)
    rest = values - high.astype(F32)
    middle = rest.astype(BF16)
    low = (rest - middle.astype(F32)).astype(BF16)
    return high, middle, low


SCALAR = pl.BlockSpec(memory_space=pltpu.SMEM)
WHOLE = pl.BlockSpec(memory_space=pltpu.VMEM)
ANYWHERE = pl.BlockSpec(memory_space=pl.ANY)


def call(kernel, name, out_shape, flops, scratch=(), scalars=0, anywhere=0, arrays=0):
    shapes = out_shape if isinstance(out_shape, list) else [out_shape]
    size = sum(math.prod(s.shape) * s.dtype.itemsize for s in shapes)
    return pl.pallas_call(
        kernel,
        out_shape=out_shape,
        scratch_shapes=list(scratch),
        in_specs=[SCALAR] * scalars + [ANYWHERE] * anywhere + [WHOLE] * arrays,
        compiler_params=pltpu.CompilerParams(vmem_limit_bytes=VMEM_BYTES),
        cost_estimate=pl.CostEstimate(flops=flops, bytes_accessed=size, transcendentals=0),
        name=name,
    )


def rows_of(vectors):
    row = lax.broadcasted_iota(jnp.int32, (EXTRA, LANES), 0)
    out = jnp.zeros((EXTRA, LANES), F32)
    for k, vector in enumerate(vectors):
        for p, piece in enumerate(split3(vector)):
            for q in range(2):
                value = piece.astype(F32)[:, q * LANES : (q + 1) * LANES]
                out = jnp.where(row == 6 * k + 2 * p + q, value, out)
    return out.astype(BF16)


def read_rows(summed, k):
    halves = [
        sum(summed[6 * k + 2 * p + q : 6 * k + 2 * p + q + 1] for p in range(3)) for q in range(2)
    ]
    return jnp.concatenate(halves, axis=1)


def exponents(bounds):
    return jnp.ceil(jnp.log2(jnp.maximum(bounds, 1e-30)))


def half_pieces(powers, vectors):
    pieces = [powers]
    for vector in vectors:
        power = exponents(jnp.abs(vector)) + 1.0
        scaled = vector * jnp.exp2(-power) * 2048.0
        high = jnp.floor(scaled + 0.5)
        pieces += [power, high / 2048.0, jnp.floor((scaled - high) * 2048.0 + 0.5) / 2048.0]
    return pieces


def half_rows(powers, vectors):
    row = lax.broadcasted_iota(jnp.int32, (SCALARS, LANES), 0)
    lane = lax.broadcasted_iota(jnp.int32, (SCALARS, LANES), 1)
    out = jnp.zeros((SCALARS, LANES), F32)
    for p, piece in enumerate(half_pieces(powers, vectors)):
        out = jnp.where(row == p, piece[:, :LANES], out)
        rest = piece[:, LANES : LANES + 16]
        rest = jnp.concatenate([rest] * (LANES // 16), axis=1)
        out = jnp.where((row == SCALARS - 1) & (lane // 16 == p), rest, out)
    return out


def half_row(parts_ref, first, p):
    rest = parts_ref[:, first + SCALARS - 1, :][:, 16 * p : 16 * p + 16]
    empty = jnp.zeros((parts_ref.shape[0], LANES - 16), F32)
    return jnp.concatenate([parts_ref[:, first + p, :], rest, empty], axis=1)


def half_vector(parts_ref, first, k):
    power, high, low = (half_row(parts_ref, first, 1 + 3 * k + p) for p in range(3))
    return jnp.sum(jnp.exp2(power) * (high + low / 2048.0), axis=0, keepdims=True)


def sum_scaled(parts_ref, classes):
    scales = jnp.exp2(half_row(parts_ref, classes, 0)).T
    total = parts_ref[0, :classes] * scales[:classes, :1]
    for k in range(1, parts_ref.shape[0]):
        total = total + parts_ref[k, :classes] * scales[:classes, k : k + 1]
    return total


def columns(vectors, classes):
    turned = stack_rows(vectors).T
    return [turned[:classes, k : k + 1] for k in range(len(vectors))]


def column(vector, classes):
    return jnp.broadcast_to(vector, (8, vector.shape[1])).T[:classes, :1]


def lane_sums(values):
    folded = sum(values[:, k : k + LANES] for k in range(0, values.shape[1], LANES))
    empty = jnp.zeros((2 * LANES - values.shape[0], LANES), F32)
    return jnp.sum(jnp.concatenate([folded, empty], axis=0).T, axis=0, keepdims=True)


def stack_rows(vectors):
    row = lax.broadcasted_iota(jnp.int32, (8, 2 * LANES), 0)
    out = jnp.zeros((8, 2 * LANES), F32)
    for k, vector in enumerate(vectors):
        out = jnp.where(row == k, vector, out)
    return out


def shape(dims, dtype):
    return jax.ShapeDtypeStruct(dims, dtype)


def tail(squares, first, pad):
    pieces = [p.astype(F32) for p in split3(-0.5 * squares)]
    row = lax.broadcasted_iota(jnp.int32, (pad, squares.shape[1]), 0)
    out = jnp.where((row >= 3 - first) & (row < 6 - first), 1.0, 0.0)
    for k in range(3):
        out = jnp.where(row == k + first, pieces[k], out)
    return out


def copies_kernel(block_ref, copies_ref):
    features, lanes = block_ref.shape
    for k in range(copies_ref.shape[0]):
        for q in range(lanes // LANES):
            copies_ref[k, q * features : (q + 1) * features] = block_ref[
                :, q * LANES : (q + 1) * LANES
            ]


def copies(block, number):
    out = shape((number, block.size // LANES, LANES), block.dtype)
    return call(copies_kernel, "copies", out, 1 << 20, arrays=1)(block)


def prepare_kernel(index_ref, centers_ref, sides_ref, one_hot_ref, chunk_ref):
    features, count = centers_ref.shape
    lanes = one_hot_ref.shape[0]
    center_float = centers_ref[...].astype(F32)
    center_sq = jnp.sum(center_float * center_float, axis=0, keepdims=True)
    side = jnp.concatenate([center_float, tail(center_sq, 3, DEPTH - features)], axis=0)
    sides_ref[...] = side.T.astype(BF16)
    chunk_ref[...] = index_ref[...] // lanes
    within = index_ref[...] % lanes
    row = lax.broadcasted_iota(jnp.int32, (lanes, index_ref.shape[1]), 0)
    one_hot_ref[...] = (row == within).astype(F32).astype(BF16)


def prepare(index, centers, lanes):
    features, count = centers.shape
    examples = index.shape[1]
    return call(
        prepare_kernel,
        "prepare",
        [shape((count, DEPTH), BF16), shape((lanes, examples), BF16), shape(index.shape, jnp.int32)],
        1 << 20,
        arrays=2,
    )(index, centers)


def tile_kernel(
    alpha_hbm, chunk_ref, pool_ref, one_hot_ref, sides_ref, tile_ref, turned_ref, rows_ref,
    side_ref, base_ref, alpha_ref, alpha_sem,
):
    fetch = pltpu.make_async_copy(alpha_hbm, alpha_ref, alpha_sem)
    fetch.start()
    chunks, height, _ = pool_ref.shape
    lanes = one_hot_ref.shape[0]
    features = height * LANES // lanes
    count, examples = tile_ref.shape
    share = rows_ref.shape[2]
    scale = 4.0 / features * math.log2(math.e)
    pool = jnp.concatenate(
        [
            pool_ref[:, q * features : (q + 1) * features, :].reshape(chunks * features, LANES)
            for q in range(lanes // LANES)
        ],
        axis=1,
    )
    for b in range(examples // BAND):
        here = slice(b * BAND, (b + 1) * BAND)
        chunk = chunk_ref[:, here]
        picked = jnp.dot(pool, one_hot_ref[:, here], preferred_element_type=F32)
        points = jnp.where(chunk == 0, picked[:features], 0.0)
        for k in range(1, chunks):
            points = jnp.where(chunk == k, picked[k * features : (k + 1) * features], points)
        point_sq = jnp.sum(points * points, axis=0, keepdims=True)
        side = jnp.concatenate([points, tail(point_sq, 0, DEPTH - features)], axis=0)
        side_ref[:, here] = side.astype(BF16)
    fetch.wait()
    for b in range(count // BAND):
        here = slice(b * BAND, (b + 1) * BAND)
        near = jnp.dot(sides_ref[here, :], side_ref[...], preferred_element_type=F32)
        values = jnp.exp2(near * scale).astype(BF16)
        tile_ref[here, :] = values
        turned_ref[:, here] = values.T
        rows = jnp.dot(alpha_ref[:, here], values, preferred_element_type=F32)
        base_ref[...] = rows if b == 0 else base_ref[...] + rows
    for k in range(examples // share):
        rows_ref[k] = base_ref[:, k * share : (k + 1) * share]


def make_tile(chunk, row_pool, one_hot, sides, alpha, share):
    examples, count = chunk.shape[1], sides.shape[0]
    classes = alpha.shape[0]
    return call(
        tile_kernel,
        "tile",
        [
            shape((count, examples), BF16),
            shape((examples, count), BF16),
            shape((examples // share, classes, share), F32),
        ],
        4 << 30,
        [
            pltpu.VMEM((DEPTH, examples), BF16),
            pltpu.VMEM((classes, examples), F32),
            pltpu.VMEM(alpha.shape, BF16),
            pltpu.SemaphoreType.DMA,
        ],
        anywhere=1,
        arrays=4,
    )(alpha, chunk, row_pool, one_hot, sides)


def factors_kernel(core_ref, precond_ref, high_ref, low_ref, high_turned_ref, low_turned_ref):
    order = precond_ref.shape[1]
    half = high_ref.shape[0]
    first = core_ref[0] * half
    for k in range(half // order):
        here = slice(k * order, (k + 1) * order)
        block = precond_ref[pl.ds(pl.multiple_of(first + k * order, order), order), :]
        high = block.astype(BF16)
        high_ref[here] = high
        low_ref[here] = (block - high.astype(F32)).astype(BF16)
        turned = block.T
        high = turned.astype(BF16)
        high_turned_ref[here] = high
        low_turned_ref[here] = (turned - high.astype(F32)).astype(BF16)


def factors(core, precond):
    out = shape((precond.shape[0] // 2, precond.shape[1]), BF16)
    return call(factors_kernel, "factors", [out] * 4, 1 << 20, scalars=1, arrays=1)(core, precond)


def block_products(values, high_ref, low_ref):
    order = high_ref.shape[1]
    out = []
    for k in range(high_ref.shape[0] // order):
        here = slice(k * order, (k + 1) * order)
        block = values[:, here]
        high = block.astype(BF16)
        low = (block - high.astype(F32)).astype(BF16)
        product = jnp.dot(high, high_ref[here], preferred_element_type=F32)
        product += jnp.dot(high, low_ref[here], preferred_element_type=F32)
        product += jnp.dot(low, high_ref[here], preferred_element_type=F32)
        out.append(product)
    return jnp.concatenate(out, axis=1)


def put_lifted(ref, second_ref, lifted, vectors):
    classes, half = lifted.shape[0], ref.shape[1]
    ref[:classes] = lifted[:, :half]
    second_ref[...] = lifted[:, half:]
    row = lax.broadcasted_iota(jnp.int32, (EXTRA, 2 * LANES), 0)
    out = jnp.zeros((EXTRA, 2 * LANES), F32)
    for k, vector in enumerate(vectors):
        for p, piece in enumerate(split3(vector)):
            out = jnp.where(row == 3 * k + p, piece.astype(F32), out)
    ref[classes:, : 2 * LANES] = out.astype(BF16)
    ref[classes:, 2 * LANES :] = jnp.zeros((EXTRA, half - 2 * LANES), BF16)


def forward_own_kernel(core_ref, own_ref, second_ref, tile_ref, sums_ref):
    classes, wide = second_ref.shape
    first = core_ref[0] * (2 * wide)
    mine = [pl.ds(pl.multiple_of(first + k * wide, wide), wide) for k in range(2)]
    for b in range(sums_ref.shape[1] // BAND):
        here = slice(b * BAND, (b + 1) * BAND)
        rows = jnp.dot(own_ref[:classes], tile_ref[mine[0], here], preferred_element_type=F32)
        rows += jnp.dot(second_ref[...], tile_ref[mine[1], here], preferred_element_type=F32)
        sums_ref[:, here] = rows


def forward_more_kernel(core_ref, sums_ref, other_ref, tile_ref, more_ref):
    classes, wide = sums_ref.shape[0], other_ref.shape[1]
    theirs = pl.ds(pl.multiple_of((1 - core_ref[0]) * (2 * wide), wide), wide)
    for b in range(sums_ref.shape[1] // BAND):
        here = slice(b * BAND, (b + 1) * BAND)
        rows = jnp.dot(other_ref[:classes], tile_ref[theirs, here], preferred_element_type=F32)
        more_ref[:, here] = sums_ref[:, here] + rows


def forward_kernel(core_ref, first_ref, own_ref, other_ref, second_ref, tile_ref, rows_ref):
    classes, half = first_ref.shape[0], other_ref.shape[1]
    share = rows_ref.shape[2]
    examples = tile_ref.shape[1]
    theirs = pl.ds(pl.multiple_of((1 - core_ref[0]) * (2 * half) + half, half), half)
    part = [ref[classes:, : 2 * LANES].astype(F32) for ref in (own_ref, other_ref)]
    part = part[0] + part[1]
    part = [part[3 * k : 3 * k + 1] + part[3 * k + 1 : 3 * k + 2] + part[3 * k + 2 : 3 * k + 3] for k in range(3)]
    powers = exponents(part[2]) - 14.0
    extra = half_rows(powers, part[:2])
    scales = column(jnp.exp2(-powers), classes)
    for b in range(examples // BAND):
        here = slice(b * BAND, (b + 1) * BAND)
        rows = jnp.dot(second_ref[...], tile_ref[theirs, here], preferred_element_type=F32)
        rows = (rows + first_ref[:, here]) * scales
        for k in range(BAND // share):
            at = b * (BAND // share) + k
            rows_ref[at, :classes] = rows[:, k * share : (k + 1) * share]
            rows_ref[at, classes:] = extra


def forward(core, own, other, tile, share):
    classes = own[1].shape[0]
    examples = tile.shape[1]
    sums = shape((classes, examples), F32)
    first = call(
        forward_own_kernel, "forward_own", sums, 604 << 20, scalars=1, arrays=3
    )(core, *own, tile)
    first = call(
        forward_more_kernel, "forward_more", sums, 302 << 20, scalars=1, arrays=3
    )(core, first, other[0], tile)
    return call(
        forward_kernel,
        "forward",
        shape((examples // share, classes + SCALARS, share), F32),
        302 << 20,
        scalars=1,
        arrays=5,
    )(core, first, own[0], *other, tile)


def backward_other_kernel(
    core_ref, values_ref, turned_ref, first_ref, second_ref, flat_ref, row_ref
):
    shares, height, share = values_ref.shape
    classes, examples = flat_ref.shape
    wide = first_ref.shape[1]
    for k in range(shares):
        flat_ref[:, k * share : (k + 1) * share] = values_ref[k, :classes]
    row = jnp.zeros((8, 2 * LANES), F32)
    if height > classes:
        total = values_ref[0, classes:].astype(F32)
        for k in range(1, shares):
            total = total + values_ref[k, classes:].astype(F32)
        row = jnp.broadcast_to(read_rows(total, 0), (8, 2 * LANES))
    row_ref[...] = row
    first_ref[classes:, : 2 * LANES] = row
    first_ref[classes:, 2 * LANES :] = jnp.zeros((8, wide - 2 * LANES), F32)
    for k, ref in enumerate((first_ref, second_ref)):
        for b in range(wide // BAND):
            there = (1 - core_ref[0]) * (2 * wide) + k * wide + b * BAND
            ref[:classes, b * BAND : (b + 1) * BAND] = jnp.dot(
                flat_ref[...],
                turned_ref[:, pl.ds(pl.multiple_of(there, BAND), BAND)],
                preferred_element_type=F32,
            )


def backward_own_kernel(core_ref, flat_ref, turned_ref, own_ref):
    half = own_ref.shape[1]
    for b in range(half // BAND):
        there = pl.ds(pl.multiple_of(core_ref[0] * half + b * BAND, BAND), BAND)
        own_ref[:, b * BAND : (b + 1) * BAND] = jnp.dot(
            flat_ref[...], turned_ref[:, there], preferred_element_type=F32
        )


def backward_other(core, values, turned, classes):
    examples, count = turned.shape
    return call(
        backward_other_kernel,
        "backward_other",
        [
            shape((classes + SCALARS, count // 4), F32),
            shape((classes, count // 4), F32),
            shape((classes, examples), BF16),
            shape((8, 2 * LANES), F32),
        ],
        604 << 20,
        scalars=1,
        arrays=2,
    )(core, values, turned)


def backward_own(core, flat, turned):
    return call(
        backward_own_kernel,
        "backward_own",
        shape((flat.shape[0], turned.shape[1] // 2), F32),
        604 << 20,
        scalars=1,
        arrays=2,
    )(core, flat, turned)


def put_halves(ref, values, powers, vectors):
    classes, wide = values.shape
    ref[:classes] = values
    row = lax.broadcasted_iota(jnp.int32, (SCALARS, 2 * LANES), 0)
    out = jnp.zeros((SCALARS, 2 * LANES), F32)
    for p, piece in enumerate(half_pieces(powers, vectors)):
        out = jnp.where(row == p, piece, out)
    ref[classes:, : 2 * LANES] = out
    ref[classes:, 2 * LANES :] = jnp.zeros((SCALARS, wide - 2 * LANES), F32)


def pack_halves(ref, values, vectors):
    classes = values.shape[0]
    size = jnp.max(jnp.abs(values), axis=1, keepdims=True)
    powers = exponents(size) - 14.0
    empty = jnp.zeros((2 * LANES - classes, LANES), F32)
    row = jnp.concatenate([jnp.broadcast_to(powers, (classes, LANES)), empty], axis=0).T[:1]
    put_halves(ref, values * jnp.exp2(-powers), row, vectors)


def powers_of(ref):
    classes = ref.shape[0] - SCALARS
    return ref[classes : classes + 1, : 2 * LANES]


def unpack_pairs(pairs):
    refs = [ref for pair in pairs for ref in pair]
    classes = refs[0].shape[0] - SCALARS
    scales = columns([jnp.exp2(powers_of(ref)) for ref in refs], classes)
    values = [ref[:classes] * scale for ref, scale in zip(refs, scales)]
    return [values[2 * k] + values[2 * k + 1] for k in range(len(pairs))]


def unpack_vector(ref):
    classes = ref.shape[0] - SCALARS
    power, high, low = (ref[classes + p : classes + p + 1, : 2 * LANES] for p in range(1, 4))
    return jnp.exp2(power) * (high + low / 2048.0)


def join_first_kernel(own_ref, row_ref, got_ref, sum_ref):
    classes, wide = own_ref.shape[0], sum_ref.shape[1]
    vector = row_ref[:1] + got_ref[classes : classes + 1, : 2 * LANES]
    pack_halves(sum_ref, own_ref[:, :wide] + got_ref[:classes], [vector])


def join_second_kernel(own_ref, got_ref, sum_ref):
    pack_halves(sum_ref, own_ref[:, sum_ref.shape[1] :] + got_ref[...], [])


def join(own, row, first, second):
    half = shape((own.shape[0] + SCALARS, own.shape[1] // 2), F32)
    return (
        call(join_first_kernel, "join_first", half, 1 << 20, arrays=3)(own, row, first),
        call(join_second_kernel, "join_second", half, 1 << 20, arrays=2)(own, second),
    )


def add_kernel(own_ref, got_ref, sum_ref):
    classes = own_ref.shape[0] - SCALARS
    powers = jnp.maximum(powers_of(own_ref), powers_of(got_ref)) + 1.0
    own, got = columns(
        [jnp.exp2(powers_of(own_ref) - powers), jnp.exp2(powers_of(got_ref) - powers)], classes
    )
    vector = unpack_vector(own_ref) + unpack_vector(got_ref)
    put_halves(sum_ref, own_ref[:classes] * own + got_ref[:classes] * got, powers, [vector])


def add_halves(own, got):
    return call(add_kernel, "add", shape(own.shape, F32), 1 << 20, arrays=2)(own, got)


def gradient_kernel(base_ref, label_ref, weight_ref, hessian_ref, send_ref):
    classes, share = base_ref.shape
    base = base_ref[...]
    probability = jax.nn.sigmoid(base)
    row = lax.broadcasted_iota(jnp.int32, (classes, share), 0)
    target = jnp.where(row == label_ref[...], 1.0, 0.0)
    hessian_ref[...] = weight_ref[...] * probability * (1.0 - probability)
    gradient = (weight_ref[...] * (probability - target)).astype(BF16)
    for k in range(send_ref.shape[0]):
        send_ref[k] = gradient


def gradient(base, label, weight, shares):
    return call(
        gradient_kernel,
        "gradient",
        [shape(base.shape, F32), shape((shares,) + base.shape, BF16)],
        1 << 20,
        arrays=3,
    )(base, label, weight)


def residual_kernel(
    total, one_ref, one_in_ref, two_ref, two_in_ref, high_ref, low_ref, high_turned_ref,
    low_turned_ref, residual_ref, lifted_ref, second_ref,
):
    one, two = unpack_pairs(((one_ref, one_in_ref), (two_ref, two_in_ref)))
    sums = jnp.concatenate([one, two], axis=1)
    residual = block_products(sums, high_ref, low_ref) * (-1.0 / total)
    residual_ref[...] = residual
    lifted = block_products(residual, high_turned_ref, low_turned_ref).astype(BF16)
    zero = jnp.zeros((1, 2 * LANES), F32)
    sizes = lane_sums(jnp.abs(lifted.astype(F32)))
    put_lifted(lifted_ref, second_ref, lifted, [lane_sums(residual * residual), zero, sizes])


def first_residual(total, sums, blocks):
    classes, wide = sums[2].shape[0] - SCALARS, sums[2].shape[1]
    return call(
        functools.partial(residual_kernel, total),
        "residual",
        [
            shape((classes, 2 * wide), F32),
            shape((classes + EXTRA, wide), BF16),
            shape((classes, wide), BF16),
        ],
        450 << 20,
        arrays=8,
    )(*sums, *blocks)


def weigh_kernel(parts_ref, hessian_ref, image_ref, norm_ref, send_ref):
    classes = hessian_ref.shape[0]
    image = sum_scaled(parts_ref, classes)
    image_ref[...] = image
    norm_ref[...] = stack_rows([half_vector(parts_ref, classes, 0)])
    weighted = (hessian_ref[...] * image).astype(BF16)
    extra = rows_of([lane_sums(weighted.astype(F32) * image)])
    for k in range(send_ref.shape[0]):
        send_ref[k, :classes] = weighted
        send_ref[k, classes:] = extra


def weigh(parts, hessian):
    return call(
        weigh_kernel,
        "weigh",
        [
            shape(hessian.shape, F32),
            shape((8, 2 * LANES), F32),
            shape((parts.shape[0], hessian.shape[0] + EXTRA, hessian.shape[1]), BF16),
        ],
        1 << 20,
        arrays=2,
    )(parts, hessian)


def step_kernel(
    total, one_ref, one_in_ref, two_ref, two_in_ref, high_ref, low_ref, high_turned_ref,
    low_turned_ref, residual_ref, norm_ref, lifted_ref, second_ref, rough_ref,
):
    classes = residual_ref.shape[0]
    one, two = unpack_pairs(((one_ref, one_in_ref), (two_ref, two_in_ref)))
    curve = (unpack_vector(one_ref) + unpack_vector(one_in_ref)) / total
    norm = norm_ref[:1]
    lane = lax.broadcasted_iota(jnp.int32, (1, 2 * LANES), 1)
    rough = jnp.where(lane < classes, norm / (curve + RIDGE * norm), 0.0)
    rough_ref[...] = stack_rows([rough])
    sums = jnp.concatenate([one, two], axis=1)
    old = residual_ref[...]
    image = block_products(sums, high_ref, low_ref) / total + RIDGE * old
    new = old - column(rough, classes) * image
    lifted = block_products(new, high_turned_ref, low_turned_ref).astype(BF16)
    sizes = lane_sums(jnp.abs(lifted.astype(F32)))
    put_lifted(lifted_ref, second_ref, lifted, [lane_sums(old * new), lane_sums(new * new), sizes])


def step(total, sums, blocks, residual, norm):
    classes, half = residual.shape
    return call(
        functools.partial(step_kernel, total),
        "step",
        [
            shape((classes + EXTRA, half // 2), BF16),
            shape((classes, half // 2), BF16),
            shape((8, 2 * LANES), F32),
        ],
        450 << 20,
        arrays=10,
    )(*sums, *blocks, residual, norm)


def curve_kernel(
    parts_ref, hessian_ref, image_ref, norm_ref, rough_ref, last_ref, scales_ref, curve_ref
):
    classes = hessian_ref.shape[0]
    last = sum_scaled(parts_ref, classes)
    last_ref[...] = last
    cross = half_vector(parts_ref, classes, 0)
    norm_rough = half_vector(parts_ref, classes, 1)
    norm = norm_ref[:1]
    lane = lax.broadcasted_iota(jnp.int32, (1, 2 * LANES), 1)
    excess = jnp.where(lane < classes, cross / (norm - cross), 0.0)
    grown = 1.0 + excess
    norm_next = grown * (grown * norm_rough - 2.0 * excess * cross) + excess * excess * norm
    ratio = jnp.where(lane < classes, norm_next / norm, 0.0)
    ridge = RIDGE * (norm_next + ratio * ratio * norm)
    scales_ref[...] = stack_rows(
        [rough_ref[:1] * grown, grown, ratio - excess, norm_next, ridge]
    )
    scale, other = columns([grown, ratio - excess], classes)
    rows = scale * last + other * image_ref[...]
    weighted = (hessian_ref[...] * rows).astype(BF16).astype(F32)
    curve_ref[...] = lane_sums(weighted * rows)


def last_curve(parts, hessian, image, norm, rough):
    row = shape((8, 2 * LANES), F32)
    return call(
        curve_kernel,
        "curve",
        [shape(hessian.shape, F32), row, shape((1, 2 * LANES), F32)],
        1 << 20,
        arrays=5,
    )(parts, hessian, image, norm, rough)


def margins_kernel(total, curve_ref, scales_ref, base_ref, image_ref, last_ref, margins_ref):
    classes = base_ref.shape[0]
    curve = jnp.sum(curve_ref[:, 0], axis=0, keepdims=True)
    first, grown, other = scales_ref[0:1], scales_ref[1:2], scales_ref[2:3]
    lane = lax.broadcasted_iota(jnp.int32, (1, 2 * LANES), 1)
    second = jnp.where(
        lane < classes, scales_ref[3:4] / (curve / total + scales_ref[4:5]), 0.0
    )
    image_scale, last_scale = columns([first + second * other, second * grown], classes)
    margins_ref[...] = base_ref[...] + image_scale * image_ref[...] + last_scale * last_ref[...]


def margins(total, curve, scales, base, image, last):
    return call(
        functools.partial(margins_kernel, total), "margins", shape(base.shape, F32), 1 << 20, arrays=5
    )(curve, scales, base, image, last)


def shards(pool, indices, labels, example_weight, centers, alpha, precond):
    n_ex, n_ctr = lax.axis_size("ex"), lax.axis_size("ctr")
    classes, count = alpha.shape
    examples = indices.shape[0]
    share = examples // n_ctr
    total = float(examples * n_ex)
    core = (lax.axis_index("ex") % 2).reshape(1)
    core_pairs = [(i, i ^ 1) for i in range(n_ex)]

    def over_y(array, flip):
        pairs = [(2 * y + c, 2 * (y ^ flip) + c) for y in range(n_ex // 2) for c in range(2)]
        return lax.ppermute(array, "ex", pairs)

    def over_cores(array):
        return lax.ppermute(array, "ex", core_pairs)

    def trade(parts):
        return lax.all_to_all(parts, "ctr", 0, 0)

    def trade_halves(parts):
        return trade(parts.astype(F16)).astype(F32)

    def swap(array, flip):
        array = lax.reduce_precision(array, 5, 10)
        return array, over_y(array.astype(F16), flip).astype(F32)

    def sum_examples(send):
        first, second, flat, row = backward_other(core, trade(send), turned, classes)
        got = over_cores(first), over_cores(second)
        one, two = join(backward_own(core, flat, turned), row, *got)
        one, two = swap(one, 3), swap(two, 1)
        one, two = add_halves(*one), add_halves(*two)
        return (*swap(one, 1), *swap(two, 3)), got[0]

    offset = lax.axis_index("ctr") * share
    label = lax.dynamic_slice_in_dim(labels, offset, share, 0).reshape(1, share)
    weight = lax.dynamic_slice_in_dim(example_weight, offset, share, 0).reshape(1, share)
    index = indices.reshape(1, examples)
    sides, one_hot, chunk = prepare(index, centers, pool.shape[1])
    row_pool = trade(copies(pool, n_ctr))
    row_pool, sides, one_hot, chunk, label, weight, core = lax.optimization_barrier(
        (row_pool, sides, one_hot, chunk, label, weight, core)
    )
    tile, turned, rows = make_tile(chunk, row_pool, one_hot, sides, alpha, share)
    base = jnp.sum(trade_halves(rows), axis=0)
    hessian, send = gradient(base, label, weight, n_ctr)

    sums, got = sum_examples(send)
    got, late_core = lax.optimization_barrier((got, core))
    blocks = factors(late_core, precond)
    residual, *lifted = first_residual(total, sums, blocks)
    rows = forward(core, lifted, [over_cores(part) for part in lifted], tile, share)
    image, norm, send = weigh(trade_halves(rows), hessian)

    sums, _ = sum_examples(send)
    *lifted, rough = step(total, sums, blocks, residual, norm)
    rows = forward(core, lifted, [over_cores(part) for part in lifted], tile, share)
    last, scales, curve = last_curve(trade_halves(rows), hessian, image, norm, rough)

    curve = jnp.broadcast_to(curve, (n_ex * n_ctr,) + curve.shape)
    curve = lax.all_to_all(curve, ("ex", "ctr"), 0, 0)
    return margins(total, curve, scales, base, image, last)


def solution(mesh):
    return jax.shard_map(
        shards,
        mesh=mesh,
        in_specs=(
            P(None, ("ex", "ctr")),
            P("ex"),
            P("ex"),
            P("ex"),
            P(None, "ctr"),
            P(None, "ctr"),
            P("ctr", None),
        ),
        out_specs=P(None, ("ex", "ctr")),
        check_vma=False,
    )
```

```python
import functools
import math

import jax
import jax.numpy as jnp
from jax import lax
from jax.experimental import pallas as pl
from jax.experimental.pallas import tpu as pltpu
from jax.sharding import PartitionSpec as P

RIDGE = 0.0001
F32 = jnp.float32
F16 = jnp.float16
BF16 = jnp.bfloat16
VMEM_BYTES = 24 * 1024 * 1024
DEPTH = 128
BAND = 256
EXTRA = 16
SCALARS = 8
LANES = 128
NT = (((1,), (1,)), ((), ()))
TN = (((0,), (0,)), ((), ()))


def split3(values):
    high = values.astype(BF16)
    rest = values - high.astype(F32)
    middle = rest.astype(BF16)
    low = (rest - middle.astype(F32)).astype(BF16)
    return high, middle, low


SCALAR = pl.BlockSpec(memory_space=pltpu.SMEM)
WHOLE = pl.BlockSpec(memory_space=pltpu.VMEM)
ANYWHERE = pl.BlockSpec(memory_space=pl.ANY)


def call(kernel, name, out_shape, flops, scratch=(), scalars=0, anywhere=0, arrays=0):
    shapes = out_shape if isinstance(out_shape, list) else [out_shape]
    size = sum(math.prod(s.shape) * s.dtype.itemsize for s in shapes)
    return pl.pallas_call(
        kernel,
        out_shape=out_shape,
        scratch_shapes=list(scratch),
        in_specs=[SCALAR] * scalars + [ANYWHERE] * anywhere + [WHOLE] * arrays,
        compiler_params=pltpu.CompilerParams(vmem_limit_bytes=VMEM_BYTES),
        cost_estimate=pl.CostEstimate(flops=flops, bytes_accessed=size, transcendentals=0),
        name=name,
    )


def rows_of(vectors):
    row = lax.broadcasted_iota(jnp.int32, (EXTRA, LANES), 0)
    out = jnp.zeros((EXTRA, LANES), F32)
    for k, vector in enumerate(vectors):
        for p, piece in enumerate(split3(vector)):
            for q in range(2):
                value = piece.astype(F32)[:, q * LANES : (q + 1) * LANES]
                out = jnp.where(row == 6 * k + 2 * p + q, value, out)
    return out.astype(BF16)


def read_rows(summed, k):
    halves = [
        sum(summed[6 * k + 2 * p + q : 6 * k + 2 * p + q + 1] for p in range(3)) for q in range(2)
    ]
    return jnp.concatenate(halves, axis=1)


def exponents(bounds):
    return jnp.ceil(jnp.log2(jnp.maximum(bounds, 1e-30)))


def half_pieces(powers, vectors):
    pieces = [powers]
    for vector in vectors:
        power = exponents(jnp.abs(vector)) + 1.0
        scaled = vector * jnp.exp2(-power) * 2048.0
        high = jnp.floor(scaled + 0.5)
        pieces += [power, high / 2048.0, jnp.floor((scaled - high) * 2048.0 + 0.5) / 2048.0]
    return pieces


def half_rows(powers, vectors):
    row = lax.broadcasted_iota(jnp.int32, (SCALARS, LANES), 0)
    lane = lax.broadcasted_iota(jnp.int32, (SCALARS, LANES), 1)
    out = jnp.zeros((SCALARS, LANES), F32)
    for p, piece in enumerate(half_pieces(powers, vectors)):
        out = jnp.where(row == p, piece[:, :LANES], out)
        rest = piece[:, LANES : LANES + 16]
        rest = jnp.concatenate([rest] * (LANES // 16), axis=1)
        out = jnp.where((row == SCALARS - 1) & (lane // 16 == p), rest, out)
    return out


def half_row(parts_ref, first, p):
    rest = parts_ref[:, first + SCALARS - 1, :][:, 16 * p : 16 * p + 16]
    empty = jnp.zeros((parts_ref.shape[0], LANES - 16), F32)
    return jnp.concatenate([parts_ref[:, first + p, :], rest, empty], axis=1)


def half_vector(parts_ref, first, k):
    power, high, low = (half_row(parts_ref, first, 1 + 3 * k + p) for p in range(3))
    return jnp.sum(jnp.exp2(power) * (high + low / 2048.0), axis=0, keepdims=True)


def sum_scaled(parts_ref, classes):
    scales = jnp.exp2(half_row(parts_ref, classes, 0)).T
    total = parts_ref[0, :classes] * scales[:classes, :1]
    for k in range(1, parts_ref.shape[0]):
        total = total + parts_ref[k, :classes] * scales[:classes, k : k + 1]
    return total


def columns(vectors, classes):
    turned = stack_rows(vectors).T
    return [turned[:classes, k : k + 1] for k in range(len(vectors))]


def column(vector, classes):
    return jnp.broadcast_to(vector, (8, vector.shape[1])).T[:classes, :1]


def lane_sums_of(arrays):
    classes = arrays[0].shape[0]
    lane = lax.broadcasted_iota(jnp.int32, (classes, LANES), 1)
    out = jnp.zeros((classes, LANES), F32)
    for k, values in enumerate(arrays):
        folded = sum(values[:, j : j + LANES] for j in range(0, values.shape[1], LANES))
        out = jnp.where(lane == k, jnp.sum(folded, axis=1, keepdims=True), out)
    empty = jnp.zeros((2 * LANES - classes, LANES), F32)
    turned = jnp.concatenate([out, empty], axis=0).T
    return [turned[k : k + 1] for k in range(len(arrays))]


def stack_rows(vectors):
    row = lax.broadcasted_iota(jnp.int32, (8, 2 * LANES), 0)
    out = jnp.zeros((8, 2 * LANES), F32)
    for k, vector in enumerate(vectors):
        out = jnp.where(row == k, vector, out)
    return out


def shape(dims, dtype):
    return jax.ShapeDtypeStruct(dims, dtype)


def tail(squares, first, pad):
    pieces = [p.astype(F32) for p in split3(-0.5 * squares)]
    row = lax.broadcasted_iota(jnp.int32, (pad, squares.shape[1]), 0)
    out = jnp.where((row >= 3 - first) & (row < 6 - first), 1.0, 0.0)
    for k in range(3):
        out = jnp.where(row == k + first, pieces[k], out)
    return out


def copies_kernel(block_ref, copies_ref):
    features, lanes = block_ref.shape
    for k in range(copies_ref.shape[0]):
        for q in range(lanes // LANES):
            copies_ref[k, q * features : (q + 1) * features] = block_ref[
                :, q * LANES : (q + 1) * LANES
            ]


def copies(block, number):
    out = shape((number, block.size // LANES, LANES), block.dtype)
    return call(copies_kernel, "copies", out, 1 << 20, arrays=1)(block)


def prepare_kernel(index_ref, centers_ref, sides_ref, one_hot_ref, chunk_ref):
    features, count = centers_ref.shape
    lanes = one_hot_ref.shape[0]
    center_float = centers_ref[...].astype(F32)
    center_sq = jnp.sum(center_float * center_float, axis=0, keepdims=True)
    side = jnp.concatenate([center_float, tail(center_sq, 3, DEPTH - features)], axis=0)
    sides_ref[...] = side.T.astype(BF16)
    chunk_ref[...] = index_ref[...] // lanes
    within = index_ref[...] % lanes
    row = lax.broadcasted_iota(jnp.int32, (lanes, index_ref.shape[1]), 0)
    one_hot_ref[...] = (row == within).astype(F32).astype(BF16)


def prepare(index, centers, lanes):
    features, count = centers.shape
    examples = index.shape[1]
    return call(
        prepare_kernel,
        "prepare",
        [shape((count, DEPTH), BF16), shape((lanes, examples), BF16), shape(index.shape, jnp.int32)],
        1 << 20,
        arrays=2,
    )(index, centers)


def tile_kernel(
    alpha_hbm, chunk_ref, pool_ref, one_hot_ref, sides_ref, tile_ref, turned_ref, rows_ref,
    side_ref, base_ref, alpha_ref, alpha_sem,
):
    fetch = pltpu.make_async_copy(alpha_hbm, alpha_ref, alpha_sem)
    fetch.start()
    chunks, height, _ = pool_ref.shape
    lanes = one_hot_ref.shape[0]
    features = height * LANES // lanes
    count, examples = tile_ref.shape
    share = rows_ref.shape[2]
    scale = 4.0 / features * math.log2(math.e)
    pool = jnp.concatenate(
        [
            pool_ref[:, q * features : (q + 1) * features, :].reshape(chunks * features, LANES)
            for q in range(lanes // LANES)
        ],
        axis=1,
    )
    for b in range(examples // BAND):
        here = slice(b * BAND, (b + 1) * BAND)
        chunk = chunk_ref[:, here]
        picked = jnp.dot(pool, one_hot_ref[:, here], preferred_element_type=F32)
        points = jnp.where(chunk == 0, picked[:features], 0.0)
        for k in range(1, chunks):
            points = jnp.where(chunk == k, picked[k * features : (k + 1) * features], points)
        point_sq = jnp.sum(points * points, axis=0, keepdims=True)
        side = jnp.concatenate([points, tail(point_sq, 0, DEPTH - features)], axis=0)
        side_ref[:, here] = side.astype(BF16)
    fetch.wait()
    for b in range(count // BAND):
        here = slice(b * BAND, (b + 1) * BAND)
        near = jnp.dot(sides_ref[here, :], side_ref[...], preferred_element_type=F32)
        values = jnp.exp2(near * scale).astype(BF16)
        tile_ref[here, :] = values
        turned_ref[:, here] = values.T
        rows = jnp.dot(alpha_ref[:, here], values, preferred_element_type=F32)
        base_ref[...] = rows if b == 0 else base_ref[...] + rows
    for k in range(examples // share):
        rows_ref[k] = base_ref[:, k * share : (k + 1) * share]


def make_tile(chunk, row_pool, one_hot, sides, alpha, share):
    examples, count = chunk.shape[1], sides.shape[0]
    classes = alpha.shape[0]
    return call(
        tile_kernel,
        "tile",
        [
            shape((count, examples), BF16),
            shape((examples, count), BF16),
            shape((examples // share, classes, share), F32),
        ],
        4 << 30,
        [
            pltpu.VMEM((DEPTH, examples), BF16),
            pltpu.VMEM((classes, examples), F32),
            pltpu.VMEM(alpha.shape, BF16),
            pltpu.SemaphoreType.DMA,
        ],
        anywhere=1,
        arrays=4,
    )(alpha, chunk, row_pool, one_hot, sides)


def factors_kernel(core_ref, precond_ref, high_ref, low_ref, high_turned_ref, low_turned_ref):
    order = precond_ref.shape[1]
    half = high_ref.shape[0]
    first = core_ref[0] * half
    for k in range(half // order):
        here = slice(k * order, (k + 1) * order)
        block = precond_ref[pl.ds(pl.multiple_of(first + k * order, order), order), :]
        high = block.astype(BF16)
        high_ref[here] = high
        low_ref[here] = (block - high.astype(F32)).astype(BF16)
        turned = block.T
        high = turned.astype(BF16)
        high_turned_ref[here] = high
        low_turned_ref[here] = (turned - high.astype(F32)).astype(BF16)


def factors(core, precond):
    out = shape((precond.shape[0] // 2, precond.shape[1]), BF16)
    return call(factors_kernel, "factors", [out] * 4, 1 << 20, scalars=1, arrays=1)(core, precond)


def block_products(values, high_ref, low_ref):
    order = high_ref.shape[1]
    out = []
    for k in range(high_ref.shape[0] // order):
        here = slice(k * order, (k + 1) * order)
        block = values[:, here]
        high = block.astype(BF16)
        low = (block - high.astype(F32)).astype(BF16)
        product = jnp.dot(high, high_ref[here], preferred_element_type=F32)
        product += jnp.dot(high, low_ref[here], preferred_element_type=F32)
        product += jnp.dot(low, high_ref[here], preferred_element_type=F32)
        out.append(product)
    return jnp.concatenate(out, axis=1)


def put_lifted(ref, second_ref, lifted, vectors):
    classes, half = lifted.shape[0], ref.shape[1]
    ref[:classes] = lifted[:, :half]
    second_ref[...] = lifted[:, half:]
    row = lax.broadcasted_iota(jnp.int32, (EXTRA, 2 * LANES), 0)
    out = jnp.zeros((EXTRA, 2 * LANES), F32)
    for k, vector in enumerate(vectors):
        for p, piece in enumerate(split3(vector)):
            out = jnp.where(row == 3 * k + p, piece.astype(F32), out)
    ref[classes:, : 2 * LANES] = out.astype(BF16)
    ref[classes:, 2 * LANES :] = jnp.zeros((EXTRA, half - 2 * LANES), BF16)


def forward_own_kernel(core_ref, own_ref, second_ref, tile_ref, sums_ref):
    classes, wide = second_ref.shape
    first = core_ref[0] * (2 * wide)
    mine = [pl.ds(pl.multiple_of(first + k * wide, wide), wide) for k in range(2)]
    for b in range(sums_ref.shape[1] // BAND):
        here = slice(b * BAND, (b + 1) * BAND)
        rows = jnp.dot(own_ref[:classes], tile_ref[mine[0], here], preferred_element_type=F32)
        rows += jnp.dot(second_ref[...], tile_ref[mine[1], here], preferred_element_type=F32)
        sums_ref[:, here] = rows


def forward_more_kernel(core_ref, sums_ref, other_ref, tile_ref, more_ref):
    classes, wide = sums_ref.shape[0], other_ref.shape[1]
    theirs = pl.ds(pl.multiple_of((1 - core_ref[0]) * (2 * wide), wide), wide)
    for b in range(sums_ref.shape[1] // BAND):
        here = slice(b * BAND, (b + 1) * BAND)
        rows = jnp.dot(other_ref[:classes], tile_ref[theirs, here], preferred_element_type=F32)
        more_ref[:, here] = sums_ref[:, here] + rows


def forward_kernel(core_ref, first_ref, own_ref, other_ref, second_ref, tile_ref, rows_ref):
    classes, half = first_ref.shape[0], other_ref.shape[1]
    share = rows_ref.shape[2]
    examples = tile_ref.shape[1]
    theirs = pl.ds(pl.multiple_of((1 - core_ref[0]) * (2 * half) + half, half), half)
    part = [ref[classes:, : 2 * LANES].astype(F32) for ref in (own_ref, other_ref)]
    part = part[0] + part[1]
    part = [part[3 * k : 3 * k + 1] + part[3 * k + 1 : 3 * k + 2] + part[3 * k + 2 : 3 * k + 3] for k in range(3)]
    powers = exponents(part[2]) - 14.0
    extra = half_rows(powers, part[:2])
    scales = column(jnp.exp2(-powers), classes)
    for b in range(examples // BAND):
        here = slice(b * BAND, (b + 1) * BAND)
        rows = jnp.dot(second_ref[...], tile_ref[theirs, here], preferred_element_type=F32)
        rows = (rows + first_ref[:, here]) * scales
        for k in range(BAND // share):
            at = b * (BAND // share) + k
            rows_ref[at, :classes] = rows[:, k * share : (k + 1) * share]
            rows_ref[at, classes:] = extra


def forward(core, own, other, tile, share):
    classes = own[1].shape[0]
    examples = tile.shape[1]
    sums = shape((classes, examples), F32)
    first = call(
        forward_own_kernel, "forward_own", sums, 604 << 20, scalars=1, arrays=3
    )(core, *own, tile)
    first = call(
        forward_more_kernel, "forward_more", sums, 302 << 20, scalars=1, arrays=3
    )(core, first, other[0], tile)
    return call(
        forward_kernel,
        "forward",
        shape((examples // share, classes + SCALARS, share), F32),
        302 << 20,
        scalars=1,
        arrays=5,
    )(core, first, own[0], *other, tile)


def backward_other_kernel(
    core_ref, values_ref, turned_ref, first_ref, second_ref, flat_ref, row_ref
):
    shares, height, share = values_ref.shape
    classes, examples = flat_ref.shape
    wide = first_ref.shape[1]
    for k in range(shares):
        flat_ref[:, k * share : (k + 1) * share] = values_ref[k, :classes]
    row = jnp.zeros((8, 2 * LANES), F32)
    if height > classes:
        total = values_ref[0, classes:].astype(F32)
        for k in range(1, shares):
            total = total + values_ref[k, classes:].astype(F32)
        row = jnp.broadcast_to(read_rows(total, 0), (8, 2 * LANES))
    row_ref[...] = row
    first_ref[classes:, : 2 * LANES] = row
    first_ref[classes:, 2 * LANES :] = jnp.zeros((8, wide - 2 * LANES), F32)
    for k, ref in enumerate((first_ref, second_ref)):
        for b in range(wide // BAND):
            there = (1 - core_ref[0]) * (2 * wide) + k * wide + b * BAND
            ref[:classes, b * BAND : (b + 1) * BAND] = jnp.dot(
                flat_ref[...],
                turned_ref[:, pl.ds(pl.multiple_of(there, BAND), BAND)],
                preferred_element_type=F32,
            )


def backward_own_kernel(core_ref, flat_ref, turned_ref, own_ref):
    half = own_ref.shape[1]
    for b in range(half // BAND):
        there = pl.ds(pl.multiple_of(core_ref[0] * half + b * BAND, BAND), BAND)
        own_ref[:, b * BAND : (b + 1) * BAND] = jnp.dot(
            flat_ref[...], turned_ref[:, there], preferred_element_type=F32
        )


def backward_other(core, values, turned, classes):
    examples, count = turned.shape
    return call(
        backward_other_kernel,
        "backward_other",
        [
            shape((classes + SCALARS, count // 4), F32),
            shape((classes, count // 4), F32),
            shape((classes, examples), BF16),
            shape((8, 2 * LANES), F32),
        ],
        604 << 20,
        scalars=1,
        arrays=2,
    )(core, values, turned)


def backward_own(core, flat, turned):
    return call(
        backward_own_kernel,
        "backward_own",
        shape((flat.shape[0], turned.shape[1] // 2), F32),
        604 << 20,
        scalars=1,
        arrays=2,
    )(core, flat, turned)


def put_halves(ref, values, powers, vectors):
    classes, wide = values.shape
    ref[:classes] = values
    row = lax.broadcasted_iota(jnp.int32, (SCALARS, 2 * LANES), 0)
    out = jnp.zeros((SCALARS, 2 * LANES), F32)
    for p, piece in enumerate(half_pieces(powers, vectors)):
        out = jnp.where(row == p, piece, out)
    ref[classes:, : 2 * LANES] = out
    ref[classes:, 2 * LANES :] = jnp.zeros((SCALARS, wide - 2 * LANES), F32)


def pack_halves(ref, values, vectors):
    classes = values.shape[0]
    size = jnp.max(jnp.abs(values), axis=1, keepdims=True)
    powers = exponents(size) - 14.0
    empty = jnp.zeros((2 * LANES - classes, LANES), F32)
    row = jnp.concatenate([jnp.broadcast_to(powers, (classes, LANES)), empty], axis=0).T[:1]
    put_halves(ref, values * jnp.exp2(-powers), row, vectors)


def powers_of(ref):
    classes = ref.shape[0] - SCALARS
    return ref[classes : classes + 1, : 2 * LANES]


def unpack_pairs(pairs):
    refs = [ref for pair in pairs for ref in pair]
    classes = refs[0].shape[0] - SCALARS
    scales = columns([jnp.exp2(powers_of(ref)) for ref in refs], classes)
    values = [ref[:classes] * scale for ref, scale in zip(refs, scales)]
    return [values[2 * k] + values[2 * k + 1] for k in range(len(pairs))]


def unpack_vector(ref):
    classes = ref.shape[0] - SCALARS
    power, high, low = (ref[classes + p : classes + p + 1, : 2 * LANES] for p in range(1, 4))
    return jnp.exp2(power) * (high + low / 2048.0)


def join_first_kernel(own_ref, row_ref, got_ref, sum_ref):
    classes, wide = own_ref.shape[0], sum_ref.shape[1]
    vector = row_ref[:1] + got_ref[classes : classes + 1, : 2 * LANES]
    pack_halves(sum_ref, own_ref[:, :wide] + got_ref[:classes], [vector])


def join_second_kernel(own_ref, got_ref, sum_ref):
    pack_halves(sum_ref, own_ref[:, sum_ref.shape[1] :] + got_ref[...], [])


def join(own, row, first, second):
    half = shape((own.shape[0] + SCALARS, own.shape[1] // 2), F32)
    return (
        call(join_first_kernel, "join_first", half, 1 << 20, arrays=3)(own, row, first),
        call(join_second_kernel, "join_second", half, 1 << 20, arrays=2)(own, second),
    )


def add_kernel(own_ref, got_ref, sum_ref):
    classes = own_ref.shape[0] - SCALARS
    powers = jnp.maximum(powers_of(own_ref), powers_of(got_ref)) + 1.0
    own, got = columns(
        [jnp.exp2(powers_of(own_ref) - powers), jnp.exp2(powers_of(got_ref) - powers)], classes
    )
    vector = unpack_vector(own_ref) + unpack_vector(got_ref)
    put_halves(sum_ref, own_ref[:classes] * own + got_ref[:classes] * got, powers, [vector])


def add_halves(own, got):
    return call(add_kernel, "add", shape(own.shape, F32), 1 << 20, arrays=2)(own, got)


def gradient_kernel(base_ref, label_ref, weight_ref, hessian_ref, send_ref):
    classes, share = base_ref.shape
    base = base_ref[...]
    probability = jax.nn.sigmoid(base)
    row = lax.broadcasted_iota(jnp.int32, (classes, share), 0)
    target = jnp.where(row == label_ref[...], 1.0, 0.0)
    hessian_ref[...] = weight_ref[...] * probability * (1.0 - probability)
    gradient = (weight_ref[...] * (probability - target)).astype(BF16)
    for k in range(send_ref.shape[0]):
        send_ref[k] = gradient


def gradient(base, label, weight, shares):
    return call(
        gradient_kernel,
        "gradient",
        [shape(base.shape, F32), shape((shares,) + base.shape, BF16)],
        1 << 20,
        arrays=3,
    )(base, label, weight)


def residual_kernel(
    total, one_ref, one_in_ref, two_ref, two_in_ref, high_ref, low_ref, high_turned_ref,
    low_turned_ref, residual_ref, lifted_ref, second_ref,
):
    one, two = unpack_pairs(((one_ref, one_in_ref), (two_ref, two_in_ref)))
    sums = jnp.concatenate([one, two], axis=1)
    residual = block_products(sums, high_ref, low_ref) * (-1.0 / total)
    residual_ref[...] = residual
    lifted = block_products(residual, high_turned_ref, low_turned_ref).astype(BF16)
    zero = jnp.zeros((1, 2 * LANES), F32)
    norm, sizes = lane_sums_of([residual * residual, jnp.abs(lifted.astype(F32))])
    put_lifted(lifted_ref, second_ref, lifted, [norm, zero, sizes])


def first_residual(total, sums, blocks):
    classes, wide = sums[2].shape[0] - SCALARS, sums[2].shape[1]
    return call(
        functools.partial(residual_kernel, total),
        "residual",
        [
            shape((classes, 2 * wide), F32),
            shape((classes + EXTRA, wide), BF16),
            shape((classes, wide), BF16),
        ],
        450 << 20,
        arrays=8,
    )(*sums, *blocks)


def weigh_kernel(parts_ref, hessian_ref, image_ref, norm_ref, send_ref):
    classes = hessian_ref.shape[0]
    image = sum_scaled(parts_ref, classes)
    image_ref[...] = image
    norm_ref[...] = stack_rows([half_vector(parts_ref, classes, 0)])
    weighted = (hessian_ref[...] * image).astype(BF16)
    extra = rows_of([lane_sums_of([weighted.astype(F32) * image])[0]])
    for k in range(send_ref.shape[0]):
        send_ref[k, :classes] = weighted
        send_ref[k, classes:] = extra


def weigh(parts, hessian):
    return call(
        weigh_kernel,
        "weigh",
        [
            shape(hessian.shape, F32),
            shape((8, 2 * LANES), F32),
            shape((parts.shape[0], hessian.shape[0] + EXTRA, hessian.shape[1]), BF16),
        ],
        1 << 20,
        arrays=2,
    )(parts, hessian)


def step_kernel(
    total, one_ref, one_in_ref, two_ref, two_in_ref, high_ref, low_ref, high_turned_ref,
    low_turned_ref, residual_ref, norm_ref, lifted_ref, second_ref, rough_ref,
):
    classes = residual_ref.shape[0]
    one, two = unpack_pairs(((one_ref, one_in_ref), (two_ref, two_in_ref)))
    curve = (unpack_vector(one_ref) + unpack_vector(one_in_ref)) / total
    norm = norm_ref[:1]
    lane = lax.broadcasted_iota(jnp.int32, (1, 2 * LANES), 1)
    rough = jnp.where(lane < classes, norm / (curve + RIDGE * norm), 0.0)
    rough_ref[...] = stack_rows([rough])
    sums = jnp.concatenate([one, two], axis=1)
    old = residual_ref[...]
    image = block_products(sums, high_ref, low_ref) / total + RIDGE * old
    new = old - column(rough, classes) * image
    lifted = block_products(new, high_turned_ref, low_turned_ref).astype(BF16)
    sums = lane_sums_of([old * new, new * new, jnp.abs(lifted.astype(F32))])
    put_lifted(lifted_ref, second_ref, lifted, sums)


def step(total, sums, blocks, residual, norm):
    classes, half = residual.shape
    return call(
        functools.partial(step_kernel, total),
        "step",
        [
            shape((classes + EXTRA, half // 2), BF16),
            shape((classes, half // 2), BF16),
            shape((8, 2 * LANES), F32),
        ],
        450 << 20,
        arrays=10,
    )(*sums, *blocks, residual, norm)


def curve_kernel(
    parts_ref, hessian_ref, image_ref, norm_ref, rough_ref, last_ref, scales_ref, curve_ref
):
    classes = hessian_ref.shape[0]
    last = sum_scaled(parts_ref, classes)
    last_ref[...] = last
    cross = half_vector(parts_ref, classes, 0)
    norm_rough = half_vector(parts_ref, classes, 1)
    norm = norm_ref[:1]
    lane = lax.broadcasted_iota(jnp.int32, (1, 2 * LANES), 1)
    excess = jnp.where(lane < classes, cross / (norm - cross), 0.0)
    grown = 1.0 + excess
    norm_next = grown * (grown * norm_rough - 2.0 * excess * cross) + excess * excess * norm
    ratio = jnp.where(lane < classes, norm_next / norm, 0.0)
    ridge = RIDGE * (norm_next + ratio * ratio * norm)
    scales_ref[...] = stack_rows(
        [rough_ref[:1] * grown, grown, ratio - excess, norm_next, ridge]
    )
    scale, other = columns([grown, ratio - excess], classes)
    rows = scale * last + other * image_ref[...]
    weighted = (hessian_ref[...] * rows).astype(BF16).astype(F32)
    curve_ref[...] = lane_sums_of([weighted * rows])[0]


def last_curve(parts, hessian, image, norm, rough):
    row = shape((8, 2 * LANES), F32)
    return call(
        curve_kernel,
        "curve",
        [shape(hessian.shape, F32), row, shape((1, 2 * LANES), F32)],
        1 << 20,
        arrays=5,
    )(parts, hessian, image, norm, rough)


def margins_kernel(total, curve_ref, scales_ref, base_ref, image_ref, last_ref, margins_ref):
    classes = base_ref.shape[0]
    curve = jnp.sum(curve_ref[:, 0], axis=0, keepdims=True)
    first, grown, other = scales_ref[0:1], scales_ref[1:2], scales_ref[2:3]
    lane = lax.broadcasted_iota(jnp.int32, (1, 2 * LANES), 1)
    second = jnp.where(
        lane < classes, scales_ref[3:4] / (curve / total + scales_ref[4:5]), 0.0
    )
    image_scale, last_scale = columns([first + second * other, second * grown], classes)
    margins_ref[...] = base_ref[...] + image_scale * image_ref[...] + last_scale * last_ref[...]


def margins(total, curve, scales, base, image, last):
    return call(
        functools.partial(margins_kernel, total), "margins", shape(base.shape, F32), 1 << 20, arrays=5
    )(curve, scales, base, image, last)


def shards(pool, indices, labels, example_weight, centers, alpha, precond):
    n_ex, n_ctr = lax.axis_size("ex"), lax.axis_size("ctr")
    classes, count = alpha.shape
    examples = indices.shape[0]
    share = examples // n_ctr
    total = float(examples * n_ex)
    core = (lax.axis_index("ex") % 2).reshape(1)
    core_pairs = [(i, i ^ 1) for i in range(n_ex)]

    def over_y(array, flip):
        pairs = [(2 * y + c, 2 * (y ^ flip) + c) for y in range(n_ex // 2) for c in range(2)]
        return lax.ppermute(array, "ex", pairs)

    def over_cores(array):
        return lax.ppermute(array, "ex", core_pairs)

    def trade(parts):
        return lax.all_to_all(parts, "ctr", 0, 0)

    def trade_halves(parts):
        return trade(parts.astype(F16)).astype(F32)

    def swap(array, flip):
        array = lax.reduce_precision(array, 5, 10)
        return array, over_y(array.astype(F16), flip).astype(F32)

    def sum_examples(send):
        first, second, flat, row = backward_other(core, trade(send), turned, classes)
        got = over_cores(first), over_cores(second)
        one, two = join(backward_own(core, flat, turned), row, *got)
        one, two = swap(one, 3), swap(two, 1)
        one, two = add_halves(*one), add_halves(*two)
        return (*swap(one, 1), *swap(two, 3)), got[0]

    offset = lax.axis_index("ctr") * share
    label = lax.dynamic_slice_in_dim(labels, offset, share, 0).reshape(1, share)
    weight = lax.dynamic_slice_in_dim(example_weight, offset, share, 0).reshape(1, share)
    index = indices.reshape(1, examples)
    sides, one_hot, chunk = prepare(index, centers, pool.shape[1])
    row_pool = trade(copies(pool, n_ctr))
    row_pool, sides, one_hot, chunk, label, weight, core = lax.optimization_barrier(
        (row_pool, sides, one_hot, chunk, label, weight, core)
    )
    tile, turned, rows = make_tile(chunk, row_pool, one_hot, sides, alpha, share)
    base = jnp.sum(trade_halves(rows), axis=0)
    hessian, send = gradient(base, label, weight, n_ctr)

    sums, got = sum_examples(send)
    got, late_core = lax.optimization_barrier((got, core))
    blocks = factors(late_core, precond)
    residual, *lifted = first_residual(total, sums, blocks)
    rows = forward(core, lifted, [over_cores(part) for part in lifted], tile, share)
    image, norm, send = weigh(trade_halves(rows), hessian)

    sums, _ = sum_examples(send)
    *lifted, rough = step(total, sums, blocks, residual, norm)
    rows = forward(core, lifted, [over_cores(part) for part in lifted], tile, share)
    last, scales, curve = last_curve(trade_halves(rows), hessian, image, norm, rough)

    curve = jnp.broadcast_to(curve, (n_ex * n_ctr,) + curve.shape)
    curve = lax.all_to_all(curve, ("ex", "ctr"), 0, 0)
    return margins(total, curve, scales, base, image, last)


def solution(mesh):
    return jax.shard_map(
        shards,
        mesh=mesh,
        in_specs=(
            P(None, ("ex", "ctr")),
            P("ex"),
            P("ex"),
            P("ex"),
            P(None, "ctr"),
            P(None, "ctr"),
            P("ctr", None),
        ),
        out_specs=P(None, ("ex", "ctr")),
        check_vma=False,
    )
```
